32 devices in a mesh: ctx: 16 (over z, y, x), head: 2 (over core).
Axes of the slice: x: 2, y: 2, z: 4, core: 2. Of those that a mesh axis runs over, the one named last changes fastest.
Arguments:
- lin_q: bfloat16 [8192, 8, 128], P('ctx', 'head'), may hold values from -1.5 to 1.5
- lin_k: bfloat16 [8192, 8, 128], P('ctx', 'head'), may hold values from -1.5 to 1.5
- lin_v: bfloat16 [8192, 8, 128], P('ctx', 'head'), may hold values from -3 to 3
- lin_dout: bfloat16 [8192, 8, 128], P('ctx', 'head'), may hold values from -0.29882812 to 0.29882812
- lin_decay: float32 [8, 8192], P('head', 'ctx'), may hold values from -1 to 0
- att_q: bfloat16 [8192, 8, 128], P('ctx', 'head'), may hold values from -64 to 64
- att_k: bfloat16 [8192, 128], P('ctx'), may hold values from -6 to 6
- att_v: bfloat16 [8192, 128], P('ctx'), may hold values from -6 to 6
- att_dout: bfloat16 [8192, 8, 128], P('ctx', 'head'), may hold values from -1.796875 to 1.796875
- doc_block: int32 [32], replicated, may hold values from 0 to 4, as said below
Outputs:
- lin_dq: bfloat16 [8192, 8, 128], P('ctx', 'head')
- lin_dk: bfloat16 [8192, 8, 128], P('ctx', 'head')
- lin_dv: bfloat16 [8192, 8, 128], P('ctx', 'head')
- att_dq: bfloat16 [8192, 8, 128], P('ctx', 'head')
- att_dk: bfloat16 [8192, 128], P(('ctx', 'head'))
- att_dv: bfloat16 [8192, 128], P(('ctx', 'head'))
The draws below stay inside these ranges and needn't reach their ends.
Inputs may be any that keep to these rules, and one draw needn't show every extreme that they name: doc_block starts at 0, never falls and rises by at most one from block to block; each document spans 1 to 12 blocks; the first spans exactly 12.
All inputs are finite; a program needn't handle non-finite values.
Results may differ from the reference program's by a relative error of at most 0.0052.
Values may be sent and summed in bfloat16 or wider, within the bound.
A program may use at most 128 MiB of HBM per device.

```python
import math
import jax
import jax.numpy as jnp
from jax import lax

HD = 128
TILE_WIDTH = 256
MOST_BLK = 12
TILE_NUMBER = 32
SEQ = 8192
LINEAR_ATTN_COUNT = 8
QHEADS = 8
DOCS = 5


def attention_pair(key):
    starting_number = jax.random.fold_in(key, 17)
    query_key, key_key = jax.random.split(starting_number, 2)
    queries = jnp.clip(jax.random.normal(query_key, (SEQ, QHEADS, HD), jnp.float32), -6.0, 6.0)
    keys_out = jnp.clip(jax.random.normal(key_key, (SEQ, HD), jnp.float32), -6.0, 6.0)
    return (queries, keys_out)


def draw_att_q(key, part):
    return attention_pair(key)[0].astype(jnp.bfloat16)


def draw_att_k(key, part):
    return attention_pair(key)[1].astype(jnp.bfloat16)


def draw_doc_block(key, part):
    starting_number = jax.random.fold_in(key, 41)
    others = DOCS - 1
    remaining = TILE_NUMBER - MOST_BLK
    extra = remaining - others
    capacity = MOST_BLK - 1
    slots = jnp.arange(others * capacity, dtype=jnp.int32) // capacity
    shuffled = jax.random.permutation(starting_number, slots)
    chosen = shuffled[:extra]
    counts = jnp.sum((chosen[:, None] == jnp.arange(others, dtype=jnp.int32)[None, :]).astype(jnp.int32), axis=0)
    ends = jnp.cumsum(1 + counts)
    blocks = jnp.arange(remaining, dtype=jnp.int32)
    later_ids = 1 + jnp.sum((blocks[:, None] >= ends[None, :]).astype(jnp.int32), axis=1)
    return jnp.concatenate([jnp.zeros((MOST_BLK,), jnp.int32), later_ids.astype(jnp.int32)])


def draw_lin_decay(key, part):
    starting_number = jax.random.fold_in(key, 29)
    permute_prng_seed, gradual_prng_seed, quick_prng_seed, tile_prng_seed, position_prng_seed, spurt_prng_seed, objective_prng_seed = jax.random.split(starting_number, 7)
    joined_positions = MOST_BLK * TILE_WIDTH
    fast_count = LINEAR_ATTN_COUNT // 2
    order = jax.random.permutation(permute_prng_seed, LINEAR_ATTN_COUNT)
    fast = order < fast_count
    slow_rate = jax.random.uniform(gradual_prng_seed, (LINEAR_ATTN_COUNT,), jnp.float32, 0.1, 0.5) / joined_positions
    fast_rate = jax.random.uniform(quick_prng_seed, (LINEAR_ATTN_COUNT,), jnp.float32, 1.0 / 50.0, 1.0 / 30.0)
    rate = jnp.where(fast, fast_rate, slow_rate)
    spread = math.log(2.0)
    block_factor = jnp.exp(jax.random.uniform(tile_prng_seed, (LINEAR_ATTN_COUNT, TILE_NUMBER, 1), jnp.float32, -spread, spread))
    token_factor = jnp.exp(jax.random.uniform(position_prng_seed, (LINEAR_ATTN_COUNT, TILE_NUMBER, TILE_WIDTH), jnp.float32, -spread, spread))
    constant_fraction = -rate[:, None, None] * block_factor * token_factor
    spurt_extents = jax.random.bernoulli(spurt_prng_seed, 3.0 / joined_positions, (LINEAR_ATTN_COUNT, TILE_NUMBER, TILE_WIDTH))
    objective_numbers = jax.random.uniform(objective_prng_seed, (LINEAR_ATTN_COUNT, TILE_NUMBER, TILE_WIDTH), jnp.float32, math.log(0.5), math.log(0.8))
    ultimate_outcome = constant_fraction + jnp.where(spurt_extents, objective_numbers, 0.0)
    return jnp.clip(ultimate_outcome, -1.0, 0.0).reshape(LINEAR_ATTN_COUNT, SEQ)


def block_scale(key, extent, cuts, least, high):
    factor_of = 1.0
    for axis_at, shards_of in cuts:
        steps = jax.random.uniform(jax.random.fold_in(jax.random.fold_in(key, 6), axis_at), (shards_of,), jnp.float32, least / len(cuts), high / len(cuts))
        factor_of = factor_of * jnp.repeat(jnp.exp(steps), extent[axis_at] // shards_of).reshape((-1,) + (1,) * (len(extent) - 1 - axis_at))
    return factor_of


def noise(stream_key, extent, scale, limit, cuts=(), kind=jnp.bfloat16):
    level = block_scale(stream_key, extent, cuts, -0.22, 0.18) if cuts else 1.0
    entries = jax.random.normal(stream_key, extent, jnp.float32) * scale * level
    return jnp.minimum(jnp.maximum(entries, -limit), limit).astype(kind)


def setup_inputs(seed: int = 0) -> dict:
    seeds = jax.random.split(jax.random.key(seed), 11)
    return {
        "lin_q": noise(seeds[0], (SEQ, LINEAR_ATTN_COUNT, HD), 0.25, 1.5, ((0, 16), (1, 2))),
        "lin_k": noise(seeds[1], (SEQ, LINEAR_ATTN_COUNT, HD), 0.25, 1.5, ((0, 16), (1, 2))),
        "lin_v": noise(seeds[2], (SEQ, LINEAR_ATTN_COUNT, HD), 0.5, 3.0, ((0, 16), (1, 2))),
        "lin_dout": noise(seeds[3], (SEQ, LINEAR_ATTN_COUNT, HD), 0.05, 0.29882812, ((0, 16), (1, 2))),
        "lin_decay": draw_lin_decay(jax.random.fold_in(seeds[10], 71), 0),
        "att_q": draw_att_q(jax.random.fold_in(seeds[10], 71), 0),
        "att_k": draw_att_k(jax.random.fold_in(seeds[10], 71), 0),
        "att_v": noise(seeds[7], (SEQ, HD), 1.0, 6.0, ((0, 16),)),
        "att_dout": noise(seeds[8], (SEQ, QHEADS, HD), 0.3, 1.796875, ((0, 16), (1, 2))),
        "doc_block": draw_doc_block(jax.random.fold_in(seeds[10], 71), 0),
    }


NEG = -1e30


def rounded(values):
    return lax.optimization_barrier(values.astype(jnp.bfloat16)).astype(jnp.float32)


def block_terms(queries, keys_in, values, douts, decay):
    highest = lax.Precision.HIGHEST
    queries = queries.astype(jnp.float32)
    keys_in = keys_in.astype(jnp.float32)
    values = values.astype(jnp.float32)
    douts = douts.astype(jnp.float32)
    cumulative = jnp.cumsum(decay, axis=1)
    block_total = cumulative[:, -1]
    offsets = jnp.arange(decay.shape[1], dtype=jnp.int32)
    lower_tri = (offsets[:, None] >= offsets[None, :])[None]
    spread = jnp.where(lower_tri, cumulative[:, :, None] - cumulative[:, None, :], 0.0)
    weights = jnp.where(lower_tri, jnp.exp(spread), 0.0)
    cross = jnp.einsum("thd,shd->hts", douts, values)
    inner = jnp.einsum("thd,shd->hts", queries, keys_in)
    left_mix = rounded(cross * weights)
    right_mix = rounded(inner * weights)
    grad_query = jnp.einsum("hts,shd->thd", left_mix, keys_in)
    grad_key = jnp.einsum("hts,thd->shd", left_mix, queries)
    grad_value = jnp.einsum("hts,thd->shd", right_mix, douts)
    head_decay = jnp.exp(cumulative).T[:, :, None]
    tail_decay = jnp.exp(block_total[:, None] - cumulative).T[:, :, None]
    key_state = jnp.einsum("shi,shj->hij", keys_in * tail_decay, values, precision=highest)
    query_state = jnp.einsum("thi,thj->hij", queries * head_decay, douts, precision=highest)
    return grad_query, grad_key, grad_value, head_decay, tail_decay, block_total, key_state, query_state


def finish(terms, keys_in, values, douts, into, back):
    highest = lax.Precision.HIGHEST
    grad_query, grad_key, grad_value, head_decay, tail_decay, block_total, key_state, query_state = terms
    grad_query = grad_query + head_decay * jnp.einsum("thj,hij->thi", douts.astype(jnp.float32), into, precision=highest)
    grad_key = grad_key + tail_decay * jnp.einsum("shj,hij->shi", values.astype(jnp.float32), back, precision=highest)
    grad_value = grad_value + tail_decay * jnp.einsum("shi,hij->shj", keys_in.astype(jnp.float32), back, precision=highest)
    return grad_query.astype(jnp.bfloat16), grad_key.astype(jnp.bfloat16), grad_value.astype(jnp.bfloat16)


def lightning_grads(lin_q, lin_k, lin_v, lin_dout, lin_decay, doc_block):
    block_shape = (TILE_NUMBER, TILE_WIDTH, LINEAR_ATTN_COUNT, HD)
    queries = lin_q.reshape(block_shape)
    keys_in = lin_k.reshape(block_shape)
    values = lin_v.reshape(block_shape)
    douts = lin_dout.reshape(block_shape)
    decay = lin_decay.reshape(LINEAR_ATTN_COUNT, TILE_NUMBER, TILE_WIDTH).transpose(1, 0, 2)
    terms = lax.map(lambda pieces: block_terms(*pieces), (queries, keys_in, values, douts, decay))
    same_doc = (doc_block[1:] == doc_block[:-1]).astype(jnp.float32)
    follows = jnp.concatenate([jnp.zeros((1,), jnp.float32), same_doc])
    precedes = jnp.concatenate([same_doc, jnp.zeros((1,), jnp.float32)])
    zero_state = jnp.zeros((LINEAR_ATTN_COUNT, HD, HD), jnp.float32)

    def link(carried, pieces):
        state_now, total_now, joined = pieces
        entering = joined * carried
        return state_now + jnp.exp(total_now)[:, None, None] * entering, entering

    unused_one, into_all = lax.scan(link, zero_state, (terms[6], terms[5], follows))
    unused_two, back_all = lax.scan(link, zero_state, (terms[7], terms[5], precedes), reverse=True)
    grads = lax.map(lambda pieces: finish(*pieces), (terms, keys_in, values, douts, into_all, back_all))
    return tuple(grad.reshape(SEQ, LINEAR_ATTN_COUNT, HD) for grad in grads)


def attention_grads(att_q, att_k, att_v, att_dout, doc_block):
    scale = HD ** -0.5
    window = MOST_BLK * TILE_WIDTH
    margin = window - TILE_WIDTH
    keys_pad = jnp.concatenate([jnp.zeros((margin, HD), jnp.float32), att_k.astype(jnp.float32)])
    values_pad = jnp.concatenate([jnp.zeros((margin, HD), jnp.float32), att_v.astype(jnp.float32)])
    token_doc = jnp.repeat(doc_block, TILE_WIDTH)
    key_doc = jnp.concatenate([jnp.full((margin,), -1, jnp.int32), token_doc])
    offsets_q = jnp.arange(TILE_WIDTH, dtype=jnp.int32)
    offsets_k = jnp.arange(window, dtype=jnp.int32)

    def one_block(carried, index):
        grad_keys, grad_values = carried
        begin = (index * TILE_WIDTH).astype(jnp.int32)
        queries = lax.dynamic_slice_in_dim(att_q, begin, TILE_WIDTH).astype(jnp.float32)
        douts = lax.dynamic_slice_in_dim(att_dout, begin, TILE_WIDTH).astype(jnp.float32)
        near_keys = lax.dynamic_slice_in_dim(keys_pad, begin, window)
        near_values = lax.dynamic_slice_in_dim(values_pad, begin, window)
        near_doc = lax.dynamic_slice_in_dim(key_doc, begin, window)
        query_doc = lax.dynamic_slice_in_dim(token_doc, begin, TILE_WIDTH)
        query_pos = begin + offsets_q
        key_pos = begin - margin + offsets_k
        visible = (query_doc[:, None] == near_doc[None, :]) & (key_pos[None, :] <= query_pos[:, None])
        scores = jnp.einsum("thd,sd->hts", queries, near_keys) * scale
        scores = jnp.where(visible[None], scores, NEG)
        row_max = jnp.max(scores, axis=2)
        plain = jnp.where(visible[None], jnp.exp(scores - row_max[:, :, None]), 0.0)
        row_sum = jnp.sum(plain, axis=2)
        grad_probs = jnp.einsum("thd,sd->hts", douts, near_values)
        lse = row_max + jnp.log(row_sum)
        delta = jnp.sum(plain * grad_probs, axis=2) / row_sum
        probs = jnp.where(visible[None], jnp.exp(scores - lse[:, :, None]), 0.0)
        grad_scores = probs * (grad_probs - delta[:, :, None])
        probs_b = rounded(probs)
        grad_b = rounded(grad_scores)
        block_query = jnp.einsum("hts,sd->thd", grad_b, near_keys) * scale
        part_key = jnp.einsum("hts,thd->sd", grad_b, queries)
        part_value = jnp.einsum("hts,thd->sd", probs_b, douts)
        grad_keys = lax.dynamic_update_slice_in_dim(grad_keys, lax.dynamic_slice_in_dim(grad_keys, begin, window) + part_key, begin, 0)
        grad_values = lax.dynamic_update_slice_in_dim(grad_values, lax.dynamic_slice_in_dim(grad_values, begin, window) + part_value, begin, 0)
        return (grad_keys, grad_values), block_query.astype(jnp.bfloat16)

    start = (jnp.zeros((margin + SEQ, HD), jnp.float32), jnp.zeros((margin + SEQ, HD), jnp.float32))
    finals, blocks = lax.scan(one_block, start, jnp.arange(TILE_NUMBER, dtype=jnp.int32))
    att_dq = blocks.reshape(SEQ, QHEADS, HD)
    att_dk = (finals[0][margin:] * scale).astype(jnp.bfloat16)
    att_dv = finals[1][margin:].astype(jnp.bfloat16)
    return att_dq, att_dk, att_dv


def reference(lin_q, lin_k, lin_v, lin_dout, lin_decay, att_q, att_k, att_v, att_dout, doc_block):
    lin_out = lightning_grads(lin_q, lin_k, lin_v, lin_dout, lin_decay, doc_block)
    att_out = attention_grads(att_q, att_k, att_v, att_dout, doc_block)
    return (lin_out[0], lin_out[1], lin_out[2], att_out[0], att_out[1], att_out[2])
```

```python
import functools
import math

import jax
import jax.numpy as jnp
from jax import lax
from jax.experimental import pallas as pl
from jax.experimental.pallas import tpu as pltpu
from jax.sharding import PartitionSpec as P

TILE = 256
MOST = 12
NEG = -1e30
MESH = pl.DeviceIdType.MESH
F32 = jnp.float32
BF16 = jnp.bfloat16
SHAPE = jax.ShapeDtypeStruct
DMA = pltpu.SemaphoreType.DMA
IN_VMEM = pl.BlockSpec(memory_space=pltpu.VMEM)
IN_SMEM = pl.BlockSpec(memory_space=pltpu.SMEM)
ANYWHERE = pl.BlockSpec(memory_space=pl.ANY)
VMEM_LIMIT = 60 * 1024 * 1024


def dot_nn(a, b):
    return lax.dot_general(a, b, (((1,), (0,)), ((), ())), preferred_element_type=F32)


def dot_nt(a, b):
    return lax.dot_general(a, b, (((1,), (1,)), ((), ())), preferred_element_type=F32)


def dot_tn(a, b):
    return lax.dot_general(a, b, (((0,), (0,)), ((), ())), preferred_element_type=F32)


def split(x):
    high = x.astype(BF16)
    return high, (x - high.astype(F32)).astype(BF16)


def decay_terms(me, count, nblocks, doc, dec):
    t_sub = lax.broadcasted_iota(jnp.int32, (TILE, TILE), 0)
    t_lane = lax.broadcasted_iota(jnp.int32, (TILE, TILE), 1)
    upper = (t_sub <= t_lane).astype(F32)
    lower = (t_sub >= t_lane).astype(F32)

    def link(at_one, at_two):
        one = jnp.clip(at_one, 0, count * nblocks - 1)
        two = jnp.clip(at_two, 0, count * nblocks - 1)
        inside = jnp.logical_and(at_one >= 0, at_two < count * nblocks)
        same = jnp.logical_and(doc[one] == doc[two], inside)
        return jnp.where(same, 1.0, 0.0).astype(F32)

    follows = [link(me * nblocks + b - 1, me * nblocks + b) for b in range(nblocks)]
    precedes = [link(me * nblocks + b, me * nblocks + b + 1) for b in range(nblocks)]

    cum_row, cum_col = [], []
    for b in range(nblocks):
        piece = dec[:, b * TILE : (b + 1) * TILE]
        cum_row.append(
            lax.dot_general(
                piece, upper, (((1,), (0,)), ((), ())),
                preferred_element_type=F32, precision=lax.Precision.HIGHEST,
            )
        )
        cum_col.append(
            lax.dot_general(
                lower, piece, (((1,), (1,)), ((), ())),
                preferred_element_type=F32, precision=lax.Precision.HIGHEST,
            )
        )

    def head_terms(b, h):
        row = cum_row[b][h : h + 1, :]
        col = cum_col[b][:, h : h + 1]
        total = col[TILE - 1 : TILE, :]
        return row, col, total

    return follows, precedes, head_terms, t_sub, t_lane


def whole_kernel(
    count, reach, heads, nblocks,
    doc, lq, lk, lv, ld, dec_in, aq, ado, att_k, att_v,
    lin_dq, lin_dk, lin_dv, att_dq, att_dk, att_dv,
    wide, raw, dec, q, dout, kall, vall, parts, states, grads, mixed,
    scores, probs_grad, flipped, dkey, dvalue,
    snd, got, paired, out, inbox,
    raw_sem, kv_send, kv_recv, pair_send, pair_recv, st_send, st_recv,
    pg_send, pg_recv, home_send, home_recv,
):
    me = lax.axis_index("ctx")
    core = lax.axis_index("head")
    length = nblocks * TILE
    width = lq.shape[1]
    rows = TILE * heads
    first_devs = MOST // nblocks
    in_first = me < first_devs
    nleft = jnp.minimum(jnp.where(in_first, me, me - first_devs), reach)
    nright = jnp.minimum(jnp.where(in_first, first_devs - 1 - me, count - 1 - me), reach)
    scale = width ** (-0.5)
    factor = scale * math.log2(math.e)

    loads = [
        pltpu.make_async_copy(ref, raw.at[a], raw_sem.at[a])
        for a, ref in enumerate((lq, lk, lv, ld))
    ]
    loads.append(pltpu.make_async_copy(dec_in, dec, raw_sem.at[4]))
    loads.append(pltpu.make_async_copy(aq, q, raw_sem.at[5]))
    loads.append(pltpu.make_async_copy(ado, dout, raw_sem.at[6]))
    own_rows = pl.ds(reach * length, length)
    loads.append(pltpu.make_async_copy(att_k, kall.at[own_rows], raw_sem.at[7]))
    loads.append(pltpu.make_async_copy(att_v, vall.at[own_rows], raw_sem.at[8]))
    for load in loads:
        load.start()

    barrier = pltpu.get_barrier_semaphore()
    pl.semaphore_signal(barrier, inc=1, device_id={"head": 1 - core}, device_id_type=MESH)
    for step in range(1, reach + 1):

        @pl.when(step <= nright)
        def _():
            pl.semaphore_signal(barrier, inc=1, device_id={"ctx": me + step}, device_id_type=MESH)

        @pl.when(step <= nleft)
        def _():
            pl.semaphore_signal(barrier, inc=1, device_id={"ctx": me - step}, device_id_type=MESH)

    pl.semaphore_wait(barrier, 1 + nleft + nright)

    pairs = ((att_k, kall), (att_v, vall))

    def span(step):
        if step == reach:
            return pl.multiple_of(TILE + core * (TILE // 2), TILE // 2), TILE // 2
        return pl.multiple_of(core * TILE, TILE), TILE

    def kv_copy(which, step):
        start, size = span(step)
        source, target = pairs[which]
        return pltpu.make_async_remote_copy(
            src_ref=source.at[pl.ds(start, size)],
            dst_ref=target.at[pl.ds((reach - step) * length + start, size)],
            send_sem=kv_send.at[which, step - 1],
            recv_sem=kv_recv.at[which, step - 1],
            device_id={"ctx": me + step},
            device_id_type=MESH,
        )

    def pair_copy(which, step):
        start, size = span(step)
        target = pairs[which][1]
        place = pl.ds((reach - step) * length + start, size)
        return pltpu.make_async_remote_copy(
            src_ref=target.at[place],
            dst_ref=target.at[place],
            send_sem=pair_send.at[which, step - 1],
            recv_sem=pair_recv.at[which, step - 1],
            device_id={"head": 1 - core},
            device_id_type=MESH,
        )

    def pass_on(step):
        @pl.when(step <= nleft)
        def _():
            for which in range(2):
                kv_copy(which, step).wait_recv()
                pair_copy(which, step).start()

    def state_copy(side, step):
        return pltpu.make_async_remote_copy(
            src_ref=snd.at[side],
            dst_ref=got.at[side, step - 1],
            send_sem=st_send.at[side, step - 1],
            recv_sem=st_recv.at[side, step - 1],
            device_id={"ctx": me + step if side == 0 else me - step},
            device_id_type=MESH,
        )

    for step in range(1, reach + 1):

        @pl.when(step <= nright)
        def _():
            kv_copy(0, step).start()
            kv_copy(1, step).start()

    for load in loads:
        load.wait()
    follows, precedes, head_terms, t_sub, t_lane = decay_terms(me, count, nblocks, doc, dec)

    for b in range(nblocks):
        for a in range(4):
            wide[a] = raw[a, b * rows : (b + 1) * rows, :].astype(F32)
        for h in range(heads):
            row, col, total = head_terms(b, h)
            picked = [wide[a, pl.ds(h, TILE, stride=heads), :] for a in range(4)]
            for a in range(4):
                parts[a, b, h] = picked[a].astype(BF16)
            key_high, key_low = split((picked[1] * jnp.exp(total - col)).T)
            value = picked[2].astype(BF16)
            states[0, b, h] = dot_nn(key_high, value) + dot_nn(key_low, value)
            query_high, query_low = split((picked[0] * jnp.exp(col)).T)
            dol = picked[3].astype(BF16)
            states[1, b, h] = dot_nn(query_high, dol) + dot_nn(query_low, dol)

    for h in range(heads):
        keep = [jnp.exp(head_terms(b, h)[2]) for b in range(nblocks)]
        total_l = states[0, 0, h]
        mult_l = keep[0] * follows[0]
        for b in range(1, nblocks):
            total_l = states[0, b, h] + keep[b] * follows[b] * total_l
            mult_l = mult_l * keep[b] * follows[b]
        total_r = states[1, nblocks - 1, h]
        mult_r = keep[nblocks - 1] * precedes[nblocks - 1]
        for b in reversed(range(nblocks - 1)):
            total_r = states[1, b, h] + keep[b] * precedes[b] * total_r
            mult_r = mult_r * keep[b] * precedes[b]
        for side, total, mult in ((0, total_l, mult_l), (1, total_r, mult_r)):
            high, low = split(jnp.broadcast_to(mult, (16, width)))
            snd[side, h, 0:width, :] = total.astype(BF16)
            snd[side, h, width : width + 16, :] = high
            snd[side, h, width + 16 : width + 32, :] = low

    pass_on(1)
    pass_on(2)

    def within(b):
        for h in range(heads):
            row, col, total = head_terms(b, h)
            query, key, value, dol = (parts[a, b, h] for a in range(4))
            seen = t_sub <= t_lane
            weight = jnp.where(seen, jnp.exp(jnp.where(seen, row - col, 0.0)), 0.0)
            left = (dot_nt(value, dol) * weight).astype(BF16)
            right = (dot_nt(key, query) * weight).astype(BF16)
            grads[0, b, h] = dot_tn(left, key)
            grads[1, b, h] = dot_nn(left, query)
            grads[2, b, h] = dot_nn(right, dol)

    within(0)
    pass_on(3)
    pass_on(4)
    for b in range(1, nblocks):
        within(b)
    pass_on(5)
    pass_on(6)

    for step in range(1, reach + 1):
        for side, there in ((0, nright), (1, nleft)):

            @pl.when(step <= there)
            def _():
                state_copy(side, step).start()

        for side, there in ((0, nleft), (1, nright)):

            @pl.when(step > there)
            def _():
                got[side, step - 1] = jnp.zeros(got.shape[2:], BF16)

    for step in range(1, reach + 1):

        @pl.when(step <= nleft)
        def _():
            for which in range(2):
                pair_copy(which, step).wait_recv()

    def rows_of(j):
        return pl.ds(pl.multiple_of(j * TILE, TILE), TILE)

    sources = (dkey, dvalue)

    def grad_copy(which, step):
        return pltpu.make_async_remote_copy(
            src_ref=sources[which].at[rows_of((reach - step) * nblocks + 1 - core)],
            dst_ref=paired.at[which, step],
            send_sem=pg_send.at[which, step],
            recv_sem=pg_recv.at[which, step],
            device_id={"head": 1 - core},
            device_id_type=MESH,
        )

    def home_copy(step):
        return pltpu.make_async_remote_copy(
            src_ref=out.at[step - 1],
            dst_ref=inbox.at[step - 1],
            send_sem=home_send.at[step - 1],
            recv_sem=home_recv.at[step - 1],
            device_id={"ctx": me - step},
            device_id_type=MESH,
        )

    def mine(which, step):
        place = rows_of((reach - step) * nblocks + core)
        return sources[which][place, :] + paired[which, step]

    def send_home(step):
        for which in range(2):
            grad_copy(which, step).wait_recv()
        for which in range(2):
            out[step - 1, which] = mine(which, step).astype(BF16)
        home_copy(step).start()

    chunk = rows
    base = reach * nblocks
    dkey[rows_of(base + 1), :] = jnp.zeros((TILE, width), F32)
    dvalue[rows_of(base + 1), :] = jnp.zeros((TILE, width), F32)
    token = lax.broadcasted_iota(jnp.int32, (TILE, chunk), 1) // heads
    seen_q = lax.broadcasted_iota(jnp.int32, (TILE, chunk), 0) <= token

    def folded(x, op):
        return op(x.reshape(TILE // 8, 8, chunk), axis=0)

    def attend(b):
        diag = base + b
        first = jnp.maximum(b + 1, base - nblocks * nleft)
        queries = q[b * chunk : (b + 1) * chunk, :]
        douts = dout[b * chunk : (b + 1) * chunk, :]
        here = doc[me * nblocks + b]

        def hidden(j):
            at = jnp.clip(me * nblocks - base + j, 0, count * nblocks - 1)
            return jnp.where(doc[at] == here, 0.0, -NEG).astype(F32)

        def flip(j):
            flipped[j] = kall[rows_of(j), :].astype(F32).T.astype(BF16)

        s = jnp.where(seen_q, dot_nt(kall[rows_of(diag), :], queries), NEG)
        scores[diag - b - 1] = s
        flip(diag)

        def find_max(j, top):
            s = dot_nt(kall[rows_of(j), :], queries)
            scores[j - b - 1] = s
            if b == 0:
                flip(j)
            return jnp.maximum(top, folded(s, jnp.max) - hidden(j))

        top = lax.fori_loop(first, diag, find_max, folded(s, jnp.max))
        top = jnp.max(top, axis=0, keepdims=True) * factor

        def sums(j, carried):
            amount, weighted = carried
            p = jnp.exp2(scores[j - b - 1] * factor - (top + hidden(j)))
            g = dot_nt(vall[rows_of(j), :], douts)
            scores[j - b - 1] = p
            probs_grad[j - b - 1] = g
            return amount + folded(p, jnp.sum), weighted + folded(p * g, jnp.sum)

        zero = jnp.zeros((8, chunk), F32)
        amount, weighted = lax.fori_loop(first, diag + 1, sums, (zero, zero))
        inverse = 1.0 / jnp.sum(amount, axis=0, keepdims=True)
        delta = jnp.sum(weighted, axis=0, keepdims=True) * inverse

        def one(j, acc):
            p = scores[j - b - 1] * inverse
            g = p * (probs_grad[j - b - 1] - delta)
            p = p.astype(BF16)
            g = g.astype(BF16)
            at = rows_of(j)
            if b == 0:
                dvalue[at, :] = dot_nn(p, douts)
                dkey[at, :] = dot_nn(g, queries)
            else:
                dvalue[at, :] += dot_nn(p, douts)
                dkey[at, :] += dot_nn(g, queries)
            return acc + dot_nn(flipped[j], g)

        acc = jnp.zeros((width, chunk), F32)
        if b == 0:
            acc = lax.fori_loop(first, diag + 1, one, acc)
        else:
            last = jnp.minimum(nleft, reach - 1)

            def by_step(i, acc):
                step = last - i
                j = (reach - step) * nblocks
                acc = one(j + 1, one(j, acc))
                for which in range(2):
                    grad_copy(which, step).start()

                @pl.when(i > 0)
                def _():
                    send_home(step + 1)

                return acc

            acc = lax.fori_loop(0, last + 1, by_step, acc)
        att_dq[b * chunk : (b + 1) * chunk, :] = (acc.T * scale).astype(BF16)

    attend(0)
    far = nleft == reach

    @pl.when(jnp.logical_and(far, core == 0))
    def _():
        for which in range(2):
            grad_copy(which, reach).start()

    @pl.when(jnp.logical_and(far, core == 1))
    def _():
        send_home(reach)

    attend(1)

    for side, there in ((0, nleft), (1, nright)):
        for step in range(1, reach + 1):

            @pl.when(step <= there)
            def _():
                state_copy(side, step).wait_recv()

    for h in range(heads):
        ends = []
        for side in range(2):
            state = jnp.zeros((width, width), F32)
            for step in range(reach, 0, -1):
                mult = (
                    got[side, step - 1, h, width : width + 16, :].astype(F32)[0:1]
                    + got[side, step - 1, h, width + 16 : width + 32, :].astype(F32)[0:1]
                )
                state = got[side, step - 1, h, 0:width, :].astype(F32) + mult * state
            ends.append(state)
        keep = [jnp.exp(head_terms(b, h)[2]) for b in range(nblocks)]
        state = ends[0]
        into = []
        for b in range(nblocks):
            into.append(follows[b] * state)
            state = states[0, b, h] + keep[b] * into[b]
        state = ends[1]
        back = [None] * nblocks
        for b in reversed(range(nblocks)):
            back[b] = precedes[b] * state
            state = states[1, b, h] + keep[b] * back[b]
        for b in range(nblocks):
            row, col, total = head_terms(b, h)
            query, key, value, dol = (parts[a, b, h] for a in range(4))
            head_decay = jnp.exp(col)
            tail_decay = jnp.exp(total - col)
            into_high, into_low = split(into[b])
            back_high, back_low = split(back[b])
            at = pl.ds(b * rows + h, TILE, stride=heads)
            mixed[0, at, :] = grads[0, b, h] + head_decay * (
                dot_nt(dol, into_high) + dot_nt(dol, into_low)
            )
            mixed[1, at, :] = grads[1, b, h] + tail_decay * (
                dot_nt(value, back_high) + dot_nt(value, back_low)
            )
            mixed[2, at, :] = grads[2, b, h] + tail_decay * (
                dot_nn(key, back_high) + dot_nn(key, back_low)
            )
    lin_dq[...] = mixed[0].astype(BF16)
    lin_dk[...] = mixed[1].astype(BF16)
    lin_dv[...] = mixed[2].astype(BF16)

    for which in range(2):
        grad_copy(which, 0).wait_recv()
        paired[which, 0] = mine(which, 0)

    def takes(step, there, who):
        if step < reach:
            return step <= there
        return jnp.logical_and(step <= there, core == who)

    for step in range(1, reach + 1):

        @pl.when(takes(step, nright, 1))
        def _():
            home_copy(step).wait_recv()
            for which in range(2):
                paired[which, 0] += inbox[step - 1, which].astype(F32)

    att_dk[...] = (paired[0, 0] * scale).astype(BF16)
    att_dv[...] = paired[1, 0].astype(BF16)

    for which in range(2):
        grad_copy(which, 0).wait_send()
    for step in range(1, reach + 1):

        @pl.when(step <= nright)
        def _():
            for which in range(2):
                kv_copy(which, step).wait_send()
            state_copy(0, step).wait_send()

        @pl.when(step <= nleft)
        def _():
            for which in range(2):
                pair_copy(which, step).wait_send()
            state_copy(1, step).wait_send()

        @pl.when(takes(step, nleft, 0))
        def _():
            for which in range(2):
                grad_copy(which, step).wait_send()

        @pl.when(takes(step, nleft, 1))
        def _():
            home_copy(step).wait_send()


def shards(count, lin_q, lin_k, lin_v, lin_dout, lin_decay, att_q, att_k, att_v, att_dout, doc_block):
    length, heads, width = lin_q.shape
    nblocks = length // TILE
    assert nblocks == 2
    reach = -(-(MOST - 1) // nblocks)
    rows = length * heads
    window = (reach + 1) * length
    flat = lambda x: x.reshape(rows, width)
    outs = pl.pallas_call(
        functools.partial(whole_kernel, count, reach, heads, nblocks),
        out_shape=[SHAPE((rows, width), BF16)] * 4 + [SHAPE((TILE, width), BF16)] * 2,
        in_specs=[IN_SMEM] + [ANYWHERE] * 9,
        out_specs=[IN_VMEM] * 6,
        scratch_shapes=[
            pltpu.VMEM((4, TILE * heads, width), F32),
            pltpu.VMEM((4, rows, width), BF16),
            pltpu.VMEM(lin_decay.shape, F32),
            pltpu.VMEM((rows, width), BF16),
            pltpu.VMEM((rows, width), BF16),
            pltpu.VMEM((window, width), BF16),
            pltpu.VMEM((window, width), BF16),
            pltpu.VMEM((4, nblocks, heads, TILE, width), BF16),
            pltpu.VMEM((2, nblocks, heads, width, width), F32),
            pltpu.VMEM((3, nblocks, heads, TILE, width), F32),
            pltpu.VMEM((3, rows, width), F32),
            pltpu.VMEM((MOST, TILE, TILE * heads), F32),
            pltpu.VMEM((MOST, TILE, TILE * heads), F32),
            pltpu.VMEM((window // TILE, width, TILE), BF16),
            pltpu.VMEM((window, width), F32),
            pltpu.VMEM((window, width), F32),
            pltpu.VMEM((2, heads, width + 32, width), BF16),
            pltpu.VMEM((2, reach, heads, width + 32, width), BF16),
            pltpu.VMEM((2, reach + 1, TILE, width), F32),
            pltpu.VMEM((reach, 2, TILE, width), BF16),
            pltpu.VMEM((reach, 2, TILE, width), BF16),
            DMA((9,)),
            DMA((2, reach)),
            DMA((2, reach)),
            DMA((2, reach)),
            DMA((2, reach)),
            DMA((2, reach)),
            DMA((2, reach)),
            DMA((2, reach + 1)),
            DMA((2, reach + 1)),
            DMA((reach,)),
            DMA((reach,)),
        ],
        compiler_params=pltpu.CompilerParams(
            collective_id=0, has_side_effects=True, vmem_limit_bytes=VMEM_LIMIT
        ),
        name="whole",
    )(
        doc_block, flat(lin_q), flat(lin_k), flat(lin_v), flat(lin_dout), lin_decay,
        flat(att_q), flat(att_dout), att_k, att_v,
    )
    full = lambda x: x.reshape(length, heads, width)
    return (full(outs[0]), full(outs[1]), full(outs[2]), full(outs[3]), outs[4], outs[5])


def solution(mesh):
    return jax.shard_map(
        functools.partial(shards, mesh.shape["ctx"]),
        mesh=mesh,
        in_specs=(
            P("ctx", "head", None),
            P("ctx", "head", None),
            P("ctx", "head", None),
            P("ctx", "head", None),
            P("head", "ctx"),
            P("ctx", "head", None),
            P("ctx", None),
            P("ctx", None),
            P("ctx", "head", None),
            P(),
        ),
        out_specs=(
            P("ctx", "head", None),
            P("ctx", "head", None),
            P("ctx", "head", None),
            P("ctx", "head", None),
            P(("ctx", "head"), None),
            P(("ctx", "head"), None),
        ),
        check_vma=False,
    )
```

```python
import functools
import math

import jax
import jax.numpy as jnp
from jax import lax
from jax.experimental import pallas as pl
from jax.experimental.pallas import tpu as pltpu
from jax.sharding import PartitionSpec as P

TILE = 256
MOST = 12
SHORT = 8
NEG = -1e30
MESH = pl.DeviceIdType.MESH
F32 = jnp.float32
BF16 = jnp.bfloat16
SHAPE = jax.ShapeDtypeStruct
DMA = pltpu.SemaphoreType.DMA
IN_VMEM = pl.BlockSpec(memory_space=pltpu.VMEM)
IN_SMEM = pl.BlockSpec(memory_space=pltpu.SMEM)
ANYWHERE = pl.BlockSpec(memory_space=pl.ANY)
VMEM_LIMIT = 60 * 1024 * 1024


def dot_nn(a, b):
    return lax.dot_general(a, b, (((1,), (0,)), ((), ())), preferred_element_type=F32)


def dot_nt(a, b):
    return lax.dot_general(a, b, (((1,), (1,)), ((), ())), preferred_element_type=F32)


def dot_tn(a, b):
    return lax.dot_general(a, b, (((0,), (0,)), ((), ())), preferred_element_type=F32)


def split(x):
    high = x.astype(BF16)
    return high, (x - high.astype(F32)).astype(BF16)


def decay_terms(me, count, nblocks, doc, dec):
    t_sub = lax.broadcasted_iota(jnp.int32, (TILE, TILE), 0)
    t_lane = lax.broadcasted_iota(jnp.int32, (TILE, TILE), 1)
    upper = (t_sub <= t_lane).astype(F32)
    lower = (t_sub >= t_lane).astype(F32)

    def link(at_one, at_two):
        one = jnp.clip(at_one, 0, count * nblocks - 1)
        two = jnp.clip(at_two, 0, count * nblocks - 1)
        inside = jnp.logical_and(at_one >= 0, at_two < count * nblocks)
        same = jnp.logical_and(doc[one] == doc[two], inside)
        return jnp.where(same, 1.0, 0.0).astype(F32)

    follows = [link(me * nblocks + b - 1, me * nblocks + b) for b in range(nblocks)]
    precedes = [link(me * nblocks + b, me * nblocks + b + 1) for b in range(nblocks)]

    cum_row, cum_col = [], []
    for b in range(nblocks):
        piece = dec[:, b * TILE : (b + 1) * TILE]
        cum_row.append(
            lax.dot_general(
                piece, upper, (((1,), (0,)), ((), ())),
                preferred_element_type=F32, precision=lax.Precision.HIGHEST,
            )
        )
        cum_col.append(
            lax.dot_general(
                lower, piece, (((1,), (1,)), ((), ())),
                preferred_element_type=F32, precision=lax.Precision.HIGHEST,
            )
        )

    def head_terms(b, h):
        row = cum_row[b][h : h + 1, :]
        col = cum_col[b][:, h : h + 1]
        total = col[TILE - 1 : TILE, :]
        return row, col, total

    return follows, precedes, head_terms, t_sub, t_lane


def whole_kernel(
    count, limit, heads, nblocks,
    doc, lq, lk, lv, ld, dec_in, aq, ado, att_k, att_v,
    lin_dq, lin_dk, lin_dv, att_dq, att_dk, att_dv,
    wide, raw, dec, q, dout, kall, vall, parts, states, local, grads, mixed,
    scores, probs_grad, flipped, dkey, dvalue,
    snd, got, paired, out, inbox,
    raw_sem, kv_send, kv_recv, pair_send, pair_recv, st_send, st_recv,
    pg_send, pg_recv, home_send, home_recv,
):
    me = lax.axis_index("ctx")
    core = lax.axis_index("head")
    length = nblocks * TILE
    width = lq.shape[1]
    rows = TILE * heads
    first_devs = MOST // nblocks
    in_first = me < first_devs
    later_reach = limit // nblocks
    reach = slots_of(limit, nblocks)
    most = jnp.where(in_first, first_devs - 1, later_reach)
    nleft = jnp.minimum(jnp.where(in_first, me, me - first_devs), most)
    nright = jnp.minimum(jnp.where(in_first, first_devs - 1 - me, count - 1 - me), most)
    span = jnp.where(in_first, MOST, limit)

    def takes(step, there, who):
        if isinstance(step, int) and step != later_reach:
            return step <= there
        far = jnp.logical_and(step == later_reach, jnp.logical_not(in_first))
        return jnp.logical_and(step <= there, jnp.logical_or(jnp.logical_not(far), core == who))

    scale = width ** (-0.5)
    factor = scale * math.log2(math.e)

    loads = [
        pltpu.make_async_copy(ref, raw.at[a], raw_sem.at[a])
        for a, ref in enumerate((lq, lk, lv, ld))
    ]
    loads.append(pltpu.make_async_copy(dec_in, dec, raw_sem.at[4]))
    loads.append(pltpu.make_async_copy(aq, q, raw_sem.at[5]))
    loads.append(pltpu.make_async_copy(ado, dout, raw_sem.at[6]))
    own_rows = pl.ds(reach * length, length)
    loads.append(pltpu.make_async_copy(att_k, kall.at[own_rows], raw_sem.at[7]))
    loads.append(pltpu.make_async_copy(att_v, vall.at[own_rows], raw_sem.at[8]))
    for load in loads:
        load.start()

    barrier = pltpu.get_barrier_semaphore()
    pl.semaphore_signal(barrier, inc=1, device_id={"head": 1 - core}, device_id_type=MESH)
    for step in range(1, reach + 1):

        @pl.when(step <= nright)
        def _():
            pl.semaphore_signal(barrier, inc=1, device_id={"ctx": me + step}, device_id_type=MESH)

        @pl.when(step <= nleft)
        def _():
            pl.semaphore_signal(barrier, inc=1, device_id={"ctx": me - step}, device_id_type=MESH)

    pl.semaphore_wait(barrier, 1 + nleft + nright)

    pairs = ((att_k, kall), (att_v, vall))

    def half_of(step):
        start = pl.multiple_of(core * TILE, TILE)
        return start, pl.ds((reach - step) * length + start, TILE)

    def kv_copy(which, step):
        start, place = half_of(step)
        source, target = pairs[which]
        return pltpu.make_async_remote_copy(
            src_ref=source.at[pl.ds(start, TILE)],
            dst_ref=target.at[place],
            send_sem=kv_send.at[which, step - 1],
            recv_sem=kv_recv.at[which, step - 1],
            device_id={"ctx": me + step},
            device_id_type=MESH,
        )

    def pair_copy(which, step):
        target = pairs[which][1]
        place = half_of(step)[1]
        return pltpu.make_async_remote_copy(
            src_ref=target.at[place],
            dst_ref=target.at[place],
            send_sem=pair_send.at[which, step - 1],
            recv_sem=pair_recv.at[which, step - 1],
            device_id={"head": 1 - core},
            device_id_type=MESH,
        )

    def pass_on(which, steps):
        for step in steps:
            if step <= reach:

                @pl.when(takes(step, nleft, 1))
                def _():
                    kv_copy(which, step).wait_recv()
                    pair_copy(which, step).start()

    def pair_wait(which):
        for step in range(1, reach + 1):

            @pl.when(takes(step, nleft, 0))
            def _():
                pair_copy(which, step).wait_recv()

    hops = ((1, 2), (1, 4))

    def state_copy(trip, side, k):
        hop = hops[trip][k]
        return pltpu.make_async_remote_copy(
            src_ref=snd.at[trip, side],
            dst_ref=got.at[trip, side, k],
            send_sem=st_send.at[trip, side, k],
            recv_sem=st_recv.at[trip, side, k],
            device_id={"ctx": me + hop if side == 0 else me - hop},
            device_id_type=MESH,
        )

    def state_start(trip):
        for k, hop in enumerate(hops[trip]):
            for side, there in ((0, nright), (1, nleft)):

                @pl.when(hop <= there)
                def _():
                    state_copy(trip, side, k).start()

            for side, there in ((0, nleft), (1, nright)):

                @pl.when(hop > there)
                def _():
                    got[trip, side, k] = jnp.zeros(got.shape[3:], BF16)

    def state_wait(trip):
        for k, hop in enumerate(hops[trip]):
            for side, there in ((0, nleft), (1, nright)):

                @pl.when(hop <= there)
                def _():
                    state_copy(trip, side, k).wait_recv()

    def state_write(trip, side, totals, mults):
        pads = []
        for h in range(heads):
            snd[trip, side, h * width : (h + 1) * width, :] = totals[h].astype(BF16)
            high, low = split(jnp.broadcast_to(mults[h], (1, width)))
            pads.append((high.astype(F32), low.astype(F32)))
        rows16 = [pads[h][0] for h in range(heads)] + [pads[h][1] for h in range(heads)]
        rows16.append(jnp.zeros((16 - 2 * heads, width), F32))
        snd[trip, side, heads * width :, :] = jnp.concatenate(rows16, axis=0).astype(BF16)

    def state_read(trip, side, k, h):
        at = heads * width
        total = got[trip, side, k, h * width : (h + 1) * width, :].astype(F32)
        pads = got[trip, side, k, at : at + 16, :].astype(F32)
        return total, pads[h : h + 1] + pads[heads + h : heads + h + 1]

    for which in range(2):
        for step in range(1, reach + 1):

            @pl.when(takes(step, nright, 1))
            def _():
                kv_copy(which, step).start()

    for load in loads:
        load.wait()
    follows, precedes, head_terms, t_sub, t_lane = decay_terms(me, count, nblocks, doc, dec)

    for b in range(nblocks):
        for a in range(4):
            wide[a] = raw[a, b * rows : (b + 1) * rows, :].astype(F32)
        for h in range(heads):
            row, col, total = head_terms(b, h)
            picked = [wide[a, pl.ds(h, TILE, stride=heads), :] for a in range(4)]
            for a in range(4):
                parts[a, b, h] = picked[a].astype(BF16)
            key_high, key_low = split((picked[1] * jnp.exp(total - col)).T)
            value = picked[2].astype(BF16)
            states[0, b, h] = dot_nn(key_high, value) + dot_nn(key_low, value)
            query_high, query_low = split((picked[0] * jnp.exp(col)).T)
            dol = picked[3].astype(BF16)
            states[1, b, h] = dot_nn(query_high, dol) + dot_nn(query_low, dol)

    totals, mults = ([], []), ([], [])
    for h in range(heads):
        keep = [jnp.exp(head_terms(b, h)[2]) for b in range(nblocks)]
        total_l = states[0, 0, h]
        mult_l = keep[0] * follows[0]
        for b in range(1, nblocks):
            total_l = states[0, b, h] + keep[b] * follows[b] * total_l
            mult_l = mult_l * keep[b] * follows[b]
        total_r = states[1, nblocks - 1, h]
        mult_r = keep[nblocks - 1] * precedes[nblocks - 1]
        for b in reversed(range(nblocks - 1)):
            total_r = states[1, b, h] + keep[b] * precedes[b] * total_r
            mult_r = mult_r * keep[b] * precedes[b]
        for side, total, mult in ((0, total_l, mult_l), (1, total_r, mult_r)):
            totals[side].append(total)
            mults[side].append(mult)
            local[side, h] = total
    for side in range(2):
        state_write(0, side, totals[side], mults[side])

    def state_join():
        state_wait(0)
        for side in range(2):
            joined, spans = [], []
            for h in range(heads):
                one, mult_one = state_read(0, side, 0, h)
                two, mult_two = state_read(0, side, 1, h)
                joined.append(local[side, h] + mults[side][h] * (one + mult_one * two))
                spans.append(mults[side][h] * mult_one * mult_two)
            state_write(1, side, joined, spans)
        state_start(1)

    pass_on(0, (1, 2))

    def within(b):
        for h in range(heads):
            row, col, total = head_terms(b, h)
            query, key, value, dol = (parts[a, b, h] for a in range(4))
            seen = t_sub <= t_lane
            weight = jnp.where(seen, jnp.exp(jnp.where(seen, row - col, 0.0)), 0.0)
            left = (dot_nt(value, dol) * weight).astype(BF16)
            right = (dot_nt(key, query) * weight).astype(BF16)
            grads[0, b, h] = dot_tn(left, key)
            grads[1, b, h] = dot_nn(left, query)
            grads[2, b, h] = dot_nn(right, dol)

    within(0)
    pass_on(0, (3, 4))
    for b in range(1, nblocks):
        within(b)
    pass_on(0, (5, 6))
    pair_wait(0)

    def rows_of(j):
        return pl.ds(pl.multiple_of(j * TILE, TILE), TILE)

    sources = (dkey, dvalue)

    def grad_copy(which, step):
        return pltpu.make_async_remote_copy(
            src_ref=sources[which].at[rows_of((reach - step) * nblocks + 1 - core)],
            dst_ref=paired.at[which, step],
            send_sem=pg_send.at[which, step],
            recv_sem=pg_recv.at[which, step],
            device_id={"head": 1 - core},
            device_id_type=MESH,
        )

    def home_copy(step):
        return pltpu.make_async_remote_copy(
            src_ref=out.at[step - 1],
            dst_ref=inbox.at[step - 1],
            send_sem=home_send.at[step - 1],
            recv_sem=home_recv.at[step - 1],
            device_id={"ctx": me - step},
            device_id_type=MESH,
        )

    def mine(which, step):
        place = rows_of((reach - step) * nblocks + core)
        return sources[which][place, :] + paired[which, step]

    def send_home(step):
        for which in range(2):
            grad_copy(which, step).wait_recv()
        for which in range(2):
            out[step - 1, which] = mine(which, step).astype(BF16)
        home_copy(step).start()

    chunk = rows
    base = reach * nblocks
    dkey[rows_of(base + 1), :] = jnp.zeros((TILE, width), F32)
    dvalue[rows_of(base + 1), :] = jnp.zeros((TILE, width), F32)
    token = lax.broadcasted_iota(jnp.int32, (TILE, chunk), 1) // heads
    seen_q = lax.broadcasted_iota(jnp.int32, (TILE, chunk), 0) <= token

    def folded(x, op):
        return op(x.reshape(TILE // 8, 8, chunk), axis=0)

    def attend(b):
        diag = base + b
        first = jnp.maximum(base + b + 1 - span, base - nblocks * nleft)
        queries = q[b * chunk : (b + 1) * chunk, :]
        douts = dout[b * chunk : (b + 1) * chunk, :]
        here = doc[me * nblocks + b]

        def hidden(j):
            at = jnp.clip(me * nblocks - base + j, 0, count * nblocks - 1)
            return jnp.where(doc[at] == here, 0.0, -NEG).astype(F32)

        def flip(j):
            flipped[j] = kall[rows_of(j), :].astype(F32).T.astype(BF16)

        s = jnp.where(seen_q, dot_nt(kall[rows_of(diag), :], queries), NEG)
        scores[diag - first] = s
        flip(diag)

        def find_max(j, top):
            s = dot_nt(kall[rows_of(j), :], queries)
            scores[j - first] = s
            if b == 0:
                flip(j)
            return jnp.maximum(top, folded(s, jnp.max) - hidden(j))

        top = lax.fori_loop(first, diag, find_max, folded(s, jnp.max))
        top = jnp.max(top, axis=0, keepdims=True) * factor
        if b == 0:
            pass_on(1, range(1, reach + 1))
            pair_wait(1)
            state_start(0)

        def sums(j, carried):
            amount, weighted = carried
            p = jnp.exp2(scores[j - first] * factor - (top + hidden(j)))
            g = dot_nt(vall[rows_of(j), :], douts)
            scores[j - first] = p
            probs_grad[j - first] = g
            return amount + folded(p, jnp.sum), weighted + folded(p * g, jnp.sum)

        zero = jnp.zeros((8, chunk), F32)
        amount, weighted = lax.fori_loop(first, diag + 1, sums, (zero, zero))
        inverse = 1.0 / jnp.sum(amount, axis=0, keepdims=True)
        delta = jnp.sum(weighted, axis=0, keepdims=True) * inverse

        def one(j, acc):
            p = scores[j - first] * inverse
            g = p * (probs_grad[j - first] - delta)
            p = p.astype(BF16)
            g = g.astype(BF16)
            at = rows_of(j)
            if b == 0:
                dvalue[at, :] = dot_nn(p, douts)
                dkey[at, :] = dot_nn(g, queries)
            else:
                dvalue[at, :] += dot_nn(p, douts)
                dkey[at, :] += dot_nn(g, queries)
            return acc + dot_nn(flipped[j], g)

        acc = jnp.zeros((width, chunk), F32)
        if b == 0:
            acc = lax.fori_loop(first, diag + 1, one, acc)
        else:
            last = jnp.minimum(nleft, jnp.where(in_first, reach, later_reach - 1))

            def by_step(i, acc):
                step = last - i
                j = (reach - step) * nblocks
                acc = one(j + 1, one(j, acc))
                for which in range(2):
                    grad_copy(which, step).start()

                @pl.when(i > 0)
                def _():
                    send_home(step + 1)

                return acc

            acc = lax.fori_loop(0, last + 1, by_step, acc)
        att_dq[b * chunk : (b + 1) * chunk, :] = (acc.T * scale).astype(BF16)

    attend(0)
    state_join()
    far = jnp.logical_and(jnp.logical_not(in_first), nleft == later_reach)

    @pl.when(jnp.logical_and(far, core == 0))
    def _():
        for which in range(2):
            grad_copy(which, later_reach).start()

    @pl.when(jnp.logical_and(far, core == 1))
    def _():
        send_home(later_reach)

    attend(1)
    state_wait(1)

    for h in range(heads):
        ends = []
        for side in range(2):
            near, mult = state_read(1, side, 0, h)
            state = near + mult * state_read(1, side, 1, h)[0]
            ends.append(state)
        keep = [jnp.exp(head_terms(b, h)[2]) for b in range(nblocks)]
        state = ends[0]
        into = []
        for b in range(nblocks):
            into.append(follows[b] * state)
            state = states[0, b, h] + keep[b] * into[b]
        state = ends[1]
        back = [None] * nblocks
        for b in reversed(range(nblocks)):
            back[b] = precedes[b] * state
            state = states[1, b, h] + keep[b] * back[b]
        for b in range(nblocks):
            row, col, total = head_terms(b, h)
            query, key, value, dol = (parts[a, b, h] for a in range(4))
            head_decay = jnp.exp(col)
            tail_decay = jnp.exp(total - col)
            into_high, into_low = split(into[b])
            back_high, back_low = split(back[b])
            at = pl.ds(b * rows + h, TILE, stride=heads)
            mixed[0, at, :] = grads[0, b, h] + head_decay * (
                dot_nt(dol, into_high) + dot_nt(dol, into_low)
            )
            mixed[1, at, :] = grads[1, b, h] + tail_decay * (
                dot_nt(value, back_high) + dot_nt(value, back_low)
            )
            mixed[2, at, :] = grads[2, b, h] + tail_decay * (
                dot_nn(key, back_high) + dot_nn(key, back_low)
            )
    lin_dq[...] = mixed[0].astype(BF16)
    lin_dk[...] = mixed[1].astype(BF16)
    lin_dv[...] = mixed[2].astype(BF16)

    for which in range(2):
        grad_copy(which, 0).wait_recv()
        paired[which, 0] = mine(which, 0)

    for step in range(1, reach + 1):

        @pl.when(takes(step, nright, 1))
        def _():
            home_copy(step).wait_recv()
            for which in range(2):
                paired[which, 0] += inbox[step - 1, which].astype(F32)

    att_dk[...] = (paired[0, 0] * scale).astype(BF16)
    att_dv[...] = paired[1, 0].astype(BF16)

    for which in range(2):
        grad_copy(which, 0).wait_send()
    for trip in range(2):
        for k, hop in enumerate(hops[trip]):
            for side, there in ((0, nright), (1, nleft)):

                @pl.when(hop <= there)
                def _():
                    state_copy(trip, side, k).wait_send()

    for step in range(1, reach + 1):

        @pl.when(takes(step, nright, 1))
        def _():
            for which in range(2):
                kv_copy(which, step).wait_send()

        @pl.when(takes(step, nleft, 1))
        def _():
            for which in range(2):
                pair_copy(which, step).wait_send()
            home_copy(step).wait_send()

        @pl.when(takes(step, nleft, 0))
        def _():
            for which in range(2):
                grad_copy(which, step).wait_send()


def slots_of(limit, nblocks):
    return max(MOST // nblocks - 1, limit // nblocks)


def place_kernel(*refs):
    half = (len(refs) - 1) // 2
    sems = refs[-1]
    moves = [
        pltpu.make_async_copy(refs[i], refs[half + i], sems.at[i]) for i in range(half)
    ]
    for move in moves:
        move.start()
    for move in moves:
        move.wait()


def place(outs):
    return pl.pallas_call(
        place_kernel,
        out_shape=[SHAPE(x.shape, x.dtype) for x in outs],
        in_specs=[ANYWHERE] * len(outs),
        out_specs=[ANYWHERE] * len(outs),
        scratch_shapes=[DMA((len(outs),))],
        name="place",
    )(*outs)


def call_whole(count, limit, heads, nblocks, args):
    width = args[-1].shape[1]
    rows = nblocks * TILE * heads
    reach = slots_of(limit, nblocks)
    window = (reach + 1) * nblocks * TILE
    return pl.pallas_call(
        functools.partial(whole_kernel, count, limit, heads, nblocks),
        out_shape=[SHAPE((rows, width), BF16)] * 4 + [SHAPE((TILE, width), BF16)] * 2,
        in_specs=[IN_SMEM] + [ANYWHERE] * 9,
        out_specs=[IN_VMEM] * 6,
        scratch_shapes=[
            pltpu.VMEM((4, TILE * heads, width), F32),
            pltpu.VMEM((4, rows, width), BF16),
            pltpu.VMEM((heads, nblocks * TILE), F32),
            pltpu.VMEM((rows, width), BF16),
            pltpu.VMEM((rows, width), BF16),
            pltpu.VMEM((window, width), BF16),
            pltpu.VMEM((window, width), BF16),
            pltpu.VMEM((4, nblocks, heads, TILE, width), BF16),
            pltpu.VMEM((2, nblocks, heads, width, width), F32),
            pltpu.VMEM((2, heads, width, width), F32),
            pltpu.VMEM((3, nblocks, heads, TILE, width), F32),
            pltpu.VMEM((3, rows, width), F32),
            pltpu.VMEM((MOST, TILE, TILE * heads), F32),
            pltpu.VMEM((MOST, TILE, TILE * heads), F32),
            pltpu.VMEM((window // TILE, width, TILE), BF16),
            pltpu.VMEM((window, width), F32),
            pltpu.VMEM((window, width), F32),
            pltpu.VMEM((2, 2, heads * width + 16, width), BF16),
            pltpu.VMEM((2, 2, 2, heads * width + 16, width), BF16),
            pltpu.VMEM((2, reach + 1, TILE, width), F32),
            pltpu.VMEM((reach, 2, TILE, width), BF16),
            pltpu.VMEM((reach, 2, TILE, width), BF16),
            DMA((9,)),
            DMA((2, reach)),
            DMA((2, reach)),
            DMA((2, reach)),
            DMA((2, reach)),
            DMA((2, 2, 2)),
            DMA((2, 2, 2)),
            DMA((2, reach + 1)),
            DMA((2, reach + 1)),
            DMA((reach,)),
            DMA((reach,)),
        ],
        compiler_params=pltpu.CompilerParams(
            collective_id=0 if limit == MOST else 1,
            has_side_effects=True,
            vmem_limit_bytes=VMEM_LIMIT,
        ),
        name="whole_%d" % limit,
    )(*args)


def shards(count, lin_q, lin_k, lin_v, lin_dout, lin_decay, att_q, att_k, att_v, att_dout, doc_block):
    length, heads, width = lin_q.shape
    nblocks = length // TILE
    assert nblocks == 2
    flat = lambda x: x.reshape(length * heads, width)
    args = (
        doc_block, flat(lin_q), flat(lin_k), flat(lin_v), flat(lin_dout), lin_decay,
        flat(att_q), flat(att_dout), att_k, att_v,
    )
    later = doc_block[MOST:]
    long = jnp.any(later[SHORT:] == later[:-SHORT])
    outs = lax.cond(
        long,
        lambda *a: call_whole(count, MOST, heads, nblocks, a),
        lambda *a: call_whole(count, SHORT, heads, nblocks, a),
        *args,
    )
    outs = place(outs)
    full = lambda x: x.reshape(length, heads, width)
    return (full(outs[0]), full(outs[1]), full(outs[2]), full(outs[3]), outs[4], outs[5])


def solution(mesh):
    return jax.shard_map(
        functools.partial(shards, mesh.shape["ctx"]),
        mesh=mesh,
        in_specs=(
            P("ctx", "head", None),
            P("ctx", "head", None),
            P("ctx", "head", None),
            P("ctx", "head", None),
            P("head", "ctx"),
            P("ctx", "head", None),
            P("ctx", None),
            P("ctx", None),
            P("ctx", "head", None),
            P(),
        ),
        out_specs=(
            P("ctx", "head", None),
            P("ctx", "head", None),
            P("ctx", "head", None),
            P("ctx", "head", None),
            P(("ctx", "head"), None),
            P(("ctx", "head"), None),
        ),
        check_vma=False,
    )
```

```python
import functools
import math

import jax
import jax.numpy as jnp
from jax import lax
from jax.experimental import pallas as pl
from jax.experimental.pallas import tpu as pltpu
from jax.sharding import PartitionSpec as P

TILE = 256
MOST = 12
SHORT = 8
NEG = -1e30
MESH = pl.DeviceIdType.MESH
F32 = jnp.float32
BF16 = jnp.bfloat16
SHAPE = jax.ShapeDtypeStruct
DMA = pltpu.SemaphoreType.DMA
IN_VMEM = pl.BlockSpec(memory_space=pltpu.VMEM)
IN_SMEM = pl.BlockSpec(memory_space=pltpu.SMEM)
ANYWHERE = pl.BlockSpec(memory_space=pl.ANY)
VMEM_LIMIT = 62 * 1024 * 1024


def dot_nn(a, b):
    return lax.dot_general(a, b, (((1,), (0,)), ((), ())), preferred_element_type=F32)


def dot_nt(a, b):
    return lax.dot_general(a, b, (((1,), (1,)), ((), ())), preferred_element_type=F32)


def dot_tn(a, b):
    return lax.dot_general(a, b, (((0,), (0,)), ((), ())), preferred_element_type=F32)


def split(x):
    high = x.astype(BF16)
    return high, (x - high.astype(F32)).astype(BF16)


def decay_terms(me, count, nblocks, doc, dec):
    t_sub = lax.broadcasted_iota(jnp.int32, (TILE, TILE), 0)
    t_lane = lax.broadcasted_iota(jnp.int32, (TILE, TILE), 1)
    upper = (t_sub <= t_lane).astype(F32)
    lower = (t_sub >= t_lane).astype(F32)

    def link(at_one, at_two):
        one = jnp.clip(at_one, 0, count * nblocks - 1)
        two = jnp.clip(at_two, 0, count * nblocks - 1)
        inside = jnp.logical_and(at_one >= 0, at_two < count * nblocks)
        same = jnp.logical_and(doc[one] == doc[two], inside)
        return jnp.where(same, 1.0, 0.0).astype(F32)

    follows = [link(me * nblocks + b - 1, me * nblocks + b) for b in range(nblocks)]
    precedes = [link(me * nblocks + b, me * nblocks + b + 1) for b in range(nblocks)]

    cum_row, cum_col = [], []
    for b in range(nblocks):
        piece = dec[:, b * TILE : (b + 1) * TILE]
        cum_row.append(
            lax.dot_general(
                piece, upper, (((1,), (0,)), ((), ())),
                preferred_element_type=F32, precision=lax.Precision.HIGHEST,
            )
        )
        cum_col.append(
            lax.dot_general(
                lower, piece, (((1,), (1,)), ((), ())),
                preferred_element_type=F32, precision=lax.Precision.HIGHEST,
            )
        )

    def head_terms(b, h):
        row = cum_row[b][h : h + 1, :]
        col = cum_col[b][:, h : h + 1]
        total = col[TILE - 1 : TILE, :]
        return row, col, total

    return follows, precedes, head_terms, t_sub, t_lane


def whole_kernel(
    count, limit, heads, nblocks,
    doc, lq, lk, lv, ld, dec_in, aq, ado, att_k, att_v,
    lin_dq, lin_dk, lin_dv, att_dq, att_dk, att_dv,
    wide, raw, dec, q, dout, kall, vall, parts, states, local, grads, mixed,
    scores, probs_grad, peaks, top_ref, amount_ref, weighted_ref, dq_sum, flipped, dkey, dvalue,
    snd, got, paired, out, inbox,
    raw_sem, kv_send, kv_recv, pair_send, pair_recv, st_send, st_recv,
    pg_send, pg_recv, home_send, home_recv,
):
    me = lax.axis_index("ctx")
    carry = (top_ref, amount_ref, weighted_ref)
    core = lax.axis_index("head")
    length = nblocks * TILE
    width = lq.shape[1]
    rows = TILE * heads
    first_devs = MOST // nblocks
    in_first = me < first_devs
    later_reach = limit // nblocks
    reach = slots_of(limit, nblocks)
    most = jnp.where(in_first, first_devs - 1, later_reach)
    nleft = jnp.minimum(jnp.where(in_first, me, me - first_devs), most)
    nright = jnp.minimum(jnp.where(in_first, first_devs - 1 - me, count - 1 - me), most)
    span = jnp.where(in_first, MOST, limit)

    def takes(step, there, who):
        if isinstance(step, int) and step != later_reach:
            return step <= there
        far = jnp.logical_and(step == later_reach, jnp.logical_not(in_first))
        return jnp.logical_and(step <= there, jnp.logical_or(jnp.logical_not(far), core == who))

    scale = width ** (-0.5)
    factor = scale * math.log2(math.e)

    loads = [
        pltpu.make_async_copy(ref, raw.at[a], raw_sem.at[a])
        for a, ref in enumerate((lq, lk, lv, ld))
    ]
    loads.append(pltpu.make_async_copy(dec_in, dec, raw_sem.at[4]))
    loads.append(pltpu.make_async_copy(aq, q, raw_sem.at[5]))
    loads.append(pltpu.make_async_copy(ado, dout, raw_sem.at[6]))
    own_rows = pl.ds(reach * length, length)
    loads.append(pltpu.make_async_copy(att_k, kall.at[own_rows], raw_sem.at[7]))
    loads.append(pltpu.make_async_copy(att_v, vall.at[own_rows], raw_sem.at[8]))
    for load in loads:
        load.start()

    barrier = pltpu.get_barrier_semaphore()
    pl.semaphore_signal(barrier, inc=1, device_id={"head": 1 - core}, device_id_type=MESH)
    for step in range(1, reach + 1):

        @pl.when(step <= nright)
        def _():
            pl.semaphore_signal(barrier, inc=1, device_id={"ctx": me + step}, device_id_type=MESH)

        @pl.when(step <= nleft)
        def _():
            pl.semaphore_signal(barrier, inc=1, device_id={"ctx": me - step}, device_id_type=MESH)

    pl.semaphore_wait(barrier, 1 + nleft + nright)

    pairs = ((att_k, kall), (att_v, vall))

    def half_of(step):
        start = pl.multiple_of(core * TILE, TILE)
        return start, pl.ds((reach - step) * length + start, TILE)

    def kv_copy(which, step):
        start, place = half_of(step)
        source, target = pairs[which]
        return pltpu.make_async_remote_copy(
            src_ref=source.at[pl.ds(start, TILE)],
            dst_ref=target.at[place],
            send_sem=kv_send.at[which, step - 1],
            recv_sem=kv_recv.at[which, step - 1],
            device_id={"ctx": me + step},
            device_id_type=MESH,
        )

    def pair_copy(which, step):
        target = pairs[which][1]
        place = half_of(step)[1]
        return pltpu.make_async_remote_copy(
            src_ref=target.at[place],
            dst_ref=target.at[place],
            send_sem=pair_send.at[which, step - 1],
            recv_sem=pair_recv.at[which, step - 1],
            device_id={"head": 1 - core},
            device_id_type=MESH,
        )

    def pass_on(step):
        @pl.when(takes(step, nleft, 1))
        def _():
            for which in range(2):
                kv_copy(which, step).wait_recv()
                pair_copy(which, step).start()

    def pair_wait(step):
        for which in range(2):
            pair_copy(which, step).wait_recv()

    hops = ((1, 2), (1, 4))

    def state_copy(trip, side, k):
        hop = hops[trip][k]
        return pltpu.make_async_remote_copy(
            src_ref=snd.at[trip, side],
            dst_ref=got.at[trip, side, k],
            send_sem=st_send.at[trip, side, k],
            recv_sem=st_recv.at[trip, side, k],
            device_id={"ctx": me + hop if side == 0 else me - hop},
            device_id_type=MESH,
        )

    def sent(side):
        return nright if side == 0 else nleft

    def due(side):
        return nleft if side == 0 else nright

    def state_start(trip, side):
        for k, hop in enumerate(hops[trip]):

            @pl.when(hop <= sent(side))
            def _():
                state_copy(trip, side, k).start()

            @pl.when(hop > due(side))
            def _():
                got[trip, side, k] = jnp.zeros(got.shape[3:], BF16)

    def state_wait(trip, side):
        for k, hop in enumerate(hops[trip]):

            @pl.when(hop <= due(side))
            def _():
                state_copy(trip, side, k).wait_recv()

    def state_write(trip, side, totals, mults):
        pads = []
        for h in range(heads):
            snd[trip, side, h * width : (h + 1) * width, :] = totals[h].astype(BF16)
            high, low = split(jnp.broadcast_to(mults[h], (1, width)))
            pads.append((high.astype(F32), low.astype(F32)))
        rows16 = [pads[h][0] for h in range(heads)] + [pads[h][1] for h in range(heads)]
        rows16.append(jnp.zeros((16 - 2 * heads, width), F32))
        snd[trip, side, heads * width :, :] = jnp.concatenate(rows16, axis=0).astype(BF16)

    def state_read(trip, side, k, h):
        at = heads * width
        total = got[trip, side, k, h * width : (h + 1) * width, :].astype(F32)
        pads = got[trip, side, k, at : at + 16, :].astype(F32)
        return total, pads[h : h + 1] + pads[heads + h : heads + h + 1]

    for step in range(1, reach + 1):

        @pl.when(takes(step, nright, 1))
        def _():
            for which in range(2):
                kv_copy(which, step).start()

    for load in loads:
        load.wait()
    follows, precedes, head_terms, t_sub, t_lane = decay_terms(me, count, nblocks, doc, dec)

    for b in range(nblocks):
        for a in range(4):
            wide[a] = raw[a, b * rows : (b + 1) * rows, :].astype(F32)
        for h in range(heads):
            row, col, total = head_terms(b, h)
            picked = [wide[a, pl.ds(h, TILE, stride=heads), :] for a in range(4)]
            for a in range(4):
                parts[a, b, h] = picked[a].astype(BF16)
            key_high, key_low = split((picked[1] * jnp.exp(total - col)).T)
            value = picked[2].astype(BF16)
            states[0, b, h] = dot_nn(key_high, value) + dot_nn(key_low, value)
            query_high, query_low = split((picked[0] * jnp.exp(col)).T)
            dol = picked[3].astype(BF16)
            states[1, b, h] = dot_nn(query_high, dol) + dot_nn(query_low, dol)

    totals, mults = ([], []), ([], [])
    for h in range(heads):
        keep = [jnp.exp(head_terms(b, h)[2]) for b in range(nblocks)]
        total_l = states[0, 0, h]
        mult_l = keep[0] * follows[0]
        for b in range(1, nblocks):
            total_l = states[0, b, h] + keep[b] * follows[b] * total_l
            mult_l = mult_l * keep[b] * follows[b]
        total_r = states[1, nblocks - 1, h]
        mult_r = keep[nblocks - 1] * precedes[nblocks - 1]
        for b in reversed(range(nblocks - 1)):
            total_r = states[1, b, h] + keep[b] * precedes[b] * total_r
            mult_r = mult_r * keep[b] * precedes[b]
        for side, total, mult in ((0, total_l, mult_l), (1, total_r, mult_r)):
            totals[side].append(total)
            mults[side].append(mult)
            local[side, h] = total
    for side in range(2):
        state_write(0, side, totals[side], mults[side])

    state_start(0, 1)

    def state_join(side):
        state_wait(0, side)
        joined, spans = [], []
        for h in range(heads):
            one, mult_one = state_read(0, side, 0, h)
            two, mult_two = state_read(0, side, 1, h)
            joined.append(local[side, h] + mults[side][h] * (one + mult_one * two))
            spans.append(mults[side][h] * mult_one * mult_two)
        state_write(1, side, joined, spans)
        state_start(1, side)


    def within(b):
        for h in range(heads):
            row, col, total = head_terms(b, h)
            query, key, value, dol = (parts[a, b, h] for a in range(4))
            seen = t_sub <= t_lane
            weight = jnp.where(seen, jnp.exp(jnp.where(seen, row - col, 0.0)), 0.0)
            left = (dot_nt(value, dol) * weight).astype(BF16)
            right = (dot_nt(key, query) * weight).astype(BF16)
            grads[0, b, h] = dot_tn(left, key)
            grads[1, b, h] = dot_nn(left, query)
            grads[2, b, h] = dot_nn(right, dol)

    within(0)
    pass_on(1)
    for b in range(1, nblocks):
        within(b)
    def rows_of(j):
        return pl.ds(pl.multiple_of(j * TILE, TILE), TILE)

    sources = (dkey, dvalue)

    def grad_copy(which, step):
        return pltpu.make_async_remote_copy(
            src_ref=sources[which].at[rows_of((reach - step) * nblocks + 1 - core)],
            dst_ref=paired.at[which, step],
            send_sem=pg_send.at[which, step],
            recv_sem=pg_recv.at[which, step],
            device_id={"head": 1 - core},
            device_id_type=MESH,
        )

    def home_copy(step):
        return pltpu.make_async_remote_copy(
            src_ref=out.at[step - 1],
            dst_ref=inbox.at[step - 1],
            send_sem=home_send.at[step - 1],
            recv_sem=home_recv.at[step - 1],
            device_id={"ctx": me - step},
            device_id_type=MESH,
        )

    def mine(which, step):
        place = rows_of((reach - step) * nblocks + core)
        return sources[which][place, :] + paired[which, step]

    def send_home(step):
        for which in range(2):
            grad_copy(which, step).wait_recv()
        for which in range(2):
            out[step - 1, which] = mine(which, step).astype(BF16)
        home_copy(step).start()

    chunk = rows
    base = reach * nblocks
    offset = offset_of(limit, nblocks)
    near = jnp.minimum(nleft, jnp.where(in_first, reach, later_reach - 1))
    far = jnp.logical_and(jnp.logical_not(in_first), nleft == later_reach)
    far_tile = (reach - later_reach) * nblocks + 1
    queries = [q[b * chunk : (b + 1) * chunk, :] for b in range(nblocks)]
    douts = [dout[b * chunk : (b + 1) * chunk, :] for b in range(nblocks)]
    dkey[rows_of(base + 1), :] = jnp.zeros((TILE, width), F32)
    dvalue[rows_of(base + 1), :] = jnp.zeros((TILE, width), F32)

    def keys_at(j, n):
        return pl.ds(pl.multiple_of(j * TILE, TILE), n * TILE)

    def hidden(b, j):
        at = jnp.clip(me * nblocks - base + j, 0, count * nblocks - 1)
        return jnp.where(doc[at] == doc[me * nblocks + b], 0.0, -NEG).astype(F32)

    def folded(x, op):
        return op(x.reshape(TILE // 8, 8, chunk), axis=0)

    def causal():
        token = lax.broadcasted_iota(jnp.int32, (TILE, chunk), 1) // heads
        return lax.broadcasted_iota(jnp.int32, (TILE, chunk), 0) <= token

    def flip(step, tiles):
        first = (reach - step) * nblocks + tiles[0]
        low = tiles[0] * TILE
        block = kall[keys_at(first, len(tiles)), :].astype(F32).T.astype(BF16)
        flipped[step, :, low : low + len(tiles) * TILE] = block

    def weigh(b, step, tiles, carried, diag=False):
        top, amount, weighted = carried
        first = (reach - step) * nblocks + tiles[0]
        at = keys_at(first, len(tiles))
        s = dot_nt(kall[at, :], queries[b]) * factor
        g = dot_nt(vall[at, :], douts[b])
        parts_s = [s[k * TILE : (k + 1) * TILE] for k in range(len(tiles))]
        shades = [hidden(b, first + k) for k in range(len(tiles))]
        if diag:
            parts_s[-1] = jnp.where(causal(), parts_s[-1], NEG)
        peak = folded(parts_s[0], jnp.max) - shades[0]
        for k in range(1, len(tiles)):
            peak = jnp.maximum(peak, folded(parts_s[k], jnp.max) - shades[k])
        peak = jnp.maximum(top, jnp.max(peak, axis=0, keepdims=True))
        shrink = jnp.exp2(top - peak)
        amount = amount * shrink
        weighted = weighted * shrink
        for k in range(len(tiles)):
            p = jnp.exp2(parts_s[k] - (peak + shades[k]))
            gk = g[k * TILE : (k + 1) * TILE]
            scores[first + k - offset] = p
            probs_grad[first + k - offset] = gk
            amount += folded(p, jnp.sum)
            weighted += folded(p * gk, jnp.sum)
        peaks[b, step] = peak
        return peak, amount, weighted

    def ready(carried):
        top, amount, weighted = carried
        inverse = 1.0 / jnp.sum(amount, axis=0, keepdims=True)
        delta = jnp.sum(weighted, axis=0, keepdims=True) * inverse
        return top, inverse, delta

    def grade(b, step, tiles, stats, acc):
        top, inverse, delta = stats
        first = (reach - step) * nblocks + tiles[0]
        low = tiles[0] * TILE
        size = len(tiles) * TILE
        held = pl.ds(first - offset, len(tiles))
        p = scores[held].reshape(size, chunk) * (jnp.exp2(peaks[b, step] - top) * inverse)
        g = p * (probs_grad[held].reshape(size, chunk) - delta)
        p = p.astype(BF16)
        g = g.astype(BF16)
        at = keys_at(first, len(tiles))
        if b == 0:
            dvalue[at, :] = dot_nn(p, douts[b])
            dkey[at, :] = dot_nn(g, queries[b])
        else:
            dvalue[at, :] += dot_nn(p, douts[b])
            dkey[at, :] += dot_nn(g, queries[b])
        return acc + dot_nn(flipped[step, :, low : low + size], g)

    def finish(b, acc):
        att_dq[b * chunk : (b + 1) * chunk, :] = (acc.T * scale).astype(BF16)

    flip(0, (0, 1))
    row = jnp.zeros((8, chunk), F32)
    start = (jnp.full((1, chunk), NEG, F32), row, row)
    state_zero = weigh(0, 0, (0,), start, diag=True)
    for i, ref in enumerate(carry):
        ref[...] = state_zero[i]

    def first_pass(step, carried):
        pass_on(step + 1)
        pair_wait(step)
        flip(step, (0, 1))
        return weigh(0, step, (0, 1), carried)

    carried = lax.fori_loop(1, near + 1, first_pass, state_zero)
    for i, ref in enumerate(carry):
        ref[...] = carried[i]

    @pl.when(far)
    def _():
        @pl.when(core == 0)
        def _():
            pair_wait(later_reach)

        flip(later_reach, (1,))
        more = weigh(0, later_reach, (1,), tuple(ref[...] for ref in carry))
        for i, ref in enumerate(carry):
            ref[...] = more[i]

    state_join(1)
    state_start(0, 0)

    stats = ready(tuple(ref[...] for ref in carry))
    acc = grade(0, 0, (0,), stats, jnp.zeros((width, chunk), F32))
    carried = weigh(1, 0, (0, 1), start, diag=True)

    def both(step, packed):
        carried, acc = packed
        acc = grade(0, step, (0, 1), stats, acc)
        return weigh(1, step, (0, 1), carried), acc

    carried, acc = lax.fori_loop(1, near + 1, both, (carried, acc))
    dq_sum[...] = acc

    @pl.when(far)
    def _():
        dq_sum[...] = grade(0, later_reach, (1,), stats, dq_sum[...])

        @pl.when(core == 0)
        def _():
            for which in range(2):
                grad_copy(which, later_reach).start()

    finish(0, dq_sum[...])
    state_join(0)

    @pl.when(jnp.logical_and(far, core == 1))
    def _():
        send_home(later_reach)

    last_stats = ready(carried)

    def last_pass(i, acc):
        step = near - i
        acc = grade(1, step, (0, 1), last_stats, acc)
        for which in range(2):
            grad_copy(which, step).start()

        @pl.when(i > 0)
        def _():
            send_home(step + 1)

        return acc

    finish(1, lax.fori_loop(0, near + 1, last_pass, jnp.zeros((width, chunk), F32)))
    for side in range(2):
        state_wait(1, side)

    for h in range(heads):
        ends = []
        for side in range(2):
            close, mult = state_read(1, side, 0, h)
            state = close + mult * state_read(1, side, 1, h)[0]
            ends.append(state)
        keep = [jnp.exp(head_terms(b, h)[2]) for b in range(nblocks)]
        state = ends[0]
        into = []
        for b in range(nblocks):
            into.append(follows[b] * state)
            state = states[0, b, h] + keep[b] * into[b]
        state = ends[1]
        back = [None] * nblocks
        for b in reversed(range(nblocks)):
            back[b] = precedes[b] * state
            state = states[1, b, h] + keep[b] * back[b]
        for b in range(nblocks):
            row, col, total = head_terms(b, h)
            query, key, value, dol = (parts[a, b, h] for a in range(4))
            head_decay = jnp.exp(col)
            tail_decay = jnp.exp(total - col)
            into_high, into_low = split(into[b])
            back_high, back_low = split(back[b])
            at = pl.ds(b * rows + h, TILE, stride=heads)
            mixed[0, at, :] = grads[0, b, h] + head_decay * (
                dot_nt(dol, into_high) + dot_nt(dol, into_low)
            )
            mixed[1, at, :] = grads[1, b, h] + tail_decay * (
                dot_nt(value, back_high) + dot_nt(value, back_low)
            )
            mixed[2, at, :] = grads[2, b, h] + tail_decay * (
                dot_nn(key, back_high) + dot_nn(key, back_low)
            )
    lin_dq[...] = mixed[0].astype(BF16)
    lin_dk[...] = mixed[1].astype(BF16)
    lin_dv[...] = mixed[2].astype(BF16)

    for which in range(2):
        grad_copy(which, 0).wait_recv()
        paired[which, 0] = mine(which, 0)

    for step in range(1, reach + 1):

        @pl.when(takes(step, nright, 1))
        def _():
            home_copy(step).wait_recv()
            for which in range(2):
                paired[which, 0] += inbox[step - 1, which].astype(F32)

    att_dk[...] = (paired[0, 0] * scale).astype(BF16)
    att_dv[...] = paired[1, 0].astype(BF16)

    for which in range(2):
        grad_copy(which, 0).wait_send()
    for trip in range(2):
        for k, hop in enumerate(hops[trip]):
            for side, there in ((0, nright), (1, nleft)):

                @pl.when(hop <= there)
                def _():
                    state_copy(trip, side, k).wait_send()

    for step in range(1, reach + 1):

        @pl.when(takes(step, nright, 1))
        def _():
            for which in range(2):
                kv_copy(which, step).wait_send()

        @pl.when(takes(step, nleft, 1))
        def _():
            for which in range(2):
                pair_copy(which, step).wait_send()
            home_copy(step).wait_send()

        @pl.when(takes(step, nleft, 0))
        def _():
            for which in range(2):
                grad_copy(which, step).wait_send()


def slots_of(limit, nblocks):
    return max(MOST // nblocks - 1, limit // nblocks)


def offset_of(limit, nblocks):
    return max(0, slots_of(limit, nblocks) * nblocks + 1 - MOST)


def place_kernel(*refs):
    half = (len(refs) - 1) // 2
    sems = refs[-1]
    moves = [
        pltpu.make_async_copy(refs[i], refs[half + i], sems.at[i]) for i in range(half)
    ]
    for move in moves:
        move.start()
    for move in moves:
        move.wait()


def place(outs):
    return pl.pallas_call(
        place_kernel,
        out_shape=[SHAPE(x.shape, x.dtype) for x in outs],
        in_specs=[ANYWHERE] * len(outs),
        out_specs=[ANYWHERE] * len(outs),
        scratch_shapes=[DMA((len(outs),))],
        name="place",
    )(*outs)


def call_whole(count, limit, heads, nblocks, args):
    width = args[-1].shape[1]
    rows = nblocks * TILE * heads
    reach = slots_of(limit, nblocks)
    window = (reach + 1) * nblocks * TILE
    held = (reach + 1) * nblocks - offset_of(limit, nblocks)
    return pl.pallas_call(
        functools.partial(whole_kernel, count, limit, heads, nblocks),
        out_shape=[SHAPE((rows, width), BF16)] * 4 + [SHAPE((TILE, width), BF16)] * 2,
        in_specs=[IN_SMEM] + [ANYWHERE] * 9,
        out_specs=[IN_VMEM] * 6,
        scratch_shapes=[
            pltpu.VMEM((4, TILE * heads, width), F32),
            pltpu.VMEM((4, rows, width), BF16),
            pltpu.VMEM((heads, nblocks * TILE), F32),
            pltpu.VMEM((rows, width), BF16),
            pltpu.VMEM((rows, width), BF16),
            pltpu.VMEM((window, width), BF16),
            pltpu.VMEM((window, width), BF16),
            pltpu.VMEM((4, nblocks, heads, TILE, width), BF16),
            pltpu.VMEM((2, nblocks, heads, width, width), F32),
            pltpu.VMEM((2, heads, width, width), F32),
            pltpu.VMEM((3, nblocks, heads, TILE, width), F32),
            pltpu.VMEM((3, rows, width), F32),
            pltpu.VMEM((held, TILE, TILE * heads), F32),
            pltpu.VMEM((held, TILE, TILE * heads), F32),
            pltpu.VMEM((nblocks, reach + 1, 1, TILE * heads), F32),
            pltpu.VMEM((1, TILE * heads), F32),
            pltpu.VMEM((8, TILE * heads), F32),
            pltpu.VMEM((8, TILE * heads), F32),
            pltpu.VMEM((width, TILE * heads), F32),
            pltpu.VMEM((reach + 1, width, nblocks * TILE), BF16),
            pltpu.VMEM((window, width), F32),
            pltpu.VMEM((window, width), F32),
            pltpu.VMEM((2, 2, heads * width + 16, width), BF16),
            pltpu.VMEM((2, 2, 2, heads * width + 16, width), BF16),
            pltpu.VMEM((2, reach + 1, TILE, width), F32),
            pltpu.VMEM((reach, 2, TILE, width), BF16),
            pltpu.VMEM((reach, 2, TILE, width), BF16),
            DMA((9,)),
            DMA((2, reach)),
            DMA((2, reach)),
            DMA((2, reach)),
            DMA((2, reach)),
            DMA((2, 2, 2)),
            DMA((2, 2, 2)),
            DMA((2, reach + 1)),
            DMA((2, reach + 1)),
            DMA((reach,)),
            DMA((reach,)),
        ],
        compiler_params=pltpu.CompilerParams(
            collective_id=0 if limit == MOST else 1,
            has_side_effects=True,
            vmem_limit_bytes=VMEM_LIMIT,
        ),
        name="whole_%d" % limit,
    )(*args)


def shards(count, lin_q, lin_k, lin_v, lin_dout, lin_decay, att_q, att_k, att_v, att_dout, doc_block):
    length, heads, width = lin_q.shape
    nblocks = length // TILE
    assert nblocks == 2
    flat = lambda x: x.reshape(length * heads, width)
    args = (
        doc_block, flat(lin_q), flat(lin_k), flat(lin_v), flat(lin_dout), lin_decay,
        flat(att_q), flat(att_dout), att_k, att_v,
    )
    later = doc_block[MOST:]
    long = jnp.any(later[SHORT:] == later[:-SHORT])
    outs = lax.cond(
        long,
        lambda *a: call_whole(count, MOST, heads, nblocks, a),
        lambda *a: call_whole(count, SHORT, heads, nblocks, a),
        *args,
    )
    outs = place(outs)
    full = lambda x: x.reshape(length, heads, width)
    return (full(outs[0]), full(outs[1]), full(outs[2]), full(outs[3]), outs[4], outs[5])


def solution(mesh):
    return jax.shard_map(
        functools.partial(shards, mesh.shape["ctx"]),
        mesh=mesh,
        in_specs=(
            P("ctx", "head", None),
            P("ctx", "head", None),
            P("ctx", "head", None),
            P("ctx", "head", None),
            P("head", "ctx"),
            P("ctx", "head", None),
            P("ctx", None),
            P("ctx", None),
            P("ctx", "head", None),
            P(),
        ),
        out_specs=(
            P("ctx", "head", None),
            P("ctx", "head", None),
            P("ctx", "head", None),
            P("ctx", "head", None),
            P(("ctx", "head"), None),
            P(("ctx", "head"), None),
        ),
        check_vma=False,
    )
```

```python
import functools
import math

import jax
import jax.numpy as jnp
from jax import lax
from jax.experimental import pallas as pl
from jax.experimental.pallas import tpu as pltpu
from jax.sharding import PartitionSpec as P

TILE = 256
MOST = 12
SHORT = 8
NEG = -1e30
MESH = pl.DeviceIdType.MESH
F32 = jnp.float32
BF16 = jnp.bfloat16
SHAPE = jax.ShapeDtypeStruct
DMA = pltpu.SemaphoreType.DMA
IN_VMEM = pl.BlockSpec(memory_space=pltpu.VMEM)
IN_SMEM = pl.BlockSpec(memory_space=pltpu.SMEM)
ANYWHERE = pl.BlockSpec(memory_space=pl.ANY)
VMEM_LIMIT = 60 * 1024 * 1024


def dot_nn(a, b):
    return lax.dot_general(a, b, (((1,), (0,)), ((), ())), preferred_element_type=F32)


def dot_nt(a, b):
    return lax.dot_general(a, b, (((1,), (1,)), ((), ())), preferred_element_type=F32)


def dot_tn(a, b):
    return lax.dot_general(a, b, (((0,), (0,)), ((), ())), preferred_element_type=F32)


def split(x):
    high = x.astype(BF16)
    return high, (x - high.astype(F32)).astype(BF16)


def decay_terms(me, count, nblocks, doc, dec):
    t_sub = lax.broadcasted_iota(jnp.int32, (TILE, TILE), 0)
    t_lane = lax.broadcasted_iota(jnp.int32, (TILE, TILE), 1)
    upper = (t_sub <= t_lane).astype(F32)
    lower = (t_sub >= t_lane).astype(F32)

    def link(at_one, at_two):
        one = jnp.clip(at_one, 0, count * nblocks - 1)
        two = jnp.clip(at_two, 0, count * nblocks - 1)
        inside = jnp.logical_and(at_one >= 0, at_two < count * nblocks)
        same = jnp.logical_and(doc[one] == doc[two], inside)
        return jnp.where(same, 1.0, 0.0).astype(F32)

    follows = [link(me * nblocks + b - 1, me * nblocks + b) for b in range(nblocks)]
    precedes = [link(me * nblocks + b, me * nblocks + b + 1) for b in range(nblocks)]

    cum_row, cum_col = [], []
    for b in range(nblocks):
        piece = dec[:, b * TILE : (b + 1) * TILE]
        cum_row.append(
            lax.dot_general(
                piece, upper, (((1,), (0,)), ((), ())),
                preferred_element_type=F32, precision=lax.Precision.HIGHEST,
            )
        )
        cum_col.append(
            lax.dot_general(
                lower, piece, (((1,), (1,)), ((), ())),
                preferred_element_type=F32, precision=lax.Precision.HIGHEST,
            )
        )

    def head_terms(b, h):
        row = cum_row[b][h : h + 1, :]
        col = cum_col[b][:, h : h + 1]
        total = col[TILE - 1 : TILE, :]
        return row, col, total

    return follows, precedes, head_terms, t_sub, t_lane


def whole_kernel(
    count, limit, heads, nblocks,
    doc, lq, lk, lv, ld, dec_in, aq, ado, att_k, att_v,
    lin_dq, lin_dk, lin_dv, att_dq, att_dk, att_dv,
    wide, raw, dec, q, dout, kall, vall, parts, states, local, grads,
    scores, probs_grad, peaks, top_ref, amount_ref, weighted_ref, dq_sum, flipped, dkey, dvalue,
    snd, got, paired, out, inbox,
    raw_sem, kv_send, kv_recv, pair_send, pair_recv, st_send, st_recv,
    pg_send, pg_recv, home_send, home_recv,
):
    me = lax.axis_index("ctx")
    carry = (top_ref, amount_ref, weighted_ref)
    core = lax.axis_index("head")
    length = nblocks * TILE
    width = lq.shape[1]
    rows = TILE * heads
    first_devs = MOST // nblocks
    in_first = me < first_devs
    later_reach = limit // nblocks
    reach = slots_of(limit, nblocks)
    most = jnp.where(in_first, first_devs - 1, later_reach)
    nleft = jnp.minimum(jnp.where(in_first, me, me - first_devs), most)
    nright = jnp.minimum(jnp.where(in_first, first_devs - 1 - me, count - 1 - me), most)
    span = jnp.where(in_first, MOST, limit)

    def takes(step, there, who):
        if isinstance(step, int) and step != later_reach:
            return step <= there
        far = jnp.logical_and(step == later_reach, jnp.logical_not(in_first))
        return jnp.logical_and(step <= there, jnp.logical_or(jnp.logical_not(far), core == who))

    scale = width ** (-0.5)
    factor = scale * math.log2(math.e)

    loads = [
        pltpu.make_async_copy(ref, raw.at[a], raw_sem.at[a])
        for a, ref in enumerate((lq, lk, lv, ld))
    ]
    loads.append(pltpu.make_async_copy(dec_in, dec, raw_sem.at[4]))
    loads.append(pltpu.make_async_copy(aq, q, raw_sem.at[5]))
    loads.append(pltpu.make_async_copy(ado, dout, raw_sem.at[6]))
    own_rows = pl.ds(reach * length, length)
    loads.append(pltpu.make_async_copy(att_k, kall.at[own_rows], raw_sem.at[7]))
    loads.append(pltpu.make_async_copy(att_v, vall.at[own_rows], raw_sem.at[8]))
    for load in loads:
        load.start()

    barrier = pltpu.get_barrier_semaphore()
    pl.semaphore_signal(barrier, inc=1, device_id={"head": 1 - core}, device_id_type=MESH)
    for step in range(1, reach + 1):

        @pl.when(step <= nright)
        def _():
            pl.semaphore_signal(barrier, inc=1, device_id={"ctx": me + step}, device_id_type=MESH)

        @pl.when(step <= nleft)
        def _():
            pl.semaphore_signal(barrier, inc=1, device_id={"ctx": me - step}, device_id_type=MESH)

    pl.semaphore_wait(barrier, 1 + nleft + nright)

    pairs = ((att_k, kall), (att_v, vall))

    def half_of(step):
        start = pl.multiple_of(core * TILE, TILE)
        return start, pl.ds((reach - step) * length + start, TILE)

    def kv_copy(which, step):
        start, place = half_of(step)
        source, target = pairs[which]
        return pltpu.make_async_remote_copy(
            src_ref=source.at[pl.ds(start, TILE)],
            dst_ref=target.at[place],
            send_sem=kv_send.at[which, step - 1],
            recv_sem=kv_recv.at[which, step - 1],
            device_id={"ctx": me + step},
            device_id_type=MESH,
        )

    def pair_copy(which, step):
        target = pairs[which][1]
        place = half_of(step)[1]
        return pltpu.make_async_remote_copy(
            src_ref=target.at[place],
            dst_ref=target.at[place],
            send_sem=pair_send.at[which, step - 1],
            recv_sem=pair_recv.at[which, step - 1],
            device_id={"head": 1 - core},
            device_id_type=MESH,
        )

    def pass_on(step):
        @pl.when(takes(step, nleft, 1))
        def _():
            for which in range(2):
                kv_copy(which, step).wait_recv()
                pair_copy(which, step).start()

    def pair_wait(step):
        for which in range(2):
            pair_copy(which, step).wait_recv()

    hops = ((1, 2), (1, 4))

    def state_copy(trip, side, k):
        hop = hops[trip][k]
        return pltpu.make_async_remote_copy(
            src_ref=snd.at[trip, side],
            dst_ref=got.at[trip, side, k],
            send_sem=st_send.at[trip, side, k],
            recv_sem=st_recv.at[trip, side, k],
            device_id={"ctx": me + hop if side == 0 else me - hop},
            device_id_type=MESH,
        )

    def sent(side):
        return nright if side == 0 else nleft

    def due(side):
        return nleft if side == 0 else nright

    def state_start(trip, side):
        for k, hop in enumerate(hops[trip]):

            @pl.when(hop <= sent(side))
            def _():
                state_copy(trip, side, k).start()

            @pl.when(hop > due(side))
            def _():
                got[trip, side, k] = jnp.zeros(got.shape[3:], BF16)

    def state_wait(trip, side):
        for k, hop in enumerate(hops[trip]):

            @pl.when(hop <= due(side))
            def _():
                state_copy(trip, side, k).wait_recv()

    def state_write(trip, side, totals, mults):
        pads = []
        for h in range(heads):
            snd[trip, side, h * width : (h + 1) * width, :] = totals[h].astype(BF16)
            high, low = split(jnp.broadcast_to(mults[h], (1, width)))
            pads.append((high.astype(F32), low.astype(F32)))
        rows16 = [pads[h][0] for h in range(heads)] + [pads[h][1] for h in range(heads)]
        rows16.append(jnp.zeros((16 - 2 * heads, width), F32))
        snd[trip, side, heads * width :, :] = jnp.concatenate(rows16, axis=0).astype(BF16)

    def state_read(trip, side, k, h):
        at = heads * width
        total = got[trip, side, k, h * width : (h + 1) * width, :].astype(F32)
        pads = got[trip, side, k, at : at + 16, :].astype(F32)
        return total, pads[h : h + 1] + pads[heads + h : heads + h + 1]

    for step in range(1, reach + 1):

        @pl.when(takes(step, nright, 1))
        def _():
            for which in range(2):
                kv_copy(which, step).start()

    for load in loads:
        load.wait()
    follows, precedes, head_terms, t_sub, t_lane = decay_terms(me, count, nblocks, doc, dec)

    for b in range(nblocks):
        for a in range(4):
            wide[a] = raw[a, b * rows : (b + 1) * rows, :].astype(F32)
        for h in range(heads):
            row, col, total = head_terms(b, h)
            picked = [wide[a, pl.ds(h, TILE, stride=heads), :] for a in range(4)]
            for a in range(4):
                parts[a, b, h] = picked[a].astype(BF16)
            key_high, key_low = split((picked[1] * jnp.exp(total - col)).T)
            value = picked[2].astype(BF16)
            states[0, b, h] = dot_nn(key_high, value) + dot_nn(key_low, value)
            query_high, query_low = split((picked[0] * jnp.exp(col)).T)
            dol = picked[3].astype(BF16)
            states[1, b, h] = dot_nn(query_high, dol) + dot_nn(query_low, dol)

    totals, mults = ([], []), ([], [])
    for h in range(heads):
        keep = [jnp.exp(head_terms(b, h)[2]) for b in range(nblocks)]
        total_l = states[0, 0, h]
        mult_l = keep[0] * follows[0]
        for b in range(1, nblocks):
            total_l = states[0, b, h] + keep[b] * follows[b] * total_l
            mult_l = mult_l * keep[b] * follows[b]
        total_r = states[1, nblocks - 1, h]
        mult_r = keep[nblocks - 1] * precedes[nblocks - 1]
        for b in reversed(range(nblocks - 1)):
            total_r = states[1, b, h] + keep[b] * precedes[b] * total_r
            mult_r = mult_r * keep[b] * precedes[b]
        for side, total, mult in ((0, total_l, mult_l), (1, total_r, mult_r)):
            totals[side].append(total)
            mults[side].append(mult)
            local[side, h] = total
    for side in range(2):
        state_write(0, side, totals[side], mults[side])

    state_start(0, 1)

    @pl.when(jnp.logical_not(in_first))
    def _():
        state_start(0, 0)

    def state_join(side):
        state_wait(0, side)
        joined, spans = [], []
        for h in range(heads):
            one, mult_one = state_read(0, side, 0, h)
            two, mult_two = state_read(0, side, 1, h)
            joined.append(local[side, h] + mults[side][h] * (one + mult_one * two))
            spans.append(mults[side][h] * mult_one * mult_two)
        state_write(1, side, joined, spans)
        state_start(1, side)


    def within(b):
        for h in range(heads):
            row, col, total = head_terms(b, h)
            query, key, value, dol = (parts[a, b, h] for a in range(4))
            seen = t_sub <= t_lane
            weight = jnp.where(seen, jnp.exp(jnp.where(seen, row - col, 0.0)), 0.0)
            left = (dot_nt(value, dol) * weight).astype(BF16)
            right = (dot_nt(key, query) * weight).astype(BF16)
            grads[0, b, h] = dot_tn(left, key)
            grads[1, b, h] = dot_nn(left, query)
            grads[2, b, h] = dot_nn(right, dol)

    within(0)
    pass_on(1)
    for b in range(1, nblocks):
        within(b)
    def rows_of(j):
        return pl.ds(pl.multiple_of(j * TILE, TILE), TILE)

    sources = (dkey, dvalue)

    def grad_copy(which, step):
        return pltpu.make_async_remote_copy(
            src_ref=sources[which].at[rows_of((reach - step) * nblocks + 1 - core)],
            dst_ref=paired.at[which, step],
            send_sem=pg_send.at[which, step],
            recv_sem=pg_recv.at[which, step],
            device_id={"head": 1 - core},
            device_id_type=MESH,
        )

    def home_copy(step):
        return pltpu.make_async_remote_copy(
            src_ref=out.at[step - 1],
            dst_ref=inbox.at[step - 1],
            send_sem=home_send.at[step - 1],
            recv_sem=home_recv.at[step - 1],
            device_id={"ctx": me - step},
            device_id_type=MESH,
        )

    def mine(which, step):
        place = rows_of((reach - step) * nblocks + core)
        return sources[which][place, :] + paired[which, step]

    def send_home(step):
        for which in range(2):
            grad_copy(which, step).wait_recv()
        for which in range(2):
            out[step - 1, which] = mine(which, step).astype(BF16)
        home_copy(step).start()

    chunk = rows
    base = reach * nblocks
    offset = offset_of(limit, nblocks)
    near = jnp.minimum(nleft, jnp.where(in_first, reach, later_reach - 1))
    far = jnp.logical_and(jnp.logical_not(in_first), nleft == later_reach)
    far_tile = (reach - later_reach) * nblocks + 1
    queries = [q[b * chunk : (b + 1) * chunk, :] for b in range(nblocks)]
    douts = [dout[b * chunk : (b + 1) * chunk, :] for b in range(nblocks)]
    dkey[rows_of(base + 1), :] = jnp.zeros((TILE, width), F32)
    dvalue[rows_of(base + 1), :] = jnp.zeros((TILE, width), F32)

    def keys_at(j, n):
        return pl.ds(pl.multiple_of(j * TILE, TILE), n * TILE)

    def hidden(b, j):
        at = jnp.clip(me * nblocks - base + j, 0, count * nblocks - 1)
        return jnp.where(doc[at] == doc[me * nblocks + b], 0.0, -NEG).astype(F32)

    def folded(x, op):
        return op(x.reshape(TILE // 8, 8, chunk), axis=0)

    def causal():
        token = lax.broadcasted_iota(jnp.int32, (TILE, chunk), 1) // heads
        return lax.broadcasted_iota(jnp.int32, (TILE, chunk), 0) <= token

    def flip(step, tiles):
        first = (reach - step) * nblocks + tiles[0]
        low = tiles[0] * TILE
        block = kall[keys_at(first, len(tiles)), :].astype(F32).T.astype(BF16)
        flipped[step, :, low : low + len(tiles) * TILE] = block

    def weigh(b, step, tiles, carried, diag=False):
        top, amount, weighted = carried
        first = (reach - step) * nblocks + tiles[0]
        at = keys_at(first, len(tiles))
        s = dot_nt(kall[at, :], queries[b]) * factor
        g = dot_nt(vall[at, :], douts[b])
        parts_s = [s[k * TILE : (k + 1) * TILE] for k in range(len(tiles))]
        shades = [hidden(b, first + k) for k in range(len(tiles))]
        if diag:
            parts_s[-1] = jnp.where(causal(), parts_s[-1], NEG)
        peak = folded(parts_s[0], jnp.max) - shades[0]
        for k in range(1, len(tiles)):
            peak = jnp.maximum(peak, folded(parts_s[k], jnp.max) - shades[k])
        peak = jnp.maximum(top, jnp.max(peak, axis=0, keepdims=True))
        shrink = jnp.exp2(top - peak)
        amount = amount * shrink
        weighted = weighted * shrink
        for k in range(len(tiles)):
            p = jnp.exp2(parts_s[k] - (peak + shades[k]))
            gk = g[k * TILE : (k + 1) * TILE]
            scores[first + k - offset] = p
            probs_grad[first + k - offset] = gk
            amount += folded(p, jnp.sum)
            weighted += folded(p * gk, jnp.sum)
        peaks[b, step] = peak
        return peak, amount, weighted

    def ready(carried):
        top, amount, weighted = carried
        inverse = 1.0 / jnp.sum(amount, axis=0, keepdims=True)
        delta = jnp.sum(weighted, axis=0, keepdims=True) * inverse
        return top, inverse, delta

    def grade(b, step, tiles, stats, acc):
        top, inverse, delta = stats
        first = (reach - step) * nblocks + tiles[0]
        low = tiles[0] * TILE
        size = len(tiles) * TILE
        held = pl.ds(first - offset, len(tiles))
        p = scores[held].reshape(size, chunk) * (jnp.exp2(peaks[b, step] - top) * inverse)
        g = p * (probs_grad[held].reshape(size, chunk) - delta)
        p = p.astype(BF16)
        g = g.astype(BF16)
        at = keys_at(first, len(tiles))
        if b == 0:
            dvalue[at, :] = dot_nn(p, douts[b])
            dkey[at, :] = dot_nn(g, queries[b])
        else:
            dvalue[at, :] += dot_nn(p, douts[b])
            dkey[at, :] += dot_nn(g, queries[b])
        return acc + dot_nn(flipped[step, :, low : low + size], g)

    def finish(b, acc):
        att_dq[b * chunk : (b + 1) * chunk, :] = (acc.T * scale).astype(BF16)

    flip(0, (0, 1))
    row = jnp.zeros((8, chunk), F32)
    start = (jnp.full((1, chunk), NEG, F32), row, row)
    state_zero = weigh(0, 0, (0,), start, diag=True)
    for i, ref in enumerate(carry):
        ref[...] = state_zero[i]

    def first_pass(step, carried):
        pass_on(step + 1)
        pair_wait(step)
        flip(step, (0, 1))
        return weigh(0, step, (0, 1), carried)

    carried = lax.fori_loop(1, near + 1, first_pass, state_zero)
    for i, ref in enumerate(carry):
        ref[...] = carried[i]

    @pl.when(far)
    def _():
        @pl.when(core == 0)
        def _():
            pair_wait(later_reach)

        flip(later_reach, (1,))
        more = weigh(0, later_reach, (1,), tuple(ref[...] for ref in carry))
        for i, ref in enumerate(carry):
            ref[...] = more[i]

    state_join(1)

    @pl.when(in_first)
    def _():
        state_start(0, 0)


    stats = ready(tuple(ref[...] for ref in carry))
    acc = grade(0, 0, (0,), stats, jnp.zeros((width, chunk), F32))
    carried = weigh(1, 0, (0, 1), start, diag=True)

    def both(step, packed):
        carried, acc = packed
        acc = grade(0, step, (0, 1), stats, acc)
        return weigh(1, step, (0, 1), carried), acc

    carried, acc = lax.fori_loop(1, near + 1, both, (carried, acc))
    dq_sum[...] = acc

    @pl.when(far)
    def _():
        dq_sum[...] = grade(0, later_reach, (1,), stats, dq_sum[...])

        @pl.when(core == 0)
        def _():
            for which in range(2):
                grad_copy(which, later_reach).start()

    finish(0, dq_sum[...])
    state_join(0)

    @pl.when(jnp.logical_and(far, core == 1))
    def _():
        send_home(later_reach)

    last_stats = ready(carried)

    def last_pass(i, acc):
        step = near - i
        acc = grade(1, step, (0, 1), last_stats, acc)
        for which in range(2):
            grad_copy(which, step).start()

        @pl.when(i > 0)
        def _():
            send_home(step + 1)

        return acc

    finish(1, lax.fori_loop(0, near + 1, last_pass, jnp.zeros((width, chunk), F32)))
    for side in range(2):
        state_wait(1, side)

    intos, backs = [], []
    for h in range(heads):
        ends = []
        for side in range(2):
            close, mult = state_read(1, side, 0, h)
            ends.append(close + mult * state_read(1, side, 1, h)[0])
        keep = [jnp.exp(head_terms(b, h)[2]) for b in range(nblocks)]
        state = ends[0]
        into = []
        for b in range(nblocks):
            into.append(follows[b] * state)
            state = states[0, b, h] + keep[b] * into[b]
        state = ends[1]
        back = [None] * nblocks
        for b in reversed(range(nblocks)):
            back[b] = precedes[b] * state
            state = states[1, b, h] + keep[b] * back[b]
        intos.append([x.astype(BF16) for x in into])
        backs.append([x.astype(BF16) for x in back])
    for b in range(nblocks):
        for h in range(heads):
            row, col, total = head_terms(b, h)
            query, key, value, dol = (parts[a, b, h] for a in range(4))
            head_decay = jnp.exp(col)
            tail_decay = jnp.exp(total - col)
            at = pl.ds(h, TILE, stride=heads)
            wide[0, at, :] = grads[0, b, h] + head_decay * dot_nt(dol, intos[h][b])
            wide[1, at, :] = grads[1, b, h] + tail_decay * dot_nt(value, backs[h][b])
            wide[2, at, :] = grads[2, b, h] + tail_decay * dot_nn(key, backs[h][b])
        for a, ref in enumerate((lin_dq, lin_dk, lin_dv)):
            ref[b * rows : (b + 1) * rows, :] = wide[a].astype(BF16)

    for which in range(2):
        grad_copy(which, 0).wait_recv()
        paired[which, 0] = mine(which, 0)

    for step in range(1, reach + 1):

        @pl.when(takes(step, nright, 1))
        def _():
            home_copy(step).wait_recv()
            for which in range(2):
                paired[which, 0] += inbox[step - 1, which].astype(F32)

    att_dk[...] = (paired[0, 0] * scale).astype(BF16)
    att_dv[...] = paired[1, 0].astype(BF16)

    for which in range(2):
        grad_copy(which, 0).wait_send()
    for trip in range(2):
        for k, hop in enumerate(hops[trip]):
            for side, there in ((0, nright), (1, nleft)):

                @pl.when(hop <= there)
                def _():
                    state_copy(trip, side, k).wait_send()

    for step in range(1, reach + 1):

        @pl.when(takes(step, nright, 1))
        def _():
            for which in range(2):
                kv_copy(which, step).wait_send()

        @pl.when(takes(step, nleft, 1))
        def _():
            for which in range(2):
                pair_copy(which, step).wait_send()
            home_copy(step).wait_send()

        @pl.when(takes(step, nleft, 0))
        def _():
            for which in range(2):
                grad_copy(which, step).wait_send()


def slots_of(limit, nblocks):
    return max(MOST // nblocks - 1, limit // nblocks)


def offset_of(limit, nblocks):
    return max(0, slots_of(limit, nblocks) * nblocks + 1 - MOST)


def place_kernel(*refs):
    half = (len(refs) - 1) // 2
    sems = refs[-1]
    moves = [
        pltpu.make_async_copy(refs[i], refs[half + i], sems.at[i]) for i in range(half)
    ]
    for move in moves:
        move.start()
    for move in moves:
        move.wait()


def place(outs):
    return pl.pallas_call(
        place_kernel,
        out_shape=[SHAPE(x.shape, x.dtype) for x in outs],
        in_specs=[ANYWHERE] * len(outs),
        out_specs=[ANYWHERE] * len(outs),
        scratch_shapes=[DMA((len(outs),))],
        name="place",
    )(*outs)


def call_whole(count, limit, heads, nblocks, args):
    width = args[-1].shape[1]
    rows = nblocks * TILE * heads
    reach = slots_of(limit, nblocks)
    window = (reach + 1) * nblocks * TILE
    held = (reach + 1) * nblocks - offset_of(limit, nblocks)
    return pl.pallas_call(
        functools.partial(whole_kernel, count, limit, heads, nblocks),
        out_shape=[SHAPE((rows, width), BF16)] * 4 + [SHAPE((TILE, width), BF16)] * 2,
        in_specs=[IN_SMEM] + [ANYWHERE] * 9,
        out_specs=[IN_VMEM] * 6,
        scratch_shapes=[
            pltpu.VMEM((4, TILE * heads, width), F32),
            pltpu.VMEM((4, rows, width), BF16),
            pltpu.VMEM((heads, nblocks * TILE), F32),
            pltpu.VMEM((rows, width), BF16),
            pltpu.VMEM((rows, width), BF16),
            pltpu.VMEM((window, width), BF16),
            pltpu.VMEM((window, width), BF16),
            pltpu.VMEM((4, nblocks, heads, TILE, width), BF16),
            pltpu.VMEM((2, nblocks, heads, width, width), F32),
            pltpu.VMEM((2, heads, width, width), F32),
            pltpu.VMEM((3, nblocks, heads, TILE, width), F32),
            pltpu.VMEM((held, TILE, TILE * heads), F32),
            pltpu.VMEM((held, TILE, TILE * heads), F32),
            pltpu.VMEM((nblocks, reach + 1, 1, TILE * heads), F32),
            pltpu.VMEM((1, TILE * heads), F32),
            pltpu.VMEM((8, TILE * heads), F32),
            pltpu.VMEM((8, TILE * heads), F32),
            pltpu.VMEM((width, TILE * heads), F32),
            pltpu.VMEM((reach + 1, width, nblocks * TILE), BF16),
            pltpu.VMEM((window, width), F32),
            pltpu.VMEM((window, width), F32),
            pltpu.VMEM((2, 2, heads * width + 16, width), BF16),
            pltpu.VMEM((2, 2, 2, heads * width + 16, width), BF16),
            pltpu.VMEM((2, reach + 1, TILE, width), F32),
            pltpu.VMEM((reach, 2, TILE, width), BF16),
            pltpu.VMEM((reach, 2, TILE, width), BF16),
            DMA((9,)),
            DMA((2, reach)),
            DMA((2, reach)),
            DMA((2, reach)),
            DMA((2, reach)),
            DMA((2, 2, 2)),
            DMA((2, 2, 2)),
            DMA((2, reach + 1)),
            DMA((2, reach + 1)),
            DMA((reach,)),
            DMA((reach,)),
        ],
        compiler_params=pltpu.CompilerParams(
            collective_id=0 if limit == MOST else 1,
            has_side_effects=True,
            vmem_limit_bytes=VMEM_LIMIT,
        ),
        name="whole_%d" % limit,
    )(*args)


def shards(count, lin_q, lin_k, lin_v, lin_dout, lin_decay, att_q, att_k, att_v, att_dout, doc_block):
    length, heads, width = lin_q.shape
    nblocks = length // TILE
    assert nblocks == 2
    flat = lambda x: x.reshape(length * heads, width)
    args = (
        doc_block, flat(lin_q), flat(lin_k), flat(lin_v), flat(lin_dout), lin_decay,
        flat(att_q), flat(att_dout), att_k, att_v,
    )
    later = doc_block[MOST:]
    long = jnp.any(later[SHORT:] == later[:-SHORT])
    outs = lax.cond(
        long,
        lambda *a: call_whole(count, MOST, heads, nblocks, a),
        lambda *a: call_whole(count, SHORT, heads, nblocks, a),
        *args,
    )
    outs = place(outs)
    full = lambda x: x.reshape(length, heads, width)
    return (full(outs[0]), full(outs[1]), full(outs[2]), full(outs[3]), outs[4], outs[5])


def solution(mesh):
    return jax.shard_map(
        functools.partial(shards, mesh.shape["ctx"]),
        mesh=mesh,
        in_specs=(
            P("ctx", "head", None),
            P("ctx", "head", None),
            P("ctx", "head", None),
            P("ctx", "head", None),
            P("head", "ctx"),
            P("ctx", "head", None),
            P("ctx", None),
            P("ctx", None),
            P("ctx", "head", None),
            P(),
        ),
        out_specs=(
            P("ctx", "head", None),
            P("ctx", "head", None),
            P("ctx", "head", None),
            P("ctx", "head", None),
            P(("ctx", "head"), None),
            P(("ctx", "head"), None),
        ),
        check_vma=False,
    )
```

```python
import functools
import math

import jax
import jax.numpy as jnp
from jax import lax
from jax.experimental import pallas as pl
from jax.experimental.pallas import tpu as pltpu
from jax.sharding import PartitionSpec as P

TILE = 256
MOST = 12
SHORT = 8
NEG = -1e30
MESH = pl.DeviceIdType.MESH
F32 = jnp.float32
BF16 = jnp.bfloat16
SHAPE = jax.ShapeDtypeStruct
DMA = pltpu.SemaphoreType.DMA
IN_VMEM = pl.BlockSpec(memory_space=pltpu.VMEM)
IN_SMEM = pl.BlockSpec(memory_space=pltpu.SMEM)
ANYWHERE = pl.BlockSpec(memory_space=pl.ANY)
VMEM_LIMIT = 60 * 1024 * 1024


def dot_nn(a, b):
    return lax.dot_general(a, b, (((1,), (0,)), ((), ())), preferred_element_type=F32)


def dot_nt(a, b):
    return lax.dot_general(a, b, (((1,), (1,)), ((), ())), preferred_element_type=F32)


def dot_tn(a, b):
    return lax.dot_general(a, b, (((0,), (0,)), ((), ())), preferred_element_type=F32)


def split(x):
    high = x.astype(BF16)
    return high, (x - high.astype(F32)).astype(BF16)


def decay_terms(me, count, nblocks, doc, dec):
    t_sub = lax.broadcasted_iota(jnp.int32, (TILE, TILE), 0)
    t_lane = lax.broadcasted_iota(jnp.int32, (TILE, TILE), 1)
    upper = (t_sub <= t_lane).astype(F32)
    lower = (t_sub >= t_lane).astype(F32)

    def link(at_one, at_two):
        one = jnp.clip(at_one, 0, count * nblocks - 1)
        two = jnp.clip(at_two, 0, count * nblocks - 1)
        inside = jnp.logical_and(at_one >= 0, at_two < count * nblocks)
        same = jnp.logical_and(doc[one] == doc[two], inside)
        return jnp.where(same, 1.0, 0.0).astype(F32)

    follows = [link(me * nblocks + b - 1, me * nblocks + b) for b in range(nblocks)]
    precedes = [link(me * nblocks + b, me * nblocks + b + 1) for b in range(nblocks)]

    cum_row, cum_col = [], []
    for b in range(nblocks):
        piece = dec[:, b * TILE : (b + 1) * TILE]
        cum_row.append(
            lax.dot_general(
                piece, upper, (((1,), (0,)), ((), ())),
                preferred_element_type=F32, precision=lax.Precision.HIGHEST,
            )
        )
        cum_col.append(
            lax.dot_general(
                lower, piece, (((1,), (1,)), ((), ())),
                preferred_element_type=F32, precision=lax.Precision.HIGHEST,
            )
        )

    def head_terms(b, h):
        row = cum_row[b][h : h + 1, :]
        col = cum_col[b][:, h : h + 1]
        total = col[TILE - 1 : TILE, :]
        return row, col, total

    return follows, precedes, head_terms, t_sub, t_lane


def whole_kernel(
    count, limit, heads, nblocks,
    doc, lq, lk, lv, ld, dec_in, aq, ado, att_k, att_v,
    lin_dq, lin_dk, lin_dv, att_dq, att_dk, att_dv,
    wide, raw, dec, q, dout, kall, vall, parts, states, local, grads,
    scores, probs_grad, peaks, top_ref, amount_ref, weighted_ref, middle, dq_sum, flipped, dkey, dvalue,
    snd, got, paired, out, inbox,
    raw_sem, kv_send, kv_recv, pair_send, pair_recv, st_send, st_recv,
    pg_send, pg_recv, home_send, home_recv,
):
    me = lax.axis_index("ctx")
    carry = (top_ref, amount_ref, weighted_ref)
    core = lax.axis_index("head")
    length = nblocks * TILE
    width = lq.shape[1]
    rows = TILE * heads
    first_devs = MOST // nblocks
    in_first = me < first_devs
    later_reach = limit // nblocks
    reach = slots_of(limit, nblocks)
    most = jnp.where(in_first, first_devs - 1, later_reach)
    nleft = jnp.minimum(jnp.where(in_first, me, me - first_devs), most)
    nright = jnp.minimum(jnp.where(in_first, first_devs - 1 - me, count - 1 - me), most)
    span = jnp.where(in_first, MOST, limit)

    def takes(step, there, who):
        if isinstance(step, int) and step != later_reach:
            return step <= there
        far = jnp.logical_and(step == later_reach, jnp.logical_not(in_first))
        return jnp.logical_and(step <= there, jnp.logical_or(jnp.logical_not(far), core == who))

    scale = width ** (-0.5)
    factor = scale * math.log2(math.e)

    loads = [
        pltpu.make_async_copy(ref, raw.at[a], raw_sem.at[a])
        for a, ref in enumerate((lq, lk, lv, ld))
    ]
    loads.append(pltpu.make_async_copy(dec_in, dec, raw_sem.at[4]))
    loads.append(pltpu.make_async_copy(aq, q, raw_sem.at[5]))
    loads.append(pltpu.make_async_copy(ado, dout, raw_sem.at[6]))
    own_rows = pl.ds(reach * length, length)
    loads.append(pltpu.make_async_copy(att_k, kall.at[own_rows], raw_sem.at[7]))
    loads.append(pltpu.make_async_copy(att_v, vall.at[own_rows], raw_sem.at[8]))
    for load in loads:
        load.start()

    barrier = pltpu.get_barrier_semaphore()
    pl.semaphore_signal(barrier, inc=1, device_id={"head": 1 - core}, device_id_type=MESH)
    for step in range(1, reach + 1):

        @pl.when(step <= nright)
        def _():
            pl.semaphore_signal(barrier, inc=1, device_id={"ctx": me + step}, device_id_type=MESH)

        @pl.when(step <= nleft)
        def _():
            pl.semaphore_signal(barrier, inc=1, device_id={"ctx": me - step}, device_id_type=MESH)

    pl.semaphore_wait(barrier, 1 + nleft + nright)

    pairs = ((att_k, kall), (att_v, vall))

    def half_of(step):
        start = pl.multiple_of(core * TILE, TILE)
        return start, pl.ds((reach - step) * length + start, TILE)

    def kv_copy(which, step):
        start, place = half_of(step)
        source, target = pairs[which]
        return pltpu.make_async_remote_copy(
            src_ref=source.at[pl.ds(start, TILE)],
            dst_ref=target.at[place],
            send_sem=kv_send.at[which, step - 1],
            recv_sem=kv_recv.at[which, step - 1],
            device_id={"ctx": me + step},
            device_id_type=MESH,
        )

    def pair_copy(which, step):
        target = pairs[which][1]
        place = half_of(step)[1]
        return pltpu.make_async_remote_copy(
            src_ref=target.at[place],
            dst_ref=target.at[place],
            send_sem=pair_send.at[which, step - 1],
            recv_sem=pair_recv.at[which, step - 1],
            device_id={"head": 1 - core},
            device_id_type=MESH,
        )

    def pass_on(step):
        @pl.when(takes(step, nleft, 1))
        def _():
            for which in range(2):
                kv_copy(which, step).wait_recv()
                pair_copy(which, step).start()

    def pair_wait(step):
        for which in range(2):
            pair_copy(which, step).wait_recv()

    hops = ((1, 2), (1, 4))

    def state_copy(trip, side, k):
        hop = hops[trip][k]
        return pltpu.make_async_remote_copy(
            src_ref=snd.at[trip, side],
            dst_ref=got.at[trip, side, k],
            send_sem=st_send.at[trip, side, k],
            recv_sem=st_recv.at[trip, side, k],
            device_id={"ctx": me + hop if side == 0 else me - hop},
            device_id_type=MESH,
        )

    def sent(side):
        return nright if side == 0 else nleft

    def due(side):
        return nleft if side == 0 else nright

    def state_start(trip, side):
        for k, hop in enumerate(hops[trip]):

            @pl.when(hop <= sent(side))
            def _():
                state_copy(trip, side, k).start()

            @pl.when(hop > due(side))
            def _():
                got[trip, side, k] = jnp.zeros(got.shape[3:], BF16)

    def state_wait(trip, side):
        for k, hop in enumerate(hops[trip]):

            @pl.when(hop <= due(side))
            def _():
                state_copy(trip, side, k).wait_recv()

    def state_write(trip, side, totals, mults):
        pads = []
        for h in range(heads):
            snd[trip, side, h * width : (h + 1) * width, :] = totals[h].astype(BF16)
            high, low = split(jnp.broadcast_to(mults[h], (1, width)))
            pads.append((high.astype(F32), low.astype(F32)))
        rows16 = [pads[h][0] for h in range(heads)] + [pads[h][1] for h in range(heads)]
        rows16.append(jnp.zeros((16 - 2 * heads, width), F32))
        snd[trip, side, heads * width :, :] = jnp.concatenate(rows16, axis=0).astype(BF16)

    def state_read(trip, side, k, h):
        at = heads * width
        total = got[trip, side, k, h * width : (h + 1) * width, :].astype(F32)
        pads = got[trip, side, k, at : at + 16, :].astype(F32)
        return total, pads[h : h + 1] + pads[heads + h : heads + h + 1]

    for step in range(1, reach + 1):

        @pl.when(takes(step, nright, 1))
        def _():
            for which in range(2):
                kv_copy(which, step).start()

    for load in loads:
        load.wait()
    follows, precedes, head_terms, t_sub, t_lane = decay_terms(me, count, nblocks, doc, dec)

    for b in range(nblocks):
        for a in range(4):
            wide[a % 3] = raw[a, b * rows : (b + 1) * rows, :].astype(F32)
            for h in range(heads):
                parts[a, b, h] = wide[a % 3, pl.ds(h, TILE, stride=heads), :].astype(BF16)
        for h in range(heads):
            row, col, total = head_terms(b, h)
            picked = [parts[a, b, h].astype(F32) for a in range(4)]
            key_high, key_low = split((picked[1] * jnp.exp(total - col)).T)
            value = picked[2].astype(BF16)
            states[0, b, h] = dot_nn(key_high, value) + dot_nn(key_low, value)
            query_high, query_low = split((picked[0] * jnp.exp(col)).T)
            dol = picked[3].astype(BF16)
            states[1, b, h] = dot_nn(query_high, dol) + dot_nn(query_low, dol)

    totals, mults = ([], []), ([], [])
    for h in range(heads):
        keep = [jnp.exp(head_terms(b, h)[2]) for b in range(nblocks)]
        total_l = states[0, 0, h]
        mult_l = keep[0] * follows[0]
        for b in range(1, nblocks):
            total_l = states[0, b, h] + keep[b] * follows[b] * total_l
            mult_l = mult_l * keep[b] * follows[b]
        total_r = states[1, nblocks - 1, h]
        mult_r = keep[nblocks - 1] * precedes[nblocks - 1]
        for b in reversed(range(nblocks - 1)):
            total_r = states[1, b, h] + keep[b] * precedes[b] * total_r
            mult_r = mult_r * keep[b] * precedes[b]
        for side, total, mult in ((0, total_l, mult_l), (1, total_r, mult_r)):
            totals[side].append(total)
            mults[side].append(mult)
            local[side, h] = total
    for side in range(2):
        state_write(0, side, totals[side], mults[side])

    state_start(0, 1)

    @pl.when(jnp.logical_not(in_first))
    def _():
        state_start(0, 0)

    def state_join(side):
        state_wait(0, side)
        joined, spans = [], []
        for h in range(heads):
            one, mult_one = state_read(0, side, 0, h)
            two, mult_two = state_read(0, side, 1, h)
            joined.append(local[side, h] + mults[side][h] * (one + mult_one * two))
            spans.append(mults[side][h] * mult_one * mult_two)
        state_write(1, side, joined, spans)
        state_start(1, side)


    def within(b):
        for h in range(heads):
            row, col, total = head_terms(b, h)
            query, key, value, dol = (parts[a, b, h] for a in range(4))
            seen = t_sub <= t_lane
            weight = jnp.where(seen, jnp.exp(jnp.where(seen, row - col, 0.0)), 0.0)
            left = (dot_nt(value, dol) * weight).astype(BF16)
            right = (dot_nt(key, query) * weight).astype(BF16)
            grads[0, b, h] = dot_tn(left, key)
            grads[1, b, h] = dot_nn(left, query)
            grads[2, b, h] = dot_nn(right, dol)

    within(0)
    pass_on(1)
    for b in range(1, nblocks):
        within(b)
    def rows_of(j):
        return pl.ds(pl.multiple_of(j * TILE, TILE), TILE)

    sources = (dkey, dvalue)

    def grad_copy(which, step):
        return pltpu.make_async_remote_copy(
            src_ref=sources[which].at[rows_of((reach - step) * nblocks + 1 - core)],
            dst_ref=paired.at[which, step],
            send_sem=pg_send.at[which, step],
            recv_sem=pg_recv.at[which, step],
            device_id={"head": 1 - core},
            device_id_type=MESH,
        )

    def home_copy(step):
        return pltpu.make_async_remote_copy(
            src_ref=out.at[step - 1],
            dst_ref=inbox.at[step - 1],
            send_sem=home_send.at[step - 1],
            recv_sem=home_recv.at[step - 1],
            device_id={"ctx": me - step},
            device_id_type=MESH,
        )

    def mine(which, step):
        place = rows_of((reach - step) * nblocks + core)
        return sources[which][place, :] + paired[which, step]

    def send_home(step):
        for which in range(2):
            grad_copy(which, step).wait_recv()
        for which in range(2):
            out[step - 1, which] = mine(which, step).astype(BF16)
        home_copy(step).start()

    chunk = rows
    base = reach * nblocks
    offset = offset_of(limit, nblocks)
    near = jnp.minimum(nleft, jnp.where(in_first, reach, later_reach - 1))
    far = jnp.logical_and(jnp.logical_not(in_first), nleft == later_reach)
    far_tile = (reach - later_reach) * nblocks + 1
    queries = [q[b * chunk : (b + 1) * chunk, :] for b in range(nblocks)]
    douts = [dout[b * chunk : (b + 1) * chunk, :] for b in range(nblocks)]
    scores[0, base + 1 - offset] = jnp.zeros((TILE, chunk), BF16)
    probs_grad[0, base + 1 - offset] = jnp.zeros((TILE, chunk), BF16)

    def keys_at(j, n):
        return pl.ds(pl.multiple_of(j * TILE, TILE), n * TILE)

    def hidden(b, j):
        at = jnp.clip(me * nblocks - base + j, 0, count * nblocks - 1)
        return jnp.where(doc[at] == doc[me * nblocks + b], 0.0, -NEG).astype(F32)

    def folded(x, op):
        return op(x.reshape(TILE // 8, 8, chunk), axis=0)

    def causal():
        token = lax.broadcasted_iota(jnp.int32, (TILE, chunk), 1) // heads
        return lax.broadcasted_iota(jnp.int32, (TILE, chunk), 0) <= token

    def flip(step, tiles):
        first = (reach - step) * nblocks + tiles[0]
        low = tiles[0] * TILE
        block = kall[keys_at(first, len(tiles)), :].astype(F32).T.astype(BF16)
        flipped[step, :, low : low + len(tiles) * TILE] = block

    def weigh(b, step, tiles, carried, diag=False):
        top, amount, weighted = carried
        first = (reach - step) * nblocks + tiles[0]
        at = keys_at(first, len(tiles))
        s = dot_nt(kall[at, :], queries[b]) * factor
        g = dot_nt(vall[at, :], douts[b])
        parts_s = [s[k * TILE : (k + 1) * TILE] for k in range(len(tiles))]
        shades = [hidden(b, first + k) for k in range(len(tiles))]
        if diag:
            parts_s[-1] = jnp.where(causal(), parts_s[-1], NEG)
        peak = folded(parts_s[0], jnp.max) - shades[0]
        for k in range(1, len(tiles)):
            peak = jnp.maximum(peak, folded(parts_s[k], jnp.max) - shades[k])
        peak = jnp.maximum(top, jnp.max(peak, axis=0, keepdims=True))
        shrink = jnp.exp2(top - peak)
        amount = amount * shrink
        weighted = weighted * shrink
        for k in range(len(tiles)):
            p = jnp.exp2(parts_s[k] - (peak + shades[k]))
            gk = g[k * TILE : (k + 1) * TILE]
            scores[b, first + k - offset] = p.astype(BF16)
            amount += folded(p, jnp.sum)
            weighted += folded(p * gk, jnp.sum)
        if diag:
            middle[b] = jnp.sum(weighted, axis=0, keepdims=True) / jnp.sum(
                amount, axis=0, keepdims=True
            )
        mid = middle[b]
        for k in range(len(tiles)):
            gk = g[k * TILE : (k + 1) * TILE]
            probs_grad[b, first + k - offset] = (gk - mid).astype(BF16)
        peaks[b, step] = peak
        return peak, amount, weighted

    def ready(b, carried):
        top, amount, weighted = carried
        inverse = 1.0 / jnp.sum(amount, axis=0, keepdims=True)
        delta = jnp.sum(weighted, axis=0, keepdims=True) * inverse
        return top, inverse, delta - middle[b]

    def grade(b, step, tiles, stats):
        top, inverse, delta = stats
        first = (reach - step) * nblocks + tiles[0]
        size = len(tiles) * TILE
        held = pl.ds(first - offset, len(tiles))
        p = scores[b, held].reshape(size, chunk).astype(F32)
        p = p * (jnp.exp2(peaks[b, step] - top) * inverse)
        g = p * (probs_grad[b, held].reshape(size, chunk).astype(F32) - delta)
        return p.astype(BF16), g.astype(BF16)

    def finish(b, acc):
        att_dq[b * chunk : (b + 1) * chunk, :] = (acc.T * scale).astype(BF16)

    flip(0, (0, 1))
    row = jnp.zeros((8, chunk), F32)
    start = (jnp.full((1, chunk), NEG, F32), row, row)

    def first_pass(step, carried):
        pass_on(step + 1)
        pair_wait(step)
        flip(step, (0, 1))
        return tuple(weigh(b, step, (0, 1), carried[b]) for b in range(nblocks))

    carried = (weigh(0, 0, (0,), start, diag=True), weigh(1, 0, (0, 1), start, diag=True))

    @pl.when(nright <= 0)
    def _():
        state_join(1)

    carried = lax.fori_loop(1, near + 1, first_pass, carried)
    for i, ref in enumerate(carry):
        ref[...] = carried[0][i]

    @pl.when(far)
    def _():
        @pl.when(core == 0)
        def _():
            pair_wait(later_reach)

        flip(later_reach, (1,))
        more = weigh(0, later_reach, (1,), tuple(ref[...] for ref in carry))
        for i, ref in enumerate(carry):
            ref[...] = more[i]

    @pl.when(nright > 0)
    def _():
        state_join(1)

    @pl.when(in_first)
    def _():
        state_start(0, 0)

    @pl.when(jnp.logical_not(in_first))
    def _():
        state_join(0)

    stats = (ready(0, tuple(ref[...] for ref in carry)), ready(1, carried[1]))
    dq_sum[...] = jnp.zeros((width, chunk), F32)

    @pl.when(far)
    def _():
        at = keys_at(far_tile, 1)
        p, g = grade(0, later_reach, (1,), stats[0])
        dkey[at, :] = dot_nn(g, queries[0])
        dvalue[at, :] = dot_nn(p, douts[0])
        dq_sum[...] = dot_nn(flipped[later_reach, :, TILE : 2 * TILE], g)

        @pl.when(core == 0)
        def _():
            for which in range(2):
                grad_copy(which, later_reach).start()

    def last_pass(i, acc):
        step = near - i
        at = keys_at((reach - step) * nblocks, nblocks)
        ones = [grade(b, step, (0, 1), stats[b]) for b in range(nblocks)]
        p = jnp.concatenate([one[0] for one in ones], axis=1)
        g = jnp.concatenate([one[1] for one in ones], axis=1)
        dkey[at, :] = dot_nn(g, q[...])
        dvalue[at, :] = dot_nn(p, dout[...])
        for which in range(2):
            grad_copy(which, step).start()

        @pl.when(jnp.logical_or(i > 0, jnp.logical_and(far, core == 1)))
        def _():
            send_home(step + 1)

        return acc + dot_nn(flipped[step], g)

    acc = jnp.concatenate([dq_sum[...], jnp.zeros((width, chunk), F32)], axis=1)
    acc = lax.fori_loop(0, near + 1, last_pass, acc)
    for b in range(nblocks):
        finish(b, acc[:, b * chunk : (b + 1) * chunk])

    @pl.when(in_first)
    def _():
        state_join(0)

    for side in range(2):
        state_wait(1, side)

    intos, backs = [], []
    for h in range(heads):
        ends = []
        for side in range(2):
            close, mult = state_read(1, side, 0, h)
            ends.append(close + mult * state_read(1, side, 1, h)[0])
        keep = [jnp.exp(head_terms(b, h)[2]) for b in range(nblocks)]
        state = ends[0]
        into = []
        for b in range(nblocks):
            into.append(follows[b] * state)
            state = states[0, b, h] + keep[b] * into[b]
        state = ends[1]
        back = [None] * nblocks
        for b in reversed(range(nblocks)):
            back[b] = precedes[b] * state
            state = states[1, b, h] + keep[b] * back[b]
        intos.append([x.astype(BF16) for x in into])
        backs.append([x.astype(BF16) for x in back])
    for b in range(nblocks):
        for h in range(heads):
            row, col, total = head_terms(b, h)
            query, key, value, dol = (parts[a, b, h] for a in range(4))
            head_decay = jnp.exp(col)
            tail_decay = jnp.exp(total - col)
            at = pl.ds(h, TILE, stride=heads)
            wide[0, at, :] = grads[0, b, h] + head_decay * dot_nt(dol, intos[h][b])
            wide[1, at, :] = grads[1, b, h] + tail_decay * dot_nt(value, backs[h][b])
            wide[2, at, :] = grads[2, b, h] + tail_decay * dot_nn(key, backs[h][b])
        for a, ref in enumerate((lin_dq, lin_dk, lin_dv)):
            ref[b * rows : (b + 1) * rows, :] = wide[a].astype(BF16)

    for which in range(2):
        grad_copy(which, 0).wait_recv()
        paired[which, 0] = mine(which, 0)

    for step in range(1, reach + 1):

        @pl.when(takes(step, nright, 1))
        def _():
            home_copy(step).wait_recv()
            for which in range(2):
                paired[which, 0] += inbox[step - 1, which].astype(F32)

    att_dk[...] = (paired[0, 0] * scale).astype(BF16)
    att_dv[...] = paired[1, 0].astype(BF16)

    for which in range(2):
        grad_copy(which, 0).wait_send()
    for trip in range(2):
        for k, hop in enumerate(hops[trip]):
            for side, there in ((0, nright), (1, nleft)):

                @pl.when(hop <= there)
                def _():
                    state_copy(trip, side, k).wait_send()

    for step in range(1, reach + 1):

        @pl.when(takes(step, nright, 1))
        def _():
            for which in range(2):
                kv_copy(which, step).wait_send()

        @pl.when(takes(step, nleft, 1))
        def _():
            for which in range(2):
                pair_copy(which, step).wait_send()
            home_copy(step).wait_send()

        @pl.when(takes(step, nleft, 0))
        def _():
            for which in range(2):
                grad_copy(which, step).wait_send()


def long_kernel(
    count, limit, heads, nblocks,
    doc, lq, lk, lv, ld, dec_in, aq, ado, att_k, att_v,
    lin_dq, lin_dk, lin_dv, att_dq, att_dk, att_dv,
    wide, raw, dec, q, dout, kall, vall, parts, states, local, grads,
    scores, probs_grad, peaks, top_ref, amount_ref, weighted_ref, dq_sum, flipped, dkey, dvalue,
    snd, got, paired, out, inbox,
    raw_sem, kv_send, kv_recv, pair_send, pair_recv, st_send, st_recv,
    pg_send, pg_recv, home_send, home_recv,
):
    me = lax.axis_index("ctx")
    carry = (top_ref, amount_ref, weighted_ref)
    core = lax.axis_index("head")
    length = nblocks * TILE
    width = lq.shape[1]
    rows = TILE * heads
    first_devs = MOST // nblocks
    in_first = me < first_devs
    later_reach = limit // nblocks
    reach = slots_of(limit, nblocks)
    most = jnp.where(in_first, first_devs - 1, later_reach)
    nleft = jnp.minimum(jnp.where(in_first, me, me - first_devs), most)
    nright = jnp.minimum(jnp.where(in_first, first_devs - 1 - me, count - 1 - me), most)
    span = jnp.where(in_first, MOST, limit)

    def takes(step, there, who):
        if isinstance(step, int) and step != later_reach:
            return step <= there
        far = jnp.logical_and(step == later_reach, jnp.logical_not(in_first))
        return jnp.logical_and(step <= there, jnp.logical_or(jnp.logical_not(far), core == who))

    scale = width ** (-0.5)
    factor = scale * math.log2(math.e)

    loads = [
        pltpu.make_async_copy(ref, raw.at[a], raw_sem.at[a])
        for a, ref in enumerate((lq, lk, lv, ld))
    ]
    loads.append(pltpu.make_async_copy(dec_in, dec, raw_sem.at[4]))
    loads.append(pltpu.make_async_copy(aq, q, raw_sem.at[5]))
    loads.append(pltpu.make_async_copy(ado, dout, raw_sem.at[6]))
    own_rows = pl.ds(reach * length, length)
    loads.append(pltpu.make_async_copy(att_k, kall.at[own_rows], raw_sem.at[7]))
    loads.append(pltpu.make_async_copy(att_v, vall.at[own_rows], raw_sem.at[8]))
    for load in loads:
        load.start()

    barrier = pltpu.get_barrier_semaphore()
    pl.semaphore_signal(barrier, inc=1, device_id={"head": 1 - core}, device_id_type=MESH)
    for step in range(1, reach + 1):

        @pl.when(step <= nright)
        def _():
            pl.semaphore_signal(barrier, inc=1, device_id={"ctx": me + step}, device_id_type=MESH)

        @pl.when(step <= nleft)
        def _():
            pl.semaphore_signal(barrier, inc=1, device_id={"ctx": me - step}, device_id_type=MESH)

    pl.semaphore_wait(barrier, 1 + nleft + nright)

    pairs = ((att_k, kall), (att_v, vall))

    def half_of(step):
        start = pl.multiple_of(core * TILE, TILE)
        return start, pl.ds((reach - step) * length + start, TILE)

    def kv_copy(which, step):
        start, place = half_of(step)
        source, target = pairs[which]
        return pltpu.make_async_remote_copy(
            src_ref=source.at[pl.ds(start, TILE)],
            dst_ref=target.at[place],
            send_sem=kv_send.at[which, step - 1],
            recv_sem=kv_recv.at[which, step - 1],
            device_id={"ctx": me + step},
            device_id_type=MESH,
        )

    def pair_copy(which, step):
        target = pairs[which][1]
        place = half_of(step)[1]
        return pltpu.make_async_remote_copy(
            src_ref=target.at[place],
            dst_ref=target.at[place],
            send_sem=pair_send.at[which, step - 1],
            recv_sem=pair_recv.at[which, step - 1],
            device_id={"head": 1 - core},
            device_id_type=MESH,
        )

    def pass_on(step):
        @pl.when(takes(step, nleft, 1))
        def _():
            for which in range(2):
                kv_copy(which, step).wait_recv()
                pair_copy(which, step).start()

    def pair_wait(step):
        for which in range(2):
            pair_copy(which, step).wait_recv()

    hops = ((1, 2), (1, 4))

    def state_copy(trip, side, k):
        hop = hops[trip][k]
        return pltpu.make_async_remote_copy(
            src_ref=snd.at[trip, side],
            dst_ref=got.at[trip, side, k],
            send_sem=st_send.at[trip, side, k],
            recv_sem=st_recv.at[trip, side, k],
            device_id={"ctx": me + hop if side == 0 else me - hop},
            device_id_type=MESH,
        )

    def sent(side):
        return nright if side == 0 else nleft

    def due(side):
        return nleft if side == 0 else nright

    def state_start(trip, side):
        for k, hop in enumerate(hops[trip]):

            @pl.when(hop <= sent(side))
            def _():
                state_copy(trip, side, k).start()

            @pl.when(hop > due(side))
            def _():
                got[trip, side, k] = jnp.zeros(got.shape[3:], BF16)

    def state_wait(trip, side):
        for k, hop in enumerate(hops[trip]):

            @pl.when(hop <= due(side))
            def _():
                state_copy(trip, side, k).wait_recv()

    def state_write(trip, side, totals, mults):
        pads = []
        for h in range(heads):
            snd[trip, side, h * width : (h + 1) * width, :] = totals[h].astype(BF16)
            high, low = split(jnp.broadcast_to(mults[h], (1, width)))
            pads.append((high.astype(F32), low.astype(F32)))
        rows16 = [pads[h][0] for h in range(heads)] + [pads[h][1] for h in range(heads)]
        rows16.append(jnp.zeros((16 - 2 * heads, width), F32))
        snd[trip, side, heads * width :, :] = jnp.concatenate(rows16, axis=0).astype(BF16)

    def state_read(trip, side, k, h):
        at = heads * width
        total = got[trip, side, k, h * width : (h + 1) * width, :].astype(F32)
        pads = got[trip, side, k, at : at + 16, :].astype(F32)
        return total, pads[h : h + 1] + pads[heads + h : heads + h + 1]

    for step in range(1, reach + 1):

        @pl.when(takes(step, nright, 1))
        def _():
            for which in range(2):
                kv_copy(which, step).start()

    for load in loads:
        load.wait()
    follows, precedes, head_terms, t_sub, t_lane = decay_terms(me, count, nblocks, doc, dec)

    for b in range(nblocks):
        for a in range(4):
            wide[a] = raw[a, b * rows : (b + 1) * rows, :].astype(F32)
        for h in range(heads):
            row, col, total = head_terms(b, h)
            picked = [wide[a, pl.ds(h, TILE, stride=heads), :] for a in range(4)]
            for a in range(4):
                parts[a, b, h] = picked[a].astype(BF16)
            key_high, key_low = split((picked[1] * jnp.exp(total - col)).T)
            value = picked[2].astype(BF16)
            states[0, b, h] = dot_nn(key_high, value) + dot_nn(key_low, value)
            query_high, query_low = split((picked[0] * jnp.exp(col)).T)
            dol = picked[3].astype(BF16)
            states[1, b, h] = dot_nn(query_high, dol) + dot_nn(query_low, dol)

    totals, mults = ([], []), ([], [])
    for h in range(heads):
        keep = [jnp.exp(head_terms(b, h)[2]) for b in range(nblocks)]
        total_l = states[0, 0, h]
        mult_l = keep[0] * follows[0]
        for b in range(1, nblocks):
            total_l = states[0, b, h] + keep[b] * follows[b] * total_l
            mult_l = mult_l * keep[b] * follows[b]
        total_r = states[1, nblocks - 1, h]
        mult_r = keep[nblocks - 1] * precedes[nblocks - 1]
        for b in reversed(range(nblocks - 1)):
            total_r = states[1, b, h] + keep[b] * precedes[b] * total_r
            mult_r = mult_r * keep[b] * precedes[b]
        for side, total, mult in ((0, total_l, mult_l), (1, total_r, mult_r)):
            totals[side].append(total)
            mults[side].append(mult)
            local[side, h] = total
    for side in range(2):
        state_write(0, side, totals[side], mults[side])

    state_start(0, 1)

    @pl.when(jnp.logical_not(in_first))
    def _():
        state_start(0, 0)

    def state_join(side):
        state_wait(0, side)
        joined, spans = [], []
        for h in range(heads):
            one, mult_one = state_read(0, side, 0, h)
            two, mult_two = state_read(0, side, 1, h)
            joined.append(local[side, h] + mults[side][h] * (one + mult_one * two))
            spans.append(mults[side][h] * mult_one * mult_two)
        state_write(1, side, joined, spans)
        state_start(1, side)


    def within(b):
        for h in range(heads):
            row, col, total = head_terms(b, h)
            query, key, value, dol = (parts[a, b, h] for a in range(4))
            seen = t_sub <= t_lane
            weight = jnp.where(seen, jnp.exp(jnp.where(seen, row - col, 0.0)), 0.0)
            left = (dot_nt(value, dol) * weight).astype(BF16)
            right = (dot_nt(key, query) * weight).astype(BF16)
            grads[0, b, h] = dot_tn(left, key)
            grads[1, b, h] = dot_nn(left, query)
            grads[2, b, h] = dot_nn(right, dol)

    within(0)
    pass_on(1)
    for b in range(1, nblocks):
        within(b)
    def rows_of(j):
        return pl.ds(pl.multiple_of(j * TILE, TILE), TILE)

    sources = (dkey, dvalue)

    def grad_copy(which, step):
        return pltpu.make_async_remote_copy(
            src_ref=sources[which].at[rows_of((reach - step) * nblocks + 1 - core)],
            dst_ref=paired.at[which, step],
            send_sem=pg_send.at[which, step],
            recv_sem=pg_recv.at[which, step],
            device_id={"head": 1 - core},
            device_id_type=MESH,
        )

    def home_copy(step):
        return pltpu.make_async_remote_copy(
            src_ref=out.at[step - 1],
            dst_ref=inbox.at[step - 1],
            send_sem=home_send.at[step - 1],
            recv_sem=home_recv.at[step - 1],
            device_id={"ctx": me - step},
            device_id_type=MESH,
        )

    def mine(which, step):
        place = rows_of((reach - step) * nblocks + core)
        return sources[which][place, :] + paired[which, step]

    def send_home(step):
        for which in range(2):
            grad_copy(which, step).wait_recv()
        for which in range(2):
            out[step - 1, which] = mine(which, step).astype(BF16)
        home_copy(step).start()

    chunk = rows
    base = reach * nblocks
    offset = offset_of(limit, nblocks)
    near = jnp.minimum(nleft, jnp.where(in_first, reach, later_reach - 1))
    far = jnp.logical_and(jnp.logical_not(in_first), nleft == later_reach)
    far_tile = (reach - later_reach) * nblocks + 1
    queries = [q[b * chunk : (b + 1) * chunk, :] for b in range(nblocks)]
    douts = [dout[b * chunk : (b + 1) * chunk, :] for b in range(nblocks)]
    dkey[rows_of(base + 1), :] = jnp.zeros((TILE, width), F32)
    dvalue[rows_of(base + 1), :] = jnp.zeros((TILE, width), F32)

    def keys_at(j, n):
        return pl.ds(pl.multiple_of(j * TILE, TILE), n * TILE)

    def hidden(b, j):
        at = jnp.clip(me * nblocks - base + j, 0, count * nblocks - 1)
        return jnp.where(doc[at] == doc[me * nblocks + b], 0.0, -NEG).astype(F32)

    def folded(x, op):
        return op(x.reshape(TILE // 8, 8, chunk), axis=0)

    def causal():
        token = lax.broadcasted_iota(jnp.int32, (TILE, chunk), 1) // heads
        return lax.broadcasted_iota(jnp.int32, (TILE, chunk), 0) <= token

    def flip(step, tiles):
        first = (reach - step) * nblocks + tiles[0]
        low = tiles[0] * TILE
        block = kall[keys_at(first, len(tiles)), :].astype(F32).T.astype(BF16)
        flipped[step, :, low : low + len(tiles) * TILE] = block

    def weigh(b, step, tiles, carried, diag=False):
        top, amount, weighted = carried
        first = (reach - step) * nblocks + tiles[0]
        at = keys_at(first, len(tiles))
        s = dot_nt(kall[at, :], queries[b]) * factor
        g = dot_nt(vall[at, :], douts[b])
        parts_s = [s[k * TILE : (k + 1) * TILE] for k in range(len(tiles))]
        shades = [hidden(b, first + k) for k in range(len(tiles))]
        if diag:
            parts_s[-1] = jnp.where(causal(), parts_s[-1], NEG)
        peak = folded(parts_s[0], jnp.max) - shades[0]
        for k in range(1, len(tiles)):
            peak = jnp.maximum(peak, folded(parts_s[k], jnp.max) - shades[k])
        peak = jnp.maximum(top, jnp.max(peak, axis=0, keepdims=True))
        shrink = jnp.exp2(top - peak)
        amount = amount * shrink
        weighted = weighted * shrink
        for k in range(len(tiles)):
            p = jnp.exp2(parts_s[k] - (peak + shades[k]))
            gk = g[k * TILE : (k + 1) * TILE]
            scores[first + k - offset] = p
            probs_grad[first + k - offset] = gk
            amount += folded(p, jnp.sum)
            weighted += folded(p * gk, jnp.sum)
        peaks[b, step] = peak
        return peak, amount, weighted

    def ready(carried):
        top, amount, weighted = carried
        inverse = 1.0 / jnp.sum(amount, axis=0, keepdims=True)
        delta = jnp.sum(weighted, axis=0, keepdims=True) * inverse
        return top, inverse, delta

    def grade(b, step, tiles, stats, acc):
        top, inverse, delta = stats
        first = (reach - step) * nblocks + tiles[0]
        low = tiles[0] * TILE
        size = len(tiles) * TILE
        held = pl.ds(first - offset, len(tiles))
        p = scores[held].reshape(size, chunk) * (jnp.exp2(peaks[b, step] - top) * inverse)
        g = p * (probs_grad[held].reshape(size, chunk) - delta)
        p = p.astype(BF16)
        g = g.astype(BF16)
        at = keys_at(first, len(tiles))
        if b == 0:
            dvalue[at, :] = dot_nn(p, douts[b])
            dkey[at, :] = dot_nn(g, queries[b])
        else:
            dvalue[at, :] += dot_nn(p, douts[b])
            dkey[at, :] += dot_nn(g, queries[b])
        return acc + dot_nn(flipped[step, :, low : low + size], g)

    def finish(b, acc):
        att_dq[b * chunk : (b + 1) * chunk, :] = (acc.T * scale).astype(BF16)

    flip(0, (0, 1))
    row = jnp.zeros((8, chunk), F32)
    start = (jnp.full((1, chunk), NEG, F32), row, row)
    state_zero = weigh(0, 0, (0,), start, diag=True)
    for i, ref in enumerate(carry):
        ref[...] = state_zero[i]

    def first_pass(step, carried):
        pass_on(step + 1)
        pair_wait(step)
        flip(step, (0, 1))
        return weigh(0, step, (0, 1), carried)

    carried = lax.fori_loop(1, near + 1, first_pass, state_zero)
    for i, ref in enumerate(carry):
        ref[...] = carried[i]

    @pl.when(far)
    def _():
        @pl.when(core == 0)
        def _():
            pair_wait(later_reach)

        flip(later_reach, (1,))
        more = weigh(0, later_reach, (1,), tuple(ref[...] for ref in carry))
        for i, ref in enumerate(carry):
            ref[...] = more[i]

    state_join(1)

    @pl.when(in_first)
    def _():
        state_start(0, 0)


    stats = ready(tuple(ref[...] for ref in carry))
    acc = grade(0, 0, (0,), stats, jnp.zeros((width, chunk), F32))
    carried = weigh(1, 0, (0, 1), start, diag=True)

    def both(step, packed):
        carried, acc = packed
        acc = grade(0, step, (0, 1), stats, acc)
        return weigh(1, step, (0, 1), carried), acc

    carried, acc = lax.fori_loop(1, near + 1, both, (carried, acc))
    dq_sum[...] = acc

    @pl.when(far)
    def _():
        dq_sum[...] = grade(0, later_reach, (1,), stats, dq_sum[...])

        @pl.when(core == 0)
        def _():
            for which in range(2):
                grad_copy(which, later_reach).start()

    finish(0, dq_sum[...])
    state_join(0)

    @pl.when(jnp.logical_and(far, core == 1))
    def _():
        send_home(later_reach)

    last_stats = ready(carried)

    def last_pass(i, acc):
        step = near - i
        acc = grade(1, step, (0, 1), last_stats, acc)
        for which in range(2):
            grad_copy(which, step).start()

        @pl.when(i > 0)
        def _():
            send_home(step + 1)

        return acc

    finish(1, lax.fori_loop(0, near + 1, last_pass, jnp.zeros((width, chunk), F32)))
    for side in range(2):
        state_wait(1, side)

    intos, backs = [], []
    for h in range(heads):
        ends = []
        for side in range(2):
            close, mult = state_read(1, side, 0, h)
            ends.append(close + mult * state_read(1, side, 1, h)[0])
        keep = [jnp.exp(head_terms(b, h)[2]) for b in range(nblocks)]
        state = ends[0]
        into = []
        for b in range(nblocks):
            into.append(follows[b] * state)
            state = states[0, b, h] + keep[b] * into[b]
        state = ends[1]
        back = [None] * nblocks
        for b in reversed(range(nblocks)):
            back[b] = precedes[b] * state
            state = states[1, b, h] + keep[b] * back[b]
        intos.append([x.astype(BF16) for x in into])
        backs.append([x.astype(BF16) for x in back])
    for b in range(nblocks):
        for h in range(heads):
            row, col, total = head_terms(b, h)
            query, key, value, dol = (parts[a, b, h] for a in range(4))
            head_decay = jnp.exp(col)
            tail_decay = jnp.exp(total - col)
            at = pl.ds(h, TILE, stride=heads)
            wide[0, at, :] = grads[0, b, h] + head_decay * dot_nt(dol, intos[h][b])
            wide[1, at, :] = grads[1, b, h] + tail_decay * dot_nt(value, backs[h][b])
            wide[2, at, :] = grads[2, b, h] + tail_decay * dot_nn(key, backs[h][b])
        for a, ref in enumerate((lin_dq, lin_dk, lin_dv)):
            ref[b * rows : (b + 1) * rows, :] = wide[a].astype(BF16)

    for which in range(2):
        grad_copy(which, 0).wait_recv()
        paired[which, 0] = mine(which, 0)

    for step in range(1, reach + 1):

        @pl.when(takes(step, nright, 1))
        def _():
            home_copy(step).wait_recv()
            for which in range(2):
                paired[which, 0] += inbox[step - 1, which].astype(F32)

    att_dk[...] = (paired[0, 0] * scale).astype(BF16)
    att_dv[...] = paired[1, 0].astype(BF16)

    for which in range(2):
        grad_copy(which, 0).wait_send()
    for trip in range(2):
        for k, hop in enumerate(hops[trip]):
            for side, there in ((0, nright), (1, nleft)):

                @pl.when(hop <= there)
                def _():
                    state_copy(trip, side, k).wait_send()

    for step in range(1, reach + 1):

        @pl.when(takes(step, nright, 1))
        def _():
            for which in range(2):
                kv_copy(which, step).wait_send()

        @pl.when(takes(step, nleft, 1))
        def _():
            for which in range(2):
                pair_copy(which, step).wait_send()
            home_copy(step).wait_send()

        @pl.when(takes(step, nleft, 0))
        def _():
            for which in range(2):
                grad_copy(which, step).wait_send()


def slots_of(limit, nblocks):
    return max(MOST // nblocks - 1, limit // nblocks)


def offset_of(limit, nblocks):
    return max(0, slots_of(limit, nblocks) * nblocks + 1 - MOST)


def place_kernel(*refs):
    half = (len(refs) - 1) // 2
    sems = refs[-1]
    moves = [
        pltpu.make_async_copy(refs[i], refs[half + i], sems.at[i]) for i in range(half)
    ]
    for move in moves:
        move.start()
    for move in moves:
        move.wait()


def place(outs):
    return pl.pallas_call(
        place_kernel,
        out_shape=[SHAPE(x.shape, x.dtype) for x in outs],
        in_specs=[ANYWHERE] * len(outs),
        out_specs=[ANYWHERE] * len(outs),
        scratch_shapes=[DMA((len(outs),))],
        name="place",
    )(*outs)


def call_whole(count, limit, heads, nblocks, args):
    width = args[-1].shape[1]
    rows = nblocks * TILE * heads
    reach = slots_of(limit, nblocks)
    window = (reach + 1) * nblocks * TILE
    held = (reach + 1) * nblocks - offset_of(limit, nblocks)
    return pl.pallas_call(
        functools.partial(whole_kernel, count, limit, heads, nblocks),
        out_shape=[SHAPE((rows, width), BF16)] * 4 + [SHAPE((TILE, width), BF16)] * 2,
        in_specs=[IN_SMEM] + [ANYWHERE] * 9,
        out_specs=[IN_VMEM] * 6,
        scratch_shapes=[
            pltpu.VMEM((3, TILE * heads, width), F32),
            pltpu.VMEM((4, rows, width), BF16),
            pltpu.VMEM((heads, nblocks * TILE), F32),
            pltpu.VMEM((rows, width), BF16),
            pltpu.VMEM((rows, width), BF16),
            pltpu.VMEM((window, width), BF16),
            pltpu.VMEM((window, width), BF16),
            pltpu.VMEM((4, nblocks, heads, TILE, width), BF16),
            pltpu.VMEM((2, nblocks, heads, width, width), F32),
            pltpu.VMEM((2, heads, width, width), F32),
            pltpu.VMEM((3, nblocks, heads, TILE, width), F32),
            pltpu.VMEM((nblocks, held, TILE, TILE * heads), BF16),
            pltpu.VMEM((nblocks, held, TILE, TILE * heads), BF16),
            pltpu.VMEM((nblocks, reach + 1, 1, TILE * heads), F32),
            pltpu.VMEM((1, TILE * heads), F32),
            pltpu.VMEM((8, TILE * heads), F32),
            pltpu.VMEM((8, TILE * heads), F32),
            pltpu.VMEM((nblocks, 1, TILE * heads), F32),
            pltpu.VMEM((width, TILE * heads), F32),
            pltpu.VMEM((reach + 1, width, nblocks * TILE), BF16),
            pltpu.VMEM((window, width), F32),
            pltpu.VMEM((window, width), F32),
            pltpu.VMEM((2, 2, heads * width + 16, width), BF16),
            pltpu.VMEM((2, 2, 2, heads * width + 16, width), BF16),
            pltpu.VMEM((2, reach + 1, TILE, width), F32),
            pltpu.VMEM((reach, 2, TILE, width), BF16),
            pltpu.VMEM((reach, 2, TILE, width), BF16),
            DMA((9,)),
            DMA((2, reach)),
            DMA((2, reach)),
            DMA((2, reach)),
            DMA((2, reach)),
            DMA((2, 2, 2)),
            DMA((2, 2, 2)),
            DMA((2, reach + 1)),
            DMA((2, reach + 1)),
            DMA((reach,)),
            DMA((reach,)),
        ],
        compiler_params=pltpu.CompilerParams(
            collective_id=0 if limit == MOST else 1,
            has_side_effects=True,
            vmem_limit_bytes=VMEM_LIMIT,
        ),
        name="whole_%d" % limit,
    )(*args)


def call_long(count, limit, heads, nblocks, args):
    width = args[-1].shape[1]
    rows = nblocks * TILE * heads
    reach = slots_of(limit, nblocks)
    window = (reach + 1) * nblocks * TILE
    held = (reach + 1) * nblocks - offset_of(limit, nblocks)
    return pl.pallas_call(
        functools.partial(long_kernel, count, limit, heads, nblocks),
        out_shape=[SHAPE((rows, width), BF16)] * 4 + [SHAPE((TILE, width), BF16)] * 2,
        in_specs=[IN_SMEM] + [ANYWHERE] * 9,
        out_specs=[IN_VMEM] * 6,
        scratch_shapes=[
            pltpu.VMEM((4, TILE * heads, width), F32),
            pltpu.VMEM((4, rows, width), BF16),
            pltpu.VMEM((heads, nblocks * TILE), F32),
            pltpu.VMEM((rows, width), BF16),
            pltpu.VMEM((rows, width), BF16),
            pltpu.VMEM((window, width), BF16),
            pltpu.VMEM((window, width), BF16),
            pltpu.VMEM((4, nblocks, heads, TILE, width), BF16),
            pltpu.VMEM((2, nblocks, heads, width, width), F32),
            pltpu.VMEM((2, heads, width, width), F32),
            pltpu.VMEM((3, nblocks, heads, TILE, width), F32),
            pltpu.VMEM((held, TILE, TILE * heads), F32),
            pltpu.VMEM((held, TILE, TILE * heads), F32),
            pltpu.VMEM((nblocks, reach + 1, 1, TILE * heads), F32),
            pltpu.VMEM((1, TILE * heads), F32),
            pltpu.VMEM((8, TILE * heads), F32),
            pltpu.VMEM((8, TILE * heads), F32),
            pltpu.VMEM((width, TILE * heads), F32),
            pltpu.VMEM((reach + 1, width, nblocks * TILE), BF16),
            pltpu.VMEM((window, width), F32),
            pltpu.VMEM((window, width), F32),
            pltpu.VMEM((2, 2, heads * width + 16, width), BF16),
            pltpu.VMEM((2, 2, 2, heads * width + 16, width), BF16),
            pltpu.VMEM((2, reach + 1, TILE, width), F32),
            pltpu.VMEM((reach, 2, TILE, width), BF16),
            pltpu.VMEM((reach, 2, TILE, width), BF16),
            DMA((9,)),
            DMA((2, reach)),
            DMA((2, reach)),
            DMA((2, reach)),
            DMA((2, reach)),
            DMA((2, 2, 2)),
            DMA((2, 2, 2)),
            DMA((2, reach + 1)),
            DMA((2, reach + 1)),
            DMA((reach,)),
            DMA((reach,)),
        ],
        compiler_params=pltpu.CompilerParams(
            collective_id=0 if limit == MOST else 1,
            has_side_effects=True,
            vmem_limit_bytes=VMEM_LIMIT,
        ),
        name="long_%d" % limit,
    )(*args)


def shards(count, lin_q, lin_k, lin_v, lin_dout, lin_decay, att_q, att_k, att_v, att_dout, doc_block):
    length, heads, width = lin_q.shape
    nblocks = length // TILE
    assert nblocks == 2
    flat = lambda x: x.reshape(length * heads, width)
    args = (
        doc_block, flat(lin_q), flat(lin_k), flat(lin_v), flat(lin_dout), lin_decay,
        flat(att_q), flat(att_dout), att_k, att_v,
    )
    later = doc_block[MOST:]
    long = jnp.any(later[SHORT:] == later[:-SHORT])
    outs = lax.cond(
        long,
        lambda *a: call_long(count, MOST, heads, nblocks, a),
        lambda *a: call_whole(count, SHORT, heads, nblocks, a),
        *args,
    )
    outs = place(outs)
    full = lambda x: x.reshape(length, heads, width)
    return (full(outs[0]), full(outs[1]), full(outs[2]), full(outs[3]), outs[4], outs[5])


def solution(mesh):
    return jax.shard_map(
        functools.partial(shards, mesh.shape["ctx"]),
        mesh=mesh,
        in_specs=(
            P("ctx", "head", None),
            P("ctx", "head", None),
            P("ctx", "head", None),
            P("ctx", "head", None),
            P("head", "ctx"),
            P("ctx", "head", None),
            P("ctx", None),
            P("ctx", None),
            P("ctx", "head", None),
            P(),
        ),
        out_specs=(
            P("ctx", "head", None),
            P("ctx", "head", None),
            P("ctx", "head", None),
            P("ctx", "head", None),
            P(("ctx", "head"), None),
            P(("ctx", "head"), None),
        ),
        check_vma=False,
    )
```

```python
import functools
import math

import jax
import jax.numpy as jnp
from jax import lax
from jax.experimental import pallas as pl
from jax.experimental.pallas import tpu as pltpu
from jax.sharding import PartitionSpec as P

TILE = 256
MOST = 12
SHORT = 8
NEG = -1e30
MESH = pl.DeviceIdType.MESH
F32 = jnp.float32
BF16 = jnp.bfloat16
SHAPE = jax.ShapeDtypeStruct
DMA = pltpu.SemaphoreType.DMA
IN_VMEM = pl.BlockSpec(memory_space=pltpu.VMEM)
IN_SMEM = pl.BlockSpec(memory_space=pltpu.SMEM)
ANYWHERE = pl.BlockSpec(memory_space=pl.ANY)
VMEM_LIMIT = 60 * 1024 * 1024


def dot_nn(a, b):
    return lax.dot_general(a, b, (((1,), (0,)), ((), ())), preferred_element_type=F32)


def dot_nt(a, b):
    return lax.dot_general(a, b, (((1,), (1,)), ((), ())), preferred_element_type=F32)


def dot_tn(a, b):
    return lax.dot_general(a, b, (((0,), (0,)), ((), ())), preferred_element_type=F32)


def split(x):
    high = x.astype(BF16)
    return high, (x - high.astype(F32)).astype(BF16)


def decay_terms(me, count, nblocks, doc, dec):
    t_sub = lax.broadcasted_iota(jnp.int32, (TILE, TILE), 0)
    t_lane = lax.broadcasted_iota(jnp.int32, (TILE, TILE), 1)
    upper = (t_sub <= t_lane).astype(F32)
    lower = (t_sub >= t_lane).astype(F32)

    def link(at_one, at_two):
        one = jnp.clip(at_one, 0, count * nblocks - 1)
        two = jnp.clip(at_two, 0, count * nblocks - 1)
        inside = jnp.logical_and(at_one >= 0, at_two < count * nblocks)
        same = jnp.logical_and(doc[one] == doc[two], inside)
        return jnp.where(same, 1.0, 0.0).astype(F32)

    follows = [link(me * nblocks + b - 1, me * nblocks + b) for b in range(nblocks)]
    precedes = [link(me * nblocks + b, me * nblocks + b + 1) for b in range(nblocks)]

    cum_row, cum_col = [], []
    for b in range(nblocks):
        piece = dec[:, b * TILE : (b + 1) * TILE]
        cum_row.append(
            lax.dot_general(
                piece, upper, (((1,), (0,)), ((), ())),
                preferred_element_type=F32, precision=lax.Precision.HIGHEST,
            )
        )
        cum_col.append(
            lax.dot_general(
                lower, piece, (((1,), (1,)), ((), ())),
                preferred_element_type=F32, precision=lax.Precision.HIGHEST,
            )
        )

    def head_terms(b, h):
        row = cum_row[b][h : h + 1, :]
        col = cum_col[b][:, h : h + 1]
        total = col[TILE - 1 : TILE, :]
        return row, col, total

    return follows, precedes, head_terms, t_sub, t_lane


def whole_kernel(
    count, limit, heads, nblocks,
    doc, lq, lk, lv, ld, dec_in, aq, ado, att_k, att_v,
    lin_dq, lin_dk, lin_dv, att_dq, att_dk, att_dv,
    wide, raw, dec, q, dout, kall, vall, parts, states, local, grads,
    scores, probs_grad, peaks, top_ref, amount_ref, weighted_ref, middle, dq_sum, flipped, dkey, dvalue,
    snd, got, paired, out, inbox,
    raw_sem, kv_send, kv_recv, pair_send, pair_recv, st_send, st_recv,
    pg_send, pg_recv, home_send, home_recv,
):
    me = lax.axis_index("ctx")
    carry = (top_ref, amount_ref, weighted_ref)
    core = lax.axis_index("head")
    length = nblocks * TILE
    width = lq.shape[1]
    rows = TILE * heads
    first_devs = MOST // nblocks
    in_first = me < first_devs
    later_reach = limit // nblocks
    reach = slots_of(limit, nblocks)
    most = jnp.where(in_first, first_devs - 1, later_reach)
    nleft = jnp.minimum(jnp.where(in_first, me, me - first_devs), most)
    nright = jnp.minimum(jnp.where(in_first, first_devs - 1 - me, count - 1 - me), most)
    span = jnp.where(in_first, MOST, limit)

    def takes(step, there, who):
        if isinstance(step, int) and step != later_reach:
            return step <= there
        far = jnp.logical_and(step == later_reach, jnp.logical_not(in_first))
        return jnp.logical_and(step <= there, jnp.logical_or(jnp.logical_not(far), core == who))

    scale = width ** (-0.5)
    factor = scale * math.log2(math.e)

    loads = [
        pltpu.make_async_copy(ref, raw.at[a], raw_sem.at[a])
        for a, ref in enumerate((lq, lk, lv, ld))
    ]
    loads.append(pltpu.make_async_copy(dec_in, dec, raw_sem.at[4]))
    loads.append(pltpu.make_async_copy(aq, q, raw_sem.at[5]))
    loads.append(pltpu.make_async_copy(ado, dout, raw_sem.at[6]))
    own_rows = pl.ds(reach * length, length)
    loads.append(pltpu.make_async_copy(att_k, kall.at[own_rows], raw_sem.at[7]))
    loads.append(pltpu.make_async_copy(att_v, vall.at[own_rows], raw_sem.at[8]))
    for load in loads:
        load.start()

    barrier = pltpu.get_barrier_semaphore()
    pl.semaphore_signal(barrier, inc=1, device_id={"head": 1 - core}, device_id_type=MESH)
    for step in range(1, reach + 1):

        @pl.when(step <= nright)
        def _():
            pl.semaphore_signal(barrier, inc=1, device_id={"ctx": me + step}, device_id_type=MESH)

        @pl.when(step <= nleft)
        def _():
            pl.semaphore_signal(barrier, inc=1, device_id={"ctx": me - step}, device_id_type=MESH)

    pl.semaphore_wait(barrier, 1 + nleft + nright)

    pairs = ((att_k, kall), (att_v, vall))

    def half_of(step):
        start = pl.multiple_of(core * TILE, TILE)
        return start, pl.ds((reach - step) * length + start, TILE)

    def kv_copy(which, step):
        start, place = half_of(step)
        source, target = pairs[which]
        return pltpu.make_async_remote_copy(
            src_ref=source.at[pl.ds(start, TILE)],
            dst_ref=target.at[place],
            send_sem=kv_send.at[which, step - 1],
            recv_sem=kv_recv.at[which, step - 1],
            device_id={"ctx": me + step},
            device_id_type=MESH,
        )

    def pair_copy(which, step):
        target = pairs[which][1]
        place = half_of(step)[1]
        return pltpu.make_async_remote_copy(
            src_ref=target.at[place],
            dst_ref=target.at[place],
            send_sem=pair_send.at[which, step - 1],
            recv_sem=pair_recv.at[which, step - 1],
            device_id={"head": 1 - core},
            device_id_type=MESH,
        )

    def pass_on(step):
        @pl.when(takes(step, nleft, 1))
        def _():
            for which in range(2):
                kv_copy(which, step).wait_recv()
                pair_copy(which, step).start()

    def pair_wait(step):
        for which in range(2):
            pair_copy(which, step).wait_recv()

    hops = ((1, 2), (1, 4))

    def state_copy(trip, side, k):
        hop = hops[trip][k]
        return pltpu.make_async_remote_copy(
            src_ref=snd.at[trip, side],
            dst_ref=got.at[trip, side, k],
            send_sem=st_send.at[trip, side, k],
            recv_sem=st_recv.at[trip, side, k],
            device_id={"ctx": me + hop if side == 0 else me - hop},
            device_id_type=MESH,
        )

    def sent(side):
        return nright if side == 0 else nleft

    def due(side):
        return nleft if side == 0 else nright

    def state_start(trip, side):
        for k, hop in enumerate(hops[trip]):

            @pl.when(hop <= sent(side))
            def _():
                state_copy(trip, side, k).start()

            @pl.when(hop > due(side))
            def _():
                got[trip, side, k] = jnp.zeros(got.shape[3:], BF16)

    def state_wait(trip, side):
        for k, hop in enumerate(hops[trip]):

            @pl.when(hop <= due(side))
            def _():
                state_copy(trip, side, k).wait_recv()

    def state_write(trip, side, totals, mults):
        pads = []
        for h in range(heads):
            snd[trip, side, h * width : (h + 1) * width, :] = totals[h].astype(BF16)
            high, low = split(jnp.broadcast_to(mults[h], (1, width)))
            pads.append((high.astype(F32), low.astype(F32)))
        rows16 = [pads[h][0] for h in range(heads)] + [pads[h][1] for h in range(heads)]
        rows16.append(jnp.zeros((16 - 2 * heads, width), F32))
        snd[trip, side, heads * width :, :] = jnp.concatenate(rows16, axis=0).astype(BF16)

    def state_read(trip, side, k, h):
        at = heads * width
        total = got[trip, side, k, h * width : (h + 1) * width, :].astype(F32)
        pads = got[trip, side, k, at : at + 16, :].astype(F32)
        return total, pads[h : h + 1] + pads[heads + h : heads + h + 1]

    for step in range(1, reach + 1):

        @pl.when(takes(step, nright, 1))
        def _():
            for which in range(2):
                kv_copy(which, step).start()

    for load in loads:
        load.wait()
    follows, precedes, head_terms, t_sub, t_lane = decay_terms(me, count, nblocks, doc, dec)

    for b in range(nblocks):
        for a in range(4):
            wide[a % 3] = raw[a, b * rows : (b + 1) * rows, :].astype(F32)
            for h in range(heads):
                parts[a, b, h] = wide[a % 3, pl.ds(h, TILE, stride=heads), :].astype(BF16)
        for h in range(heads):
            row, col, total = head_terms(b, h)
            picked = [parts[a, b, h].astype(F32) for a in range(4)]
            key_high, key_low = split((picked[1] * jnp.exp(total - col)).T)
            value = picked[2].astype(BF16)
            states[0, b, h] = dot_nn(key_high, value) + dot_nn(key_low, value)
            query_high, query_low = split((picked[0] * jnp.exp(col)).T)
            dol = picked[3].astype(BF16)
            states[1, b, h] = dot_nn(query_high, dol) + dot_nn(query_low, dol)

    totals, mults = ([], []), ([], [])
    for h in range(heads):
        keep = [jnp.exp(head_terms(b, h)[2]) for b in range(nblocks)]
        total_l = states[0, 0, h]
        mult_l = keep[0] * follows[0]
        for b in range(1, nblocks):
            total_l = states[0, b, h] + keep[b] * follows[b] * total_l
            mult_l = mult_l * keep[b] * follows[b]
        total_r = states[1, nblocks - 1, h]
        mult_r = keep[nblocks - 1] * precedes[nblocks - 1]
        for b in reversed(range(nblocks - 1)):
            total_r = states[1, b, h] + keep[b] * precedes[b] * total_r
            mult_r = mult_r * keep[b] * precedes[b]
        for side, total, mult in ((0, total_l, mult_l), (1, total_r, mult_r)):
            totals[side].append(total)
            mults[side].append(mult)
            local[side, h] = total
    for side in range(2):
        state_write(0, side, totals[side], mults[side])

    state_start(0, 1)

    @pl.when(jnp.logical_not(in_first))
    def _():
        state_start(0, 0)

    def state_join(side):
        state_wait(0, side)
        joined, spans = [], []
        for h in range(heads):
            one, mult_one = state_read(0, side, 0, h)
            two, mult_two = state_read(0, side, 1, h)
            joined.append(local[side, h] + mults[side][h] * (one + mult_one * two))
            spans.append(mults[side][h] * mult_one * mult_two)
        state_write(1, side, joined, spans)
        state_start(1, side)


    def within(b):
        for h in range(heads):
            row, col, total = head_terms(b, h)
            query, key, value, dol = (parts[a, b, h] for a in range(4))
            seen = t_sub <= t_lane
            weight = jnp.where(seen, jnp.exp(jnp.where(seen, row - col, 0.0)), 0.0)
            left = (dot_nt(value, dol) * weight).astype(BF16)
            right = (dot_nt(key, query) * weight).astype(BF16)
            grads[0, b, h] = dot_tn(left, key)
            grads[1, b, h] = dot_nn(left, query)
            grads[2, b, h] = dot_nn(right, dol)

    within(0)
    pass_on(1)
    for b in range(1, nblocks):
        within(b)
    def rows_of(j):
        return pl.ds(pl.multiple_of(j * TILE, TILE), TILE)

    sources = (dkey, dvalue)

    def grad_copy(which, step):
        return pltpu.make_async_remote_copy(
            src_ref=sources[which].at[rows_of((reach - step) * nblocks + 1 - core)],
            dst_ref=paired.at[which, step],
            send_sem=pg_send.at[which, step],
            recv_sem=pg_recv.at[which, step],
            device_id={"head": 1 - core},
            device_id_type=MESH,
        )

    def home_copy(step):
        return pltpu.make_async_remote_copy(
            src_ref=out.at[step - 1],
            dst_ref=inbox.at[step - 1],
            send_sem=home_send.at[step - 1],
            recv_sem=home_recv.at[step - 1],
            device_id={"ctx": me - step},
            device_id_type=MESH,
        )

    def mine(which, step):
        place = rows_of((reach - step) * nblocks + core)
        return sources[which][place, :] + paired[which, step]

    def send_home(step):
        for which in range(2):
            grad_copy(which, step).wait_recv()
        for which in range(2):
            out[step - 1, which] = mine(which, step).astype(BF16)
        home_copy(step).start()

    chunk = rows
    base = reach * nblocks
    offset = offset_of(limit, nblocks)
    near = jnp.minimum(nleft, jnp.where(in_first, reach, later_reach - 1))
    far = jnp.logical_and(jnp.logical_not(in_first), nleft == later_reach)
    far_tile = (reach - later_reach) * nblocks + 1
    queries = [q[b * chunk : (b + 1) * chunk, :] for b in range(nblocks)]
    douts = [dout[b * chunk : (b + 1) * chunk, :] for b in range(nblocks)]
    scores[0, base + 1 - offset] = jnp.zeros((TILE, chunk), BF16)
    probs_grad[0, base + 1 - offset] = jnp.zeros((TILE, chunk), BF16)

    def keys_at(j, n):
        return pl.ds(pl.multiple_of(j * TILE, TILE), n * TILE)

    def hidden(b, j):
        at = jnp.clip(me * nblocks - base + j, 0, count * nblocks - 1)
        return jnp.where(doc[at] == doc[me * nblocks + b], 0.0, -NEG).astype(F32)

    def folded(x, op):
        return op(x.reshape(TILE // 8, 8, chunk), axis=0)

    def causal():
        token = lax.broadcasted_iota(jnp.int32, (TILE, chunk), 1) // heads
        return lax.broadcasted_iota(jnp.int32, (TILE, chunk), 0) <= token

    def flip(step, tiles):
        first = (reach - step) * nblocks + tiles[0]
        low = tiles[0] * TILE
        block = kall[keys_at(first, len(tiles)), :].astype(F32).T.astype(BF16)
        flipped[step, :, low : low + len(tiles) * TILE] = block

    def weigh(b, step, tiles, carried, diag=False, given=None):
        top, amount, weighted = carried
        first = (reach - step) * nblocks + tiles[0]
        at = keys_at(first, len(tiles))
        s, g = given or (dot_nt(kall[at, :], queries[b]), dot_nt(vall[at, :], douts[b]))
        s = s * factor
        parts_s = [s[k * TILE : (k + 1) * TILE] for k in range(len(tiles))]
        shades = [hidden(b, first + k) for k in range(len(tiles))]
        if diag:
            parts_s[-1] = jnp.where(causal(), parts_s[-1], NEG)
        peak = folded(parts_s[0], jnp.max) - shades[0]
        for k in range(1, len(tiles)):
            peak = jnp.maximum(peak, folded(parts_s[k], jnp.max) - shades[k])
        peak = jnp.maximum(top, jnp.max(peak, axis=0, keepdims=True))
        shrink = jnp.exp2(top - peak)
        amount = amount * shrink
        weighted = weighted * shrink
        for k in range(len(tiles)):
            p = jnp.exp2(parts_s[k] - (peak + shades[k]))
            gk = g[k * TILE : (k + 1) * TILE]
            scores[b, first + k - offset] = p.astype(BF16)
            amount += folded(p, jnp.sum)
            weighted += folded(p * gk, jnp.sum)
        if diag:
            middle[b] = jnp.sum(weighted, axis=0, keepdims=True) / jnp.sum(
                amount, axis=0, keepdims=True
            )
        mid = middle[b]
        for k in range(len(tiles)):
            gk = g[k * TILE : (k + 1) * TILE]
            probs_grad[b, first + k - offset] = (gk - mid).astype(BF16)
        peaks[b, step] = peak
        return peak, amount, weighted

    def ready(b, carried):
        top, amount, weighted = carried
        inverse = 1.0 / jnp.sum(amount, axis=0, keepdims=True)
        delta = jnp.sum(weighted, axis=0, keepdims=True) * inverse
        return top, inverse, delta - middle[b]

    def grade(b, step, tiles, stats):
        top, inverse, delta = stats
        first = (reach - step) * nblocks + tiles[0]
        size = len(tiles) * TILE
        held = pl.ds(first - offset, len(tiles))
        p = scores[b, held].reshape(size, chunk).astype(F32)
        p = p * (jnp.exp2(peaks[b, step] - top) * inverse)
        g = p * (probs_grad[b, held].reshape(size, chunk).astype(F32) - delta)
        return p.astype(BF16), g.astype(BF16)

    def finish(b, acc):
        att_dq[b * chunk : (b + 1) * chunk, :] = (acc.T * scale).astype(BF16)

    flip(0, (0, 1))
    row = jnp.zeros((8, chunk), F32)
    start = (jnp.full((1, chunk), NEG, F32), row, row)

    def first_pass(step, carried):
        pass_on(step + 1)
        pair_wait(step)
        flip(step, (0, 1))
        at = keys_at((reach - step) * nblocks, nblocks)
        s = dot_nt(kall[at, :], q[...])
        g = dot_nt(vall[at, :], dout[...])
        cuts = [slice(b * chunk, (b + 1) * chunk) for b in range(nblocks)]
        return tuple(
            weigh(b, step, (0, 1), carried[b], given=(s[:, cuts[b]], g[:, cuts[b]]))
            for b in range(nblocks)
        )

    carried = (weigh(0, 0, (0,), start, diag=True), weigh(1, 0, (0, 1), start, diag=True))

    @pl.when(nright <= 0)
    def _():
        state_join(1)

    carried = lax.fori_loop(1, near + 1, first_pass, carried)
    for i, ref in enumerate(carry):
        ref[...] = carried[0][i]

    @pl.when(far)
    def _():
        @pl.when(core == 0)
        def _():
            pair_wait(later_reach)

        flip(later_reach, (1,))
        more = weigh(0, later_reach, (1,), tuple(ref[...] for ref in carry))
        for i, ref in enumerate(carry):
            ref[...] = more[i]

    @pl.when(nright > 0)
    def _():
        state_join(1)

    @pl.when(in_first)
    def _():
        state_start(0, 0)

    @pl.when(jnp.logical_not(in_first))
    def _():
        state_join(0)

    stats = (ready(0, tuple(ref[...] for ref in carry)), ready(1, carried[1]))
    dq_sum[...] = jnp.zeros((width, chunk), F32)

    @pl.when(far)
    def _():
        at = keys_at(far_tile, 1)
        p, g = grade(0, later_reach, (1,), stats[0])
        dkey[at, :] = dot_nn(g, queries[0])
        dvalue[at, :] = dot_nn(p, douts[0])
        dq_sum[...] = dot_nn(flipped[later_reach, :, TILE : 2 * TILE], g)

        @pl.when(core == 0)
        def _():
            for which in range(2):
                grad_copy(which, later_reach).start()

    def last_pass(i, acc):
        step = near - i
        at = keys_at((reach - step) * nblocks, nblocks)
        ones = [grade(b, step, (0, 1), stats[b]) for b in range(nblocks)]
        p = jnp.concatenate([one[0] for one in ones], axis=1)
        g = jnp.concatenate([one[1] for one in ones], axis=1)
        dkey[at, :] = dot_nn(g, q[...])
        dvalue[at, :] = dot_nn(p, dout[...])
        for which in range(2):
            grad_copy(which, step).start()

        @pl.when(jnp.logical_or(i > 0, jnp.logical_and(far, core == 1)))
        def _():
            send_home(step + 1)

        return acc + dot_nn(flipped[step], g)

    acc = jnp.concatenate([dq_sum[...], jnp.zeros((width, chunk), F32)], axis=1)
    acc = lax.fori_loop(0, near + 1, last_pass, acc)
    for b in range(nblocks):
        finish(b, acc[:, b * chunk : (b + 1) * chunk])

    @pl.when(in_first)
    def _():
        state_join(0)

    for side in range(2):
        state_wait(1, side)

    intos, backs = [], []
    for h in range(heads):
        ends = []
        for side in range(2):
            close, mult = state_read(1, side, 0, h)
            ends.append(close + mult * state_read(1, side, 1, h)[0])
        keep = [jnp.exp(head_terms(b, h)[2]) for b in range(nblocks)]
        state = ends[0]
        into = []
        for b in range(nblocks):
            into.append(follows[b] * state)
            state = states[0, b, h] + keep[b] * into[b]
        state = ends[1]
        back = [None] * nblocks
        for b in reversed(range(nblocks)):
            back[b] = precedes[b] * state
            state = states[1, b, h] + keep[b] * back[b]
        intos.append([x.astype(BF16) for x in into])
        backs.append([x.astype(BF16) for x in back])
    for b in range(nblocks):
        for h in range(heads):
            row, col, total = head_terms(b, h)
            query, key, value, dol = (parts[a, b, h] for a in range(4))
            head_decay = jnp.exp(col)
            tail_decay = jnp.exp(total - col)
            at = pl.ds(h, TILE, stride=heads)
            wide[0, at, :] = grads[0, b, h] + head_decay * dot_nt(dol, intos[h][b])
            wide[1, at, :] = grads[1, b, h] + tail_decay * dot_nt(value, backs[h][b])
            wide[2, at, :] = grads[2, b, h] + tail_decay * dot_nn(key, backs[h][b])
        for a, ref in enumerate((lin_dq, lin_dk, lin_dv)):
            ref[b * rows : (b + 1) * rows, :] = wide[a].astype(BF16)

    for which in range(2):
        grad_copy(which, 0).wait_recv()
        paired[which, 0] = mine(which, 0)

    for step in range(1, reach + 1):

        @pl.when(takes(step, nright, 1))
        def _():
            home_copy(step).wait_recv()
            for which in range(2):
                paired[which, 0] += inbox[step - 1, which].astype(F32)

    att_dk[...] = (paired[0, 0] * scale).astype(BF16)
    att_dv[...] = paired[1, 0].astype(BF16)

    for which in range(2):
        grad_copy(which, 0).wait_send()
    for trip in range(2):
        for k, hop in enumerate(hops[trip]):
            for side, there in ((0, nright), (1, nleft)):

                @pl.when(hop <= there)
                def _():
                    state_copy(trip, side, k).wait_send()

    for step in range(1, reach + 1):

        @pl.when(takes(step, nright, 1))
        def _():
            for which in range(2):
                kv_copy(which, step).wait_send()

        @pl.when(takes(step, nleft, 1))
        def _():
            for which in range(2):
                pair_copy(which, step).wait_send()
            home_copy(step).wait_send()

        @pl.when(takes(step, nleft, 0))
        def _():
            for which in range(2):
                grad_copy(which, step).wait_send()


def long_kernel(
    count, limit, heads, nblocks,
    doc, lq, lk, lv, ld, dec_in, aq, ado, att_k, att_v,
    lin_dq, lin_dk, lin_dv, att_dq, att_dk, att_dv,
    wide, raw, dec, q, dout, kall, vall, parts, states, local, grads,
    scores, probs_grad, peaks, top_ref, amount_ref, weighted_ref, dq_sum, flipped, dkey, dvalue,
    snd, got, paired, out, inbox,
    raw_sem, kv_send, kv_recv, pair_send, pair_recv, st_send, st_recv,
    pg_send, pg_recv, home_send, home_recv,
):
    me = lax.axis_index("ctx")
    carry = (top_ref, amount_ref, weighted_ref)
    core = lax.axis_index("head")
    length = nblocks * TILE
    width = lq.shape[1]
    rows = TILE * heads
    first_devs = MOST // nblocks
    in_first = me < first_devs
    later_reach = limit // nblocks
    reach = slots_of(limit, nblocks)
    most = jnp.where(in_first, first_devs - 1, later_reach)
    nleft = jnp.minimum(jnp.where(in_first, me, me - first_devs), most)
    nright = jnp.minimum(jnp.where(in_first, first_devs - 1 - me, count - 1 - me), most)
    span = jnp.where(in_first, MOST, limit)

    def takes(step, there, who):
        if isinstance(step, int) and step != later_reach:
            return step <= there
        far = jnp.logical_and(step == later_reach, jnp.logical_not(in_first))
        return jnp.logical_and(step <= there, jnp.logical_or(jnp.logical_not(far), core == who))

    scale = width ** (-0.5)
    factor = scale * math.log2(math.e)

    loads = [
        pltpu.make_async_copy(ref, raw.at[a], raw_sem.at[a])
        for a, ref in enumerate((lq, lk, lv, ld))
    ]
    loads.append(pltpu.make_async_copy(dec_in, dec, raw_sem.at[4]))
    loads.append(pltpu.make_async_copy(aq, q, raw_sem.at[5]))
    loads.append(pltpu.make_async_copy(ado, dout, raw_sem.at[6]))
    own_rows = pl.ds(reach * length, length)
    loads.append(pltpu.make_async_copy(att_k, kall.at[own_rows], raw_sem.at[7]))
    loads.append(pltpu.make_async_copy(att_v, vall.at[own_rows], raw_sem.at[8]))
    for load in loads:
        load.start()

    barrier = pltpu.get_barrier_semaphore()
    pl.semaphore_signal(barrier, inc=1, device_id={"head": 1 - core}, device_id_type=MESH)
    for step in range(1, reach + 1):

        @pl.when(step <= nright)
        def _():
            pl.semaphore_signal(barrier, inc=1, device_id={"ctx": me + step}, device_id_type=MESH)

        @pl.when(step <= nleft)
        def _():
            pl.semaphore_signal(barrier, inc=1, device_id={"ctx": me - step}, device_id_type=MESH)

    pl.semaphore_wait(barrier, 1 + nleft + nright)

    pairs = ((att_k, kall), (att_v, vall))

    def half_of(step):
        start = pl.multiple_of(core * TILE, TILE)
        return start, pl.ds((reach - step) * length + start, TILE)

    def kv_copy(which, step):
        start, place = half_of(step)
        source, target = pairs[which]
        return pltpu.make_async_remote_copy(
            src_ref=source.at[pl.ds(start, TILE)],
            dst_ref=target.at[place],
            send_sem=kv_send.at[which, step - 1],
            recv_sem=kv_recv.at[which, step - 1],
            device_id={"ctx": me + step},
            device_id_type=MESH,
        )

    def pair_copy(which, step):
        target = pairs[which][1]
        place = half_of(step)[1]
        return pltpu.make_async_remote_copy(
            src_ref=target.at[place],
            dst_ref=target.at[place],
            send_sem=pair_send.at[which, step - 1],
            recv_sem=pair_recv.at[which, step - 1],
            device_id={"head": 1 - core},
            device_id_type=MESH,
        )

    def pass_on(step):
        @pl.when(takes(step, nleft, 1))
        def _():
            for which in range(2):
                kv_copy(which, step).wait_recv()
                pair_copy(which, step).start()

    def pair_wait(step):
        for which in range(2):
            pair_copy(which, step).wait_recv()

    hops = ((1, 2), (1, 4))

    def state_copy(trip, side, k):
        hop = hops[trip][k]
        return pltpu.make_async_remote_copy(
            src_ref=snd.at[trip, side],
            dst_ref=got.at[trip, side, k],
            send_sem=st_send.at[trip, side, k],
            recv_sem=st_recv.at[trip, side, k],
            device_id={"ctx": me + hop if side == 0 else me - hop},
            device_id_type=MESH,
        )

    def sent(side):
        return nright if side == 0 else nleft

    def due(side):
        return nleft if side == 0 else nright

    def state_start(trip, side):
        for k, hop in enumerate(hops[trip]):

            @pl.when(hop <= sent(side))
            def _():
                state_copy(trip, side, k).start()

            @pl.when(hop > due(side))
            def _():
                got[trip, side, k] = jnp.zeros(got.shape[3:], BF16)

    def state_wait(trip, side):
        for k, hop in enumerate(hops[trip]):

            @pl.when(hop <= due(side))
            def _():
                state_copy(trip, side, k).wait_recv()

    def state_write(trip, side, totals, mults):
        pads = []
        for h in range(heads):
            snd[trip, side, h * width : (h + 1) * width, :] = totals[h].astype(BF16)
            high, low = split(jnp.broadcast_to(mults[h], (1, width)))
            pads.append((high.astype(F32), low.astype(F32)))
        rows16 = [pads[h][0] for h in range(heads)] + [pads[h][1] for h in range(heads)]
        rows16.append(jnp.zeros((16 - 2 * heads, width), F32))
        snd[trip, side, heads * width :, :] = jnp.concatenate(rows16, axis=0).astype(BF16)

    def state_read(trip, side, k, h):
        at = heads * width
        total = got[trip, side, k, h * width : (h + 1) * width, :].astype(F32)
        pads = got[trip, side, k, at : at + 16, :].astype(F32)
        return total, pads[h : h + 1] + pads[heads + h : heads + h + 1]

    for step in range(1, reach + 1):

        @pl.when(takes(step, nright, 1))
        def _():
            for which in range(2):
                kv_copy(which, step).start()

    for load in loads:
        load.wait()
    follows, precedes, head_terms, t_sub, t_lane = decay_terms(me, count, nblocks, doc, dec)

    for b in range(nblocks):
        for a in range(4):
            wide[a] = raw[a, b * rows : (b + 1) * rows, :].astype(F32)
        for h in range(heads):
            row, col, total = head_terms(b, h)
            picked = [wide[a, pl.ds(h, TILE, stride=heads), :] for a in range(4)]
            for a in range(4):
                parts[a, b, h] = picked[a].astype(BF16)
            key_high, key_low = split((picked[1] * jnp.exp(total - col)).T)
            value = picked[2].astype(BF16)
            states[0, b, h] = dot_nn(key_high, value) + dot_nn(key_low, value)
            query_high, query_low = split((picked[0] * jnp.exp(col)).T)
            dol = picked[3].astype(BF16)
            states[1, b, h] = dot_nn(query_high, dol) + dot_nn(query_low, dol)

    totals, mults = ([], []), ([], [])
    for h in range(heads):
        keep = [jnp.exp(head_terms(b, h)[2]) for b in range(nblocks)]
        total_l = states[0, 0, h]
        mult_l = keep[0] * follows[0]
        for b in range(1, nblocks):
            total_l = states[0, b, h] + keep[b] * follows[b] * total_l
            mult_l = mult_l * keep[b] * follows[b]
        total_r = states[1, nblocks - 1, h]
        mult_r = keep[nblocks - 1] * precedes[nblocks - 1]
        for b in reversed(range(nblocks - 1)):
            total_r = states[1, b, h] + keep[b] * precedes[b] * total_r
            mult_r = mult_r * keep[b] * precedes[b]
        for side, total, mult in ((0, total_l, mult_l), (1, total_r, mult_r)):
            totals[side].append(total)
            mults[side].append(mult)
            local[side, h] = total
    for side in range(2):
        state_write(0, side, totals[side], mults[side])

    state_start(0, 1)

    @pl.when(jnp.logical_not(in_first))
    def _():
        state_start(0, 0)

    def state_join(side):
        state_wait(0, side)
        joined, spans = [], []
        for h in range(heads):
            one, mult_one = state_read(0, side, 0, h)
            two, mult_two = state_read(0, side, 1, h)
            joined.append(local[side, h] + mults[side][h] * (one + mult_one * two))
            spans.append(mults[side][h] * mult_one * mult_two)
        state_write(1, side, joined, spans)
        state_start(1, side)


    def within(b):
        for h in range(heads):
            row, col, total = head_terms(b, h)
            query, key, value, dol = (parts[a, b, h] for a in range(4))
            seen = t_sub <= t_lane
            weight = jnp.where(seen, jnp.exp(jnp.where(seen, row - col, 0.0)), 0.0)
            left = (dot_nt(value, dol) * weight).astype(BF16)
            right = (dot_nt(key, query) * weight).astype(BF16)
            grads[0, b, h] = dot_tn(left, key)
            grads[1, b, h] = dot_nn(left, query)
            grads[2, b, h] = dot_nn(right, dol)

    within(0)
    pass_on(1)
    for b in range(1, nblocks):
        within(b)
    def rows_of(j):
        return pl.ds(pl.multiple_of(j * TILE, TILE), TILE)

    sources = (dkey, dvalue)

    def grad_copy(which, step):
        return pltpu.make_async_remote_copy(
            src_ref=sources[which].at[rows_of((reach - step) * nblocks + 1 - core)],
            dst_ref=paired.at[which, step],
            send_sem=pg_send.at[which, step],
            recv_sem=pg_recv.at[which, step],
            device_id={"head": 1 - core},
            device_id_type=MESH,
        )

    def home_copy(step):
        return pltpu.make_async_remote_copy(
            src_ref=out.at[step - 1],
            dst_ref=inbox.at[step - 1],
            send_sem=home_send.at[step - 1],
            recv_sem=home_recv.at[step - 1],
            device_id={"ctx": me - step},
            device_id_type=MESH,
        )

    def mine(which, step):
        place = rows_of((reach - step) * nblocks + core)
        return sources[which][place, :] + paired[which, step]

    def send_home(step):
        for which in range(2):
            grad_copy(which, step).wait_recv()
        for which in range(2):
            out[step - 1, which] = mine(which, step).astype(BF16)
        home_copy(step).start()

    chunk = rows
    base = reach * nblocks
    offset = offset_of(limit, nblocks)
    near = jnp.minimum(nleft, jnp.where(in_first, reach, later_reach - 1))
    far = jnp.logical_and(jnp.logical_not(in_first), nleft == later_reach)
    far_tile = (reach - later_reach) * nblocks + 1
    queries = [q[b * chunk : (b + 1) * chunk, :] for b in range(nblocks)]
    douts = [dout[b * chunk : (b + 1) * chunk, :] for b in range(nblocks)]
    dkey[rows_of(base + 1), :] = jnp.zeros((TILE, width), F32)
    dvalue[rows_of(base + 1), :] = jnp.zeros((TILE, width), F32)

    def keys_at(j, n):
        return pl.ds(pl.multiple_of(j * TILE, TILE), n * TILE)

    def hidden(b, j):
        at = jnp.clip(me * nblocks - base + j, 0, count * nblocks - 1)
        return jnp.where(doc[at] == doc[me * nblocks + b], 0.0, -NEG).astype(F32)

    def folded(x, op):
        return op(x.reshape(TILE // 8, 8, chunk), axis=0)

    def causal():
        token = lax.broadcasted_iota(jnp.int32, (TILE, chunk), 1) // heads
        return lax.broadcasted_iota(jnp.int32, (TILE, chunk), 0) <= token

    def flip(step, tiles):
        first = (reach - step) * nblocks + tiles[0]
        low = tiles[0] * TILE
        block = kall[keys_at(first, len(tiles)), :].astype(F32).T.astype(BF16)
        flipped[step, :, low : low + len(tiles) * TILE] = block

    def weigh(b, step, tiles, carried, diag=False):
        top, amount, weighted = carried
        first = (reach - step) * nblocks + tiles[0]
        at = keys_at(first, len(tiles))
        s = dot_nt(kall[at, :], queries[b]) * factor
        g = dot_nt(vall[at, :], douts[b])
        parts_s = [s[k * TILE : (k + 1) * TILE] for k in range(len(tiles))]
        shades = [hidden(b, first + k) for k in range(len(tiles))]
        if diag:
            parts_s[-1] = jnp.where(causal(), parts_s[-1], NEG)
        peak = folded(parts_s[0], jnp.max) - shades[0]
        for k in range(1, len(tiles)):
            peak = jnp.maximum(peak, folded(parts_s[k], jnp.max) - shades[k])
        peak = jnp.maximum(top, jnp.max(peak, axis=0, keepdims=True))
        shrink = jnp.exp2(top - peak)
        amount = amount * shrink
        weighted = weighted * shrink
        for k in range(len(tiles)):
            p = jnp.exp2(parts_s[k] - (peak + shades[k]))
            gk = g[k * TILE : (k + 1) * TILE]
            scores[first + k - offset] = p
            probs_grad[first + k - offset] = gk
            amount += folded(p, jnp.sum)
            weighted += folded(p * gk, jnp.sum)
        peaks[b, step] = peak
        return peak, amount, weighted

    def ready(carried):
        top, amount, weighted = carried
        inverse = 1.0 / jnp.sum(amount, axis=0, keepdims=True)
        delta = jnp.sum(weighted, axis=0, keepdims=True) * inverse
        return top, inverse, delta

    def grade(b, step, tiles, stats, acc):
        top, inverse, delta = stats
        first = (reach - step) * nblocks + tiles[0]
        low = tiles[0] * TILE
        size = len(tiles) * TILE
        held = pl.ds(first - offset, len(tiles))
        p = scores[held].reshape(size, chunk) * (jnp.exp2(peaks[b, step] - top) * inverse)
        g = p * (probs_grad[held].reshape(size, chunk) - delta)
        p = p.astype(BF16)
        g = g.astype(BF16)
        at = keys_at(first, len(tiles))
        if b == 0:
            dvalue[at, :] = dot_nn(p, douts[b])
            dkey[at, :] = dot_nn(g, queries[b])
        else:
            dvalue[at, :] += dot_nn(p, douts[b])
            dkey[at, :] += dot_nn(g, queries[b])
        return acc + dot_nn(flipped[step, :, low : low + size], g)

    def finish(b, acc):
        att_dq[b * chunk : (b + 1) * chunk, :] = (acc.T * scale).astype(BF16)

    flip(0, (0, 1))
    row = jnp.zeros((8, chunk), F32)
    start = (jnp.full((1, chunk), NEG, F32), row, row)
    state_zero = weigh(0, 0, (0,), start, diag=True)
    for i, ref in enumerate(carry):
        ref[...] = state_zero[i]

    def first_pass(step, carried):
        pass_on(step + 1)
        pair_wait(step)
        flip(step, (0, 1))
        return weigh(0, step, (0, 1), carried)

    carried = lax.fori_loop(1, near + 1, first_pass, state_zero)
    for i, ref in enumerate(carry):
        ref[...] = carried[i]

    @pl.when(far)
    def _():
        @pl.when(core == 0)
        def _():
            pair_wait(later_reach)

        flip(later_reach, (1,))
        more = weigh(0, later_reach, (1,), tuple(ref[...] for ref in carry))
        for i, ref in enumerate(carry):
            ref[...] = more[i]

    state_join(1)

    @pl.when(in_first)
    def _():
        state_start(0, 0)


    stats = ready(tuple(ref[...] for ref in carry))
    acc = grade(0, 0, (0,), stats, jnp.zeros((width, chunk), F32))
    carried = weigh(1, 0, (0, 1), start, diag=True)

    def both(step, packed):
        carried, acc = packed
        acc = grade(0, step, (0, 1), stats, acc)
        return weigh(1, step, (0, 1), carried), acc

    carried, acc = lax.fori_loop(1, near + 1, both, (carried, acc))
    dq_sum[...] = acc

    @pl.when(far)
    def _():
        dq_sum[...] = grade(0, later_reach, (1,), stats, dq_sum[...])

        @pl.when(core == 0)
        def _():
            for which in range(2):
                grad_copy(which, later_reach).start()

    finish(0, dq_sum[...])
    state_join(0)

    @pl.when(jnp.logical_and(far, core == 1))
    def _():
        send_home(later_reach)

    last_stats = ready(carried)

    def last_pass(i, acc):
        step = near - i
        acc = grade(1, step, (0, 1), last_stats, acc)
        for which in range(2):
            grad_copy(which, step).start()

        @pl.when(i > 0)
        def _():
            send_home(step + 1)

        return acc

    finish(1, lax.fori_loop(0, near + 1, last_pass, jnp.zeros((width, chunk), F32)))
    for side in range(2):
        state_wait(1, side)

    intos, backs = [], []
    for h in range(heads):
        ends = []
        for side in range(2):
            close, mult = state_read(1, side, 0, h)
            ends.append(close + mult * state_read(1, side, 1, h)[0])
        keep = [jnp.exp(head_terms(b, h)[2]) for b in range(nblocks)]
        state = ends[0]
        into = []
        for b in range(nblocks):
            into.append(follows[b] * state)
            state = states[0, b, h] + keep[b] * into[b]
        state = ends[1]
        back = [None] * nblocks
        for b in reversed(range(nblocks)):
            back[b] = precedes[b] * state
            state = states[1, b, h] + keep[b] * back[b]
        intos.append([x.astype(BF16) for x in into])
        backs.append([x.astype(BF16) for x in back])
    for b in range(nblocks):
        for h in range(heads):
            row, col, total = head_terms(b, h)
            query, key, value, dol = (parts[a, b, h] for a in range(4))
            head_decay = jnp.exp(col)
            tail_decay = jnp.exp(total - col)
            at = pl.ds(h, TILE, stride=heads)
            wide[0, at, :] = grads[0, b, h] + head_decay * dot_nt(dol, intos[h][b])
            wide[1, at, :] = grads[1, b, h] + tail_decay * dot_nt(value, backs[h][b])
            wide[2, at, :] = grads[2, b, h] + tail_decay * dot_nn(key, backs[h][b])
        for a, ref in enumerate((lin_dq, lin_dk, lin_dv)):
            ref[b * rows : (b + 1) * rows, :] = wide[a].astype(BF16)

    for which in range(2):
        grad_copy(which, 0).wait_recv()
        paired[which, 0] = mine(which, 0)

    for step in range(1, reach + 1):

        @pl.when(takes(step, nright, 1))
        def _():
            home_copy(step).wait_recv()
            for which in range(2):
                paired[which, 0] += inbox[step - 1, which].astype(F32)

    att_dk[...] = (paired[0, 0] * scale).astype(BF16)
    att_dv[...] = paired[1, 0].astype(BF16)

    for which in range(2):
        grad_copy(which, 0).wait_send()
    for trip in range(2):
        for k, hop in enumerate(hops[trip]):
            for side, there in ((0, nright), (1, nleft)):

                @pl.when(hop <= there)
                def _():
                    state_copy(trip, side, k).wait_send()

    for step in range(1, reach + 1):

        @pl.when(takes(step, nright, 1))
        def _():
            for which in range(2):
                kv_copy(which, step).wait_send()

        @pl.when(takes(step, nleft, 1))
        def _():
            for which in range(2):
                pair_copy(which, step).wait_send()
            home_copy(step).wait_send()

        @pl.when(takes(step, nleft, 0))
        def _():
            for which in range(2):
                grad_copy(which, step).wait_send()


def slots_of(limit, nblocks):
    return max(MOST // nblocks - 1, limit // nblocks)


def offset_of(limit, nblocks):
    return max(0, slots_of(limit, nblocks) * nblocks + 1 - MOST)


def place_kernel(*refs):
    half = (len(refs) - 1) // 2
    sems = refs[-1]
    moves = [
        pltpu.make_async_copy(refs[i], refs[half + i], sems.at[i]) for i in range(half)
    ]
    for move in moves:
        move.start()
    for move in moves:
        move.wait()


def place(outs):
    return pl.pallas_call(
        place_kernel,
        out_shape=[SHAPE(x.shape, x.dtype) for x in outs],
        in_specs=[ANYWHERE] * len(outs),
        out_specs=[ANYWHERE] * len(outs),
        scratch_shapes=[DMA((len(outs),))],
        name="place",
    )(*outs)


def call_whole(count, limit, heads, nblocks, args):
    width = args[-1].shape[1]
    rows = nblocks * TILE * heads
    reach = slots_of(limit, nblocks)
    window = (reach + 1) * nblocks * TILE
    held = (reach + 1) * nblocks - offset_of(limit, nblocks)
    return pl.pallas_call(
        functools.partial(whole_kernel, count, limit, heads, nblocks),
        out_shape=[SHAPE((rows, width), BF16)] * 4 + [SHAPE((TILE, width), BF16)] * 2,
        in_specs=[IN_SMEM] + [ANYWHERE] * 9,
        out_specs=[IN_VMEM] * 6,
        scratch_shapes=[
            pltpu.VMEM((3, TILE * heads, width), F32),
            pltpu.VMEM((4, rows, width), BF16),
            pltpu.VMEM((heads, nblocks * TILE), F32),
            pltpu.VMEM((rows, width), BF16),
            pltpu.VMEM((rows, width), BF16),
            pltpu.VMEM((window, width), BF16),
            pltpu.VMEM((window, width), BF16),
            pltpu.VMEM((4, nblocks, heads, TILE, width), BF16),
            pltpu.VMEM((2, nblocks, heads, width, width), F32),
            pltpu.VMEM((2, heads, width, width), F32),
            pltpu.VMEM((3, nblocks, heads, TILE, width), F32),
            pltpu.VMEM((nblocks, held, TILE, TILE * heads), BF16),
            pltpu.VMEM((nblocks, held, TILE, TILE * heads), BF16),
            pltpu.VMEM((nblocks, reach + 1, 1, TILE * heads), F32),
            pltpu.VMEM((1, TILE * heads), F32),
            pltpu.VMEM((8, TILE * heads), F32),
            pltpu.VMEM((8, TILE * heads), F32),
            pltpu.VMEM((nblocks, 1, TILE * heads), F32),
            pltpu.VMEM((width, TILE * heads), F32),
            pltpu.VMEM((reach + 1, width, nblocks * TILE), BF16),
            pltpu.VMEM((window, width), F32),
            pltpu.VMEM((window, width), F32),
            pltpu.VMEM((2, 2, heads * width + 16, width), BF16),
            pltpu.VMEM((2, 2, 2, heads * width + 16, width), BF16),
            pltpu.VMEM((2, reach + 1, TILE, width), F32),
            pltpu.VMEM((reach, 2, TILE, width), BF16),
            pltpu.VMEM((reach, 2, TILE, width), BF16),
            DMA((9,)),
            DMA((2, reach)),
            DMA((2, reach)),
            DMA((2, reach)),
            DMA((2, reach)),
            DMA((2, 2, 2)),
            DMA((2, 2, 2)),
            DMA((2, reach + 1)),
            DMA((2, reach + 1)),
            DMA((reach,)),
            DMA((reach,)),
        ],
        compiler_params=pltpu.CompilerParams(
            collective_id=0 if limit == MOST else 1,
            has_side_effects=True,
            vmem_limit_bytes=VMEM_LIMIT,
        ),
        name="whole_%d" % limit,
    )(*args)


def call_long(count, limit, heads, nblocks, args):
    width = args[-1].shape[1]
    rows = nblocks * TILE * heads
    reach = slots_of(limit, nblocks)
    window = (reach + 1) * nblocks * TILE
    held = (reach + 1) * nblocks - offset_of(limit, nblocks)
    return pl.pallas_call(
        functools.partial(long_kernel, count, limit, heads, nblocks),
        out_shape=[SHAPE((rows, width), BF16)] * 4 + [SHAPE((TILE, width), BF16)] * 2,
        in_specs=[IN_SMEM] + [ANYWHERE] * 9,
        out_specs=[IN_VMEM] * 6,
        scratch_shapes=[
            pltpu.VMEM((4, TILE * heads, width), F32),
            pltpu.VMEM((4, rows, width), BF16),
            pltpu.VMEM((heads, nblocks * TILE), F32),
            pltpu.VMEM((rows, width), BF16),
            pltpu.VMEM((rows, width), BF16),
            pltpu.VMEM((window, width), BF16),
            pltpu.VMEM((window, width), BF16),
            pltpu.VMEM((4, nblocks, heads, TILE, width), BF16),
            pltpu.VMEM((2, nblocks, heads, width, width), F32),
            pltpu.VMEM((2, heads, width, width), F32),
            pltpu.VMEM((3, nblocks, heads, TILE, width), F32),
            pltpu.VMEM((held, TILE, TILE * heads), F32),
            pltpu.VMEM((held, TILE, TILE * heads), F32),
            pltpu.VMEM((nblocks, reach + 1, 1, TILE * heads), F32),
            pltpu.VMEM((1, TILE * heads), F32),
            pltpu.VMEM((8, TILE * heads), F32),
            pltpu.VMEM((8, TILE * heads), F32),
            pltpu.VMEM((width, TILE * heads), F32),
            pltpu.VMEM((reach + 1, width, nblocks * TILE), BF16),
            pltpu.VMEM((window, width), F32),
            pltpu.VMEM((window, width), F32),
            pltpu.VMEM((2, 2, heads * width + 16, width), BF16),
            pltpu.VMEM((2, 2, 2, heads * width + 16, width), BF16),
            pltpu.VMEM((2, reach + 1, TILE, width), F32),
            pltpu.VMEM((reach, 2, TILE, width), BF16),
            pltpu.VMEM((reach, 2, TILE, width), BF16),
            DMA((9,)),
            DMA((2, reach)),
            DMA((2, reach)),
            DMA((2, reach)),
            DMA((2, reach)),
            DMA((2, 2, 2)),
            DMA((2, 2, 2)),
            DMA((2, reach + 1)),
            DMA((2, reach + 1)),
            DMA((reach,)),
            DMA((reach,)),
        ],
        compiler_params=pltpu.CompilerParams(
            collective_id=0 if limit == MOST else 1,
            has_side_effects=True,
            vmem_limit_bytes=VMEM_LIMIT,
        ),
        name="long_%d" % limit,
    )(*args)


def shards(count, lin_q, lin_k, lin_v, lin_dout, lin_decay, att_q, att_k, att_v, att_dout, doc_block):
    length, heads, width = lin_q.shape
    nblocks = length // TILE
    assert nblocks == 2
    flat = lambda x: x.reshape(length * heads, width)
    args = (
        doc_block, flat(lin_q), flat(lin_k), flat(lin_v), flat(lin_dout), lin_decay,
        flat(att_q), flat(att_dout), att_k, att_v,
    )
    later = doc_block[MOST:]
    long = jnp.any(later[SHORT:] == later[:-SHORT])
    outs = lax.cond(
        long,
        lambda *a: call_long(count, MOST, heads, nblocks, a),
        lambda *a: call_whole(count, SHORT, heads, nblocks, a),
        *args,
    )
    outs = place(outs)
    full = lambda x: x.reshape(length, heads, width)
    return (full(outs[0]), full(outs[1]), full(outs[2]), full(outs[3]), outs[4], outs[5])


def solution(mesh):
    return jax.shard_map(
        functools.partial(shards, mesh.shape["ctx"]),
        mesh=mesh,
        in_specs=(
            P("ctx", "head", None),
            P("ctx", "head", None),
            P("ctx", "head", None),
            P("ctx", "head", None),
            P("head", "ctx"),
            P("ctx", "head", None),
            P("ctx", None),
            P("ctx", None),
            P("ctx", "head", None),
            P(),
        ),
        out_specs=(
            P("ctx", "head", None),
            P("ctx", "head", None),
            P("ctx", "head", None),
            P("ctx", "head", None),
            P(("ctx", "head"), None),
            P(("ctx", "head"), None),
        ),
        check_vma=False,
    )
```
